32 devices in a mesh: seq: 8 (over z, y), ch: 4 (over x, core).
Axes of the slice: x: 2, y: 2, z: 4, core: 2. Of those that a mesh axis runs over, the one named last changes fastest.
Arguments:
- queries: bfloat16 [8192, 8192], P('seq', 'ch'), may hold values from -6 to 6
- keys: bfloat16 [8192, 8192], P('seq', 'ch'), may hold values from -6 to 6
- values: bfloat16 [8192, 8192], P('seq', 'ch'), may hold values from -6 to 6
- filters: bfloat16 [512, 128], P('ch'), may hold values from -0.5 to 0.5
- grad_out: bfloat16 [8192, 4096], P('seq', 'ch'), may hold values from -6 to 6
- out_weight: bfloat16 [4096, 8192], P('seq', 'ch'), may hold values from -0.09375 to 0.09375
Outputs:
- grad_queries: bfloat16 [8192, 8192], P('seq', 'ch')
- grad_keys: bfloat16 [8192, 8192], P('seq', 'ch')
- grad_values: bfloat16 [8192, 8192], P('seq', 'ch')
- grad_filters: float32 [512, 128], P('ch', 'seq')
- grad_weight: bfloat16 [4096, 8192], P('seq', 'ch')
The draws below stay inside these ranges and needn't reach their ends.
All inputs are finite; a program needn't handle non-finite values.
Results may differ from the reference program's by a relative error of at most 0.022.
Values may be sent and summed in bfloat16 or wider, within the bound.
No kernel may reach another device: no remote copies, remote signals or barrier semaphores. Data moves between devices by JAX's collectives and lax.ppermute only.
A program may use at most 192 MiB of HBM per device.

```python
import jax
import jax.numpy as jnp
from jax import lax

D = 8192
FEAT_OUT = 4096
GROUP = 16
FILT = 128
TOK_DEV = 1024
TOKENS = 8192
GROUPS = 512
N_SEQ = 8


def with_spikes(drawn, rng, source, target, parts, factor):
    def block_of(dim):
        return (jnp.arange(drawn.shape[dim]) // (drawn.shape[dim] // parts)).reshape((-1,) + (1,) * (drawn.ndim - 1 - dim))

    first = jax.random.permutation(rng, parts)[block_of(target)]
    far = (block_of(target) + parts // 2) % parts
    return jnp.where((block_of(source) == first) | (block_of(source) == far), factor * drawn, drawn)


def levels(own_key, dims, cuts, smallest, high):
    factor_of, own = 1.0, jax.random.fold_in(own_key, 6)
    for dim, parts in cuts:
        heights = jnp.exp(jax.random.uniform(jax.random.fold_in(own, dim), (parts,), jnp.float32, smallest / len(cuts), high / len(cuts)))
        factor_of = factor_of * jnp.repeat(heights, dims[dim] // parts).reshape([-1 if axis == dim else 1 for axis in range(len(dims))])
    return factor_of


def bell_draw(own_key, dims, scale, most, pieces=(), kind=jnp.bfloat16):
    result = scale * jax.random.normal(own_key, dims, jnp.float32)
    if pieces:
        result = result * levels(own_key, dims, pieces, -0.22, 0.18)
    return jnp.clip(result, -most, most).astype(kind)


def noise_with(stream_key, extent, scale, limit, split, heavy, kind=jnp.bfloat16):
    entries = scale * jax.random.normal(stream_key, extent, jnp.float32)
    if split:
        entries = entries * levels(stream_key, extent, split, -0.22, 0.18)
    return jnp.clip(with_spikes(entries, jax.random.fold_in(stream_key, 3), *heavy), -limit, limit).astype(kind)


def setup_inputs(seed: int = 0) -> dict:
    seeds = jax.random.split(jax.random.key(seed), 7)
    queries = bell_draw(seeds[0], (TOKENS, D), 1.0, 6.0, ((0, 8), (1, 4)))
    keys = bell_draw(seeds[1], (TOKENS, D), 1.0, 6.0, ((0, 8), (1, 4)))
    values = bell_draw(seeds[2], (TOKENS, D), 1.0, 6.0, ((0, 8), (1, 4)))
    filters = bell_draw(seeds[3], (GROUPS, FILT), FILT ** -0.5, 0.5, ((0, 4),))
    grad_out = noise_with(seeds[4], (TOKENS, FEAT_OUT), 1.0, 6.0, ((0, 8), (1, 4)), (0, 1, 8, 2.0))
    out_weight = bell_draw(seeds[5], (FEAT_OUT, D), FEAT_OUT ** -0.5, 0.09375, ((0, 8), (1, 4)))
    return {"queries": queries, "keys": keys, "values": values, "filters": filters, "grad_out": grad_out, "out_weight": out_weight}


def lag_tables(filter_taps):
    inner = jnp.arange(FILT, dtype=jnp.int32)[:, None]
    outer = jnp.arange(2 * FILT, dtype=jnp.int32)[None, :]
    back_lag = inner + FILT - outer
    ahead_lag = outer - inner
    back_ok = (back_lag >= 0) & (back_lag < FILT)
    ahead_ok = (ahead_lag >= 0) & (ahead_lag < FILT)
    back = jnp.where(back_ok[None], filter_taps[:, jnp.clip(back_lag, 0, FILT - 1)], 0.0)
    ahead = jnp.where(ahead_ok[None], filter_taps[:, jnp.clip(ahead_lag, 0, FILT - 1)], 0.0)
    return back, ahead


def paired(extended, groups):
    blocks = extended.reshape(-1, FILT, groups, GROUP)
    return jnp.concatenate([blocks[:-1], blocks[1:]], axis=1)


def lag_sums(lag_matrix):
    groups, inner, outer = lag_matrix.shape
    flat = lag_matrix.reshape(groups, inner * outer)
    flat = jnp.pad(flat, ((0, 0), (0, inner)))
    skewed = flat.reshape(groups, inner, outer + 1)
    return jnp.sum(skewed[:, :, 1:inner + 1], axis=1)[:, ::-1]


def reference(queries, keys, values, filters, grad_out, out_weight):
    single = jnp.float32
    total_rows, width = queries.shape
    out_width = grad_out.shape[1]
    groups = width // GROUP
    nblocks = total_rows // FILT
    product = (keys.astype(single) * values.astype(single)).astype(jnp.bfloat16)
    extended = jnp.concatenate([jnp.zeros((FILT, width), jnp.bfloat16), product], axis=0)
    pairs = paired(extended, groups).astype(single)
    back, ahead = lag_tables(filters.astype(single))
    mixed = jnp.einsum('gim,bmgs->bigs', back, pairs).reshape(total_rows, width)
    gated = (queries.astype(single) * mixed).astype(jnp.bfloat16)
    grad_gated = jnp.dot(grad_out, out_weight, preferred_element_type=single).astype(jnp.bfloat16)
    grad_queries = (grad_gated.astype(single) * mixed).astype(jnp.bfloat16)
    grad_mixed = (grad_gated.astype(single) * queries.astype(single)).astype(jnp.bfloat16)
    grad_ext = jnp.concatenate([grad_mixed, jnp.zeros((FILT, width), jnp.bfloat16)], axis=0)
    grad_pairs = paired(grad_ext, groups).astype(single)
    grad_product = jnp.einsum('gim,bmgs->bigs', ahead, grad_pairs).reshape(total_rows, width)
    grad_keys = (grad_product * values.astype(single)).astype(jnp.bfloat16)
    grad_values = (grad_product * keys.astype(single)).astype(jnp.bfloat16)
    own_blocks = grad_mixed.astype(single).reshape(nblocks, FILT, groups, GROUP)
    lag_matrix = jnp.einsum('bigs,bmgs->gim', own_blocks, pairs)
    grad_filters = lag_sums(lag_matrix)
    cot_blocks = grad_out.reshape(N_SEQ, TOK_DEV, out_width)
    act_blocks = gated.reshape(N_SEQ, TOK_DEV, width)

    def accumulate(index, carry):
        partial_sum = jnp.dot(cot_blocks[index].T, act_blocks[index], preferred_element_type=single)
        rounded = lax.optimization_barrier(partial_sum.astype(jnp.bfloat16))
        return carry + rounded.astype(single)

    grad_weight = lax.fori_loop(0, N_SEQ, accumulate, jnp.zeros((out_width, width), single))
    return grad_queries, grad_keys, grad_values, grad_filters, grad_weight.astype(jnp.bfloat16)
```

```python
import functools

import jax
import jax.numpy as jnp
from jax import lax
from jax.experimental import pallas as pl
from jax.experimental.pallas import tpu as pltpu
from jax.sharding import PartitionSpec as P

GROUP = 16
FILT = 128
LANES = 128
GPT = LANES // GROUP
LINE = 4
F32 = jnp.float32
BF16 = jnp.bfloat16
VMEM_LIMIT = 48 * 1024 * 1024


def params():
    return pltpu.CompilerParams(vmem_limit_bytes=VMEM_LIMIT)


def cost(flops, nbytes):
    return pl.CostEstimate(flops=int(flops), bytes_accessed=int(nbytes), transcendentals=0)


def table_kernel(back_ref, ahead_ref, back_out, ahead_out):
    for seed, out in ((back_ref, back_out), (ahead_ref, ahead_out)):
        for g in range(GPT):
            rows = jnp.broadcast_to(seed[g : g + 1, :], (FILT, 2 * FILT))
            turned = pltpu.roll(rows, 0, 1, stride=1, stride_axis=0)
            out[g * FILT : (g + 1) * FILT, :] = turned.astype(BF16)


def tables(filters):
    groups = filters.shape[0]
    taps = filters.astype(F32)
    back = jnp.concatenate(
        [jnp.zeros((groups, 1), F32), taps[:, ::-1], jnp.zeros((groups, FILT - 1), F32)], axis=1
    )
    ahead = jnp.concatenate([taps, jnp.zeros((groups, FILT), F32)], axis=1)
    seed = pl.BlockSpec((GPT, 2 * FILT), lambda i: (i, 0))
    full = pl.BlockSpec((GPT * FILT, 2 * FILT), lambda i: (i, 0))
    shape = jax.ShapeDtypeStruct((groups * FILT, 2 * FILT), BF16)
    return pl.pallas_call(
        table_kernel,
        grid=(groups // GPT,),
        in_specs=[seed, seed],
        out_specs=[full, full],
        out_shape=[shape, shape],
        compiler_params=params(),
        cost_estimate=cost(groups * 2**18, groups * 2**17),
    )(back, ahead)


def group_of_lane(rows, cols):
    return (lax.broadcasted_iota(jnp.int32, (rows, cols), 1) % LANES) // GROUP


def windows(ext, b):
    lo = b * FILT
    return jnp.concatenate([ext[lo : lo + 2 * FILT], ext[lo + FILT : lo + 3 * FILT]], axis=1)


def toeplitz(table, ext, blocks):
    group = group_of_lane(FILT, 2 * LANES)
    rows = []
    for b in range(0, blocks, 2):
        out = jnp.dot(table, windows(ext, b), preferred_element_type=F32)
        picked = out[:FILT]
        for g in range(1, GPT):
            picked = jnp.where(group == g, out[g * FILT : (g + 1) * FILT], picked)
        rows += [picked[:, :LANES], picked[:, LANES:]]
    return jnp.concatenate(rows, axis=0)


def product_of(k, v):
    return (k.astype(F32) * v.astype(F32)).astype(BF16)


def forward_kernel(q, k, v, prior, table, gated, mixed_out):
    blocks = q.shape[0] // FILT
    ext = jnp.concatenate([prior[...], product_of(k[...], v[...])], axis=0)
    mixed = toeplitz(table[...], ext, blocks)
    mixed_out[...] = mixed.astype(BF16)
    gated[...] = (q[...].astype(F32) * mixed).astype(BF16)


def forward(q, k, v, prior, table, chunk, chunks):
    rows, width = q.shape
    tiles = width // LANES // chunks
    here = pl.BlockSpec((rows, LANES), lambda i: (0, chunk * tiles + i))
    out = pl.BlockSpec((rows, LANES), lambda i: (0, i))
    shape = jax.ShapeDtypeStruct((rows, width // chunks), BF16)
    return pl.pallas_call(
        forward_kernel,
        grid=(tiles,),
        in_specs=[
            here,
            here,
            here,
            pl.BlockSpec((FILT, LANES), lambda i: (0, chunk * tiles + i)),
            pl.BlockSpec((GPT * FILT, 2 * FILT), lambda i: (chunk * tiles + i, 0)),
        ],
        out_specs=[out, out],
        out_shape=[shape, shape],
        compiler_params=params(),
        cost_estimate=cost(tiles * rows * 2 * 2**18, tiles * rows * 5 * 256 + tiles * 2**19),
    )(q, k, v, prior, table)


def middle_kernel(own, others, q, k, v, mixed, prior, *rest):
    gq_out, gm_out, taps_out = rest[-3:]
    blocks = q.shape[0] // FILT
    total = own[...].astype(F32)
    for other in others:
        total = total + other[...].astype(F32)
    gg = total.astype(BF16).astype(F32)
    gq_out[...] = (gg * mixed[...].astype(F32)).astype(BF16)
    gm = (gg * q[...].astype(F32)).astype(BF16)
    gm_out[...] = gm
    ext = jnp.concatenate([prior[...], product_of(k[...], v[...])], axis=0)
    group = group_of_lane(FILT, 2 * LANES)
    lag = jnp.zeros((GPT * FILT, 2 * FILT), F32)
    for b in range(0, blocks, 2):
        lo = b * FILT
        pair = jnp.concatenate([gm[lo : lo + FILT], gm[lo + FILT : lo + 2 * FILT]], axis=1)
        stack = jnp.concatenate(
            [jnp.where(group == g, pair, jnp.zeros_like(pair)) for g in range(GPT)], axis=0
        )
        lag = lag + lax.dot_general(
            stack, windows(ext, b), (((1,), (1,)), ((), ())), preferred_element_type=F32
        )
    lag = lag.reshape(GPT, FILT, 2 * FILT)
    half = FILT // 2
    while half >= 8:
        lag = lag[:, :half] + pltpu.roll(lag[:, half:], 2 * FILT - half, 2)
        half //= 2
    while half >= 1:
        lag = lag + pltpu.roll(pltpu.roll(lag, 2 * FILT - half, 2), 8 - half, 1)
        half //= 2
    taps_out[...] = lag[:, 0, :]


def middle(own, others, q, k, v, mixed, prior, filled, chunk, chunks):
    rows, width = q.shape
    tiles = width // LANES // chunks
    groups = width // GROUP // chunks
    here = pl.BlockSpec((rows, LANES), lambda i: (0, chunk * tiles + i))
    part = pl.BlockSpec((rows, LANES), lambda i: (0, i))
    n_other = len(others)

    def kernel(own_ref, *refs):
        middle_kernel(own_ref, refs[:n_other], *refs[n_other:])

    args = [own, *others, q, k, v, mixed, prior]
    in_specs = [part] * (1 + n_other) + [here] * 3 + [part]
    in_specs.append(pl.BlockSpec((FILT, LANES), lambda i: (0, chunk * tiles + i)))
    aliases = {}
    if filled is not None:
        aliases = {len(args): 0}
        args.append(filled)
        in_specs.append(pl.BlockSpec(memory_space=pl.ANY))
    return pl.pallas_call(
        kernel,
        grid=(tiles,),
        in_specs=in_specs,
        out_specs=[here, part, pl.BlockSpec((GPT, 2 * FILT), lambda i: (i, 0))],
        out_shape=[
            jax.ShapeDtypeStruct((rows, width), BF16),
            jax.ShapeDtypeStruct((rows, width // chunks), BF16),
            jax.ShapeDtypeStruct((groups, 2 * FILT), F32),
        ],
        input_output_aliases=aliases,
        compiler_params=params(),
        cost_estimate=cost(tiles * rows * 2 * 2**18, tiles * rows * 9 * 256),
    )(*args)


def backward_kernel(gm, later, k, v, table, *rest):
    gk_out, gv_out = rest[-2:]
    blocks = gm.shape[0] // FILT
    ext = jnp.concatenate([gm[...], later[...]], axis=0)
    gp = toeplitz(table[...], ext, blocks)
    gk_out[...] = (gp * v[...].astype(F32)).astype(BF16)
    gv_out[...] = (gp * k[...].astype(F32)).astype(BF16)


def backward(gm, later, k, v, table, filled, chunk, chunks):
    rows, width = k.shape
    tiles = width // LANES // chunks
    here = pl.BlockSpec((rows, LANES), lambda i: (0, chunk * tiles + i))
    part = pl.BlockSpec((rows, LANES), lambda i: (0, i))
    args = [gm, later, k, v, table]
    in_specs = [
        part,
        pl.BlockSpec((FILT, LANES), lambda i: (0, i)),
        here,
        here,
        pl.BlockSpec((GPT * FILT, 2 * FILT), lambda i: (chunk * tiles + i, 0)),
    ]
    aliases = {}
    if filled is not None:
        aliases = {len(args): 0, len(args) + 1: 1}
        args += filled
        in_specs += [pl.BlockSpec(memory_space=pl.ANY)] * 2
    shape = jax.ShapeDtypeStruct((rows, width), BF16)
    return pl.pallas_call(
        backward_kernel,
        grid=(tiles,),
        in_specs=in_specs,
        out_specs=[here, here],
        out_shape=[shape, shape],
        input_output_aliases=aliases,
        compiler_params=params(),
        cost_estimate=cost(tiles * rows * 2 * 2**18, tiles * rows * 5 * 256 + tiles * 2**19),
    )(*args)


def gate_kernel(order, *refs):
    out = refs[-1]
    total = jnp.dot(refs[0][0], refs[LINE][...], preferred_element_type=F32)
    for j in range(1, LINE):
        total = total + jnp.dot(refs[j][0], refs[LINE + j][...], preferred_element_type=F32)
    out[...] = total.astype(out.dtype)


def gate_grad(order, cot, weights, chunk, chunks, dtype):
    _, rows, depth = cot.shape
    width = weights[0].shape[1] // chunks
    tile = min(256, rows)

    def cot_spec(j):
        return pl.BlockSpec((1, tile, depth), lambda i, order: (order[j], i, 0))

    weight_spec = pl.BlockSpec((depth, width), lambda i, order: (0, chunk))
    return pl.pallas_call(
        gate_kernel,
        grid_spec=pltpu.PrefetchScalarGridSpec(
            num_scalar_prefetch=1,
            grid=(rows // tile,),
            in_specs=[cot_spec(j) for j in range(LINE)] + [weight_spec] * LINE,
            out_specs=pl.BlockSpec((tile, width), lambda i, order: (i, 0)),
        ),
        out_shape=jax.ShapeDtypeStruct((rows, width), dtype),
        compiler_params=params(),
        cost_estimate=cost(
            2 * rows * LINE * depth * width, 2 * LINE * depth * (rows + width) + 4 * rows * width
        ),
    )(order, *([cot] * LINE), *weights)


def shards(seq, ch, queries, keys, values, filters, grad_out, out_weight):
    inner = seq // LINE
    rows, width = queries.shape
    depth = out_weight.shape[0]
    chunks = 2 if width % (2 * LANES) == 0 else 1
    cols = width // chunks
    place = lax.axis_index("seq")
    z, y = place // inner, place % inner

    def send(x, pairs):
        return lax.ppermute(x, "seq", pairs)

    def along_line(x, pairs):
        return send(x, [(a * inner + i, b * inner + i) for a, b in pairs for i in range(inner)])

    def around_inner(x, shift):
        return send(
            x, [(a * inner + i, a * inner + (i + shift) % inner) for a in range(LINE) for i in range(inner)]
        )

    prior = send(
        product_of(keys[rows - FILT :], values[rows - FILT :]), [(i, i + 1) for i in range(seq - 1)]
    )

    up1 = along_line(out_weight, [(0, 1), (1, 2), (2, 3)])
    down1 = along_line(out_weight, [(1, 0), (2, 1), (3, 2)])

    cots = []
    if inner == 2 and ch == LINE:
        kept = lax.dynamic_slice(grad_out, (0, y * depth), (rows, depth))
        other = lax.dynamic_slice(grad_out, (0, (1 - y) * depth), (rows, depth))
        cots.append(lax.all_gather(kept, "ch", axis=0, tiled=False))
        cots.append(lax.all_gather(around_inner(other, 1), "ch", axis=0, tiled=False))
    else:
        full = lax.all_gather(grad_out, "ch", axis=1, tiled=True)
        full = full.reshape(rows, LINE, inner, depth).transpose(2, 1, 0, 3)
        for shift in range(inner):
            part = lax.dynamic_index_in_dim(full, (y + shift) % inner, 0, keepdims=False)
            cots.append(part if shift == 0 else around_inner(part, shift))

    back, ahead = tables(filters)

    gateds, mixeds = [], []
    for h in range(chunks):
        gated, mixed = forward(queries, keys, values, prior, back, h, chunks)
        gateds.append([gated] + [around_inner(gated, r) for r in range(1, inner)])
        mixeds.append(mixed)

    up2 = along_line(up1, [(1, 2), (2, 3)])
    down2 = along_line(down1, [(2, 1), (1, 0)])
    second = jnp.where(z >= 2, up2, down2)
    third = along_line(second, [(2, 3), (1, 0)])
    slot_a = jnp.where(z == 0, down1, up1)
    slot_c = jnp.where((z == 0) | (z == 3), third, down1)
    weights = [out_weight, slot_a, second, slot_c]
    order = jnp.stack(
        [
            z,
            jnp.where(z == 0, 1, z - 1),
            jnp.where(z >= 2, z - 2, z + 2),
            jnp.where(z == 3, 0, jnp.where(z == 1, 2, 3)),
        ]
    ).astype(jnp.int32)

    def partial(block, h):
        total = None
        for cot, gated in zip(cots, gateds[h]):
            lhs = lax.dynamic_index_in_dim(cot, block, 0, keepdims=False)
            term = lax.dot_general(lhs, gated, (((0,), (0,)), ((), ())), preferred_element_type=F32)
            total = term if total is None else total + term
        return total

    grad_weights = []
    for h in range(chunks):
        first = partial(jnp.where(z == 0, 3, 0), h).astype(BF16)
        got = along_line(first, [(0, 1), (3, 2)])
        block = jnp.where(z == 0, 2, jnp.where(z == 1, 3, jnp.where(z == 2, 0, 1)))
        mid = (partial(block, h) + got.astype(F32)).astype(BF16)
        outer_in = along_line(mid, [(0, 1), (3, 2)])
        inner_in = along_line(mid, [(1, 2), (2, 1)])
        add_up = jnp.where(z == 1, outer_in, inner_in).astype(F32)
        add_down = jnp.where(z == 1, inner_in, outer_in).astype(F32)
        last_up = (partial(jnp.minimum(z + 1, 3), h) + add_up).astype(BF16)
        last_down = (partial(jnp.maximum(z - 1, 0), h) + add_down).astype(BF16)
        from_below = along_line(last_up, [(0, 1), (1, 2), (2, 3)])
        from_above = along_line(last_down, [(1, 0), (2, 1), (3, 2)])
        total = partial(z, h) + from_below.astype(F32) + from_above.astype(F32)
        grad_weights.append(total.astype(BF16))
    grad_weight = jnp.concatenate(grad_weights, axis=1)

    owns, others = [], []
    for h in range(chunks):
        others.append(
            [
                around_inner(gate_grad(order, cots[r], weights, h, chunks, BF16), inner - r)
                for r in range(1, inner)
            ]
        )
    for h in range(chunks):
        owns.append(gate_grad(order, cots[0], weights, h, chunks, F32))

    grad_queries = None
    grad_kv = None
    taps = []
    for h in range(chunks):
        here = slice(h * cols, (h + 1) * cols)
        grad_queries, gm, lag = middle(
            owns[h], others[h], queries, keys, values, mixeds[h], prior, grad_queries, h, chunks
        )
        later = send(gm[:FILT], [(i + 1, i) for i in range(seq - 1)])
        grad_kv = backward(gm, later, keys, values, ahead, grad_kv, h, chunks)
        taps.append(lag)
    taps = jnp.concatenate(taps, axis=0)[:, 1 : FILT + 1][:, ::-1]
    taps = taps.T.reshape(seq, FILT // seq, -1)
    taps = jnp.sum(lax.all_to_all(taps, "seq", 0, 0), axis=0)
    return grad_queries, *grad_kv, taps.T, grad_weight


def solution(mesh):
    sizes = dict(mesh.shape)
    return jax.shard_map(
        functools.partial(shards, sizes["seq"], sizes["ch"]),
        mesh=mesh,
        in_specs=(
            P("seq", "ch"),
            P("seq", "ch"),
            P("seq", "ch"),
            P("ch", None),
            P("seq", "ch"),
            P("seq", "ch"),
        ),
        out_specs=(P("seq", "ch"), P("seq", "ch"), P("seq", "ch"), P("ch", "seq"), P("seq", "ch")),
        check_vma=False,
    )
```

```python
import functools

import jax
import jax.numpy as jnp
from jax import lax
from jax.experimental import pallas as pl
from jax.experimental.pallas import tpu as pltpu
from jax.sharding import PartitionSpec as P

GROUP = 16
FILT = 128
LANES = 128
GPT = LANES // GROUP
LINE = 4
F32 = jnp.float32
BF16 = jnp.bfloat16
VMEM_LIMIT = 48 * 1024 * 1024


def params():
    return pltpu.CompilerParams(vmem_limit_bytes=VMEM_LIMIT)


def cost(flops, nbytes):
    return pl.CostEstimate(flops=int(flops) // 64, bytes_accessed=int(nbytes) // 64, transcendentals=0)


def fence(*arrays):
    return lax.optimization_barrier(arrays)


def after(x, *others):
    return lax.optimization_barrier((x, *others))[0]


def table_kernel(back_ref, ahead_ref, back_out, ahead_out):
    for seed, out in ((back_ref, back_out), (ahead_ref, ahead_out)):
        for g in range(GPT):
            rows = jnp.broadcast_to(seed[g : g + 1, :], (FILT, 2 * FILT))
            turned = pltpu.roll(rows, 0, 1, stride=1, stride_axis=0)
            out[g * FILT : (g + 1) * FILT, :] = turned.astype(BF16)


def tables(filters):
    groups = filters.shape[0]
    taps = filters.astype(F32)
    back = jnp.concatenate(
        [jnp.zeros((groups, 1), F32), taps[:, ::-1], jnp.zeros((groups, FILT - 1), F32)], axis=1
    )
    ahead = jnp.concatenate([taps, jnp.zeros((groups, FILT), F32)], axis=1)
    seed = pl.BlockSpec((GPT, 2 * FILT), lambda i: (i, 0))
    full = pl.BlockSpec((GPT * FILT, 2 * FILT), lambda i: (i, 0))
    shape = jax.ShapeDtypeStruct((groups * FILT, 2 * FILT), BF16)
    return pl.pallas_call(
        table_kernel,
        grid=(groups // GPT,),
        in_specs=[seed, seed],
        out_specs=[full, full],
        out_shape=[shape, shape],
        compiler_params=params(),
        cost_estimate=cost(groups * 2**18, groups * 2**17),
    )(back, ahead)


def group_of_lane(rows, cols):
    return (lax.broadcasted_iota(jnp.int32, (rows, cols), 1) % LANES) // GROUP


def windows(ext, b):
    lo = b * FILT
    return jnp.concatenate([ext[lo : lo + 2 * FILT], ext[lo + FILT : lo + 3 * FILT]], axis=1)


def toeplitz(table, ext, blocks):
    group = group_of_lane(FILT, 2 * LANES)
    rows = []
    for b in range(0, blocks, 2):
        out = jnp.dot(table, windows(ext, b), preferred_element_type=F32)
        picked = out[:FILT]
        for g in range(1, GPT):
            picked = jnp.where(group == g, out[g * FILT : (g + 1) * FILT], picked)
        rows += [picked[:, :LANES], picked[:, LANES:]]
    return jnp.concatenate(rows, axis=0)


def product_of(k, v):
    return (k.astype(F32) * v.astype(F32)).astype(BF16)


def forward_kernel(q, k, v, prior, table, gated, mixed_out):
    blocks = q.shape[0] // FILT
    ext = jnp.concatenate([prior[...], product_of(k[...], v[...])], axis=0)
    mixed = toeplitz(table[...], ext, blocks)
    mixed_out[...] = mixed.astype(BF16)
    gated[...] = (q[...].astype(F32) * mixed).astype(BF16)


def forward(q, k, v, prior, table, chunk, chunks):
    rows, width = q.shape
    tiles = width // LANES // chunks
    here = pl.BlockSpec((rows, LANES), lambda i: (0, chunk * tiles + i))
    out = pl.BlockSpec((rows, LANES), lambda i: (0, i))
    shape = jax.ShapeDtypeStruct((rows, width // chunks), BF16)
    return pl.pallas_call(
        forward_kernel,
        grid=(tiles,),
        in_specs=[
            here,
            here,
            here,
            pl.BlockSpec((FILT, LANES), lambda i: (0, chunk * tiles + i)),
            pl.BlockSpec((GPT * FILT, 2 * FILT), lambda i: (chunk * tiles + i, 0)),
        ],
        out_specs=[out, out],
        out_shape=[shape, shape],
        compiler_params=params(),
        cost_estimate=cost(tiles * rows * 2 * 2**18, tiles * rows * 5 * 256 + tiles * 2**19),
    )(q, k, v, prior, table)


def middle_kernel(own, others, q, k, v, mixed, prior, *rest):
    gq_out, gm_out, taps_out = rest[-3:]
    blocks = q.shape[0] // FILT
    total = own[...].astype(F32)
    for other in others:
        total = total + other[...].astype(F32)
    gg = total.astype(BF16).astype(F32)
    gq_out[...] = (gg * mixed[...].astype(F32)).astype(BF16)
    gm = (gg * q[...].astype(F32)).astype(BF16)
    gm_out[...] = gm
    ext = jnp.concatenate([prior[...], product_of(k[...], v[...])], axis=0)
    group = group_of_lane(FILT, 2 * LANES)
    lag = jnp.zeros((GPT * FILT, 2 * FILT), F32)
    for b in range(0, blocks, 2):
        lo = b * FILT
        pair = jnp.concatenate([gm[lo : lo + FILT], gm[lo + FILT : lo + 2 * FILT]], axis=1)
        stack = jnp.concatenate(
            [jnp.where(group == g, pair, jnp.zeros_like(pair)) for g in range(GPT)], axis=0
        )
        lag = lag + lax.dot_general(
            stack, windows(ext, b), (((1,), (1,)), ((), ())), preferred_element_type=F32
        )
    lag = lag.reshape(GPT, FILT, 2 * FILT)
    half = FILT // 2
    while half >= 8:
        lag = lag[:, :half] + pltpu.roll(lag[:, half:], 2 * FILT - half, 2)
        half //= 2
    while half >= 1:
        lag = lag + pltpu.roll(pltpu.roll(lag, 2 * FILT - half, 2), 8 - half, 1)
        half //= 2
    taps_out[...] = lag[:, 0, :]


def middle(own, others, q, k, v, mixed, prior, filled, chunk, chunks):
    rows, width = q.shape
    tiles = width // LANES // chunks
    groups = width // GROUP // chunks
    here = pl.BlockSpec((rows, LANES), lambda i: (0, chunk * tiles + i))
    part = pl.BlockSpec((rows, LANES), lambda i: (0, i))
    n_other = len(others)

    def kernel(own_ref, *refs):
        middle_kernel(own_ref, refs[:n_other], *refs[n_other:])

    args = [own, *others, q, k, v, mixed, prior]
    in_specs = [part] * (1 + n_other) + [here] * 3 + [part]
    in_specs.append(pl.BlockSpec((FILT, LANES), lambda i: (0, chunk * tiles + i)))
    aliases = {}
    if filled is not None:
        aliases = {len(args): 0}
        args.append(filled)
        in_specs.append(pl.BlockSpec(memory_space=pl.ANY))
    return pl.pallas_call(
        kernel,
        grid=(tiles,),
        in_specs=in_specs,
        out_specs=[here, part, pl.BlockSpec((GPT, 2 * FILT), lambda i: (i, 0))],
        out_shape=[
            jax.ShapeDtypeStruct((rows, width), BF16),
            jax.ShapeDtypeStruct((rows, width // chunks), BF16),
            jax.ShapeDtypeStruct((groups, 2 * FILT), F32),
        ],
        input_output_aliases=aliases,
        compiler_params=params(),
        cost_estimate=cost(tiles * rows * 2 * 2**18, tiles * rows * 9 * 256),
    )(*args)


def backward_kernel(gm, later, k, v, table, *rest):
    gk_out, gv_out = rest[-2:]
    blocks = gm.shape[0] // FILT
    ext = jnp.concatenate([gm[...], later[...]], axis=0)
    gp = toeplitz(table[...], ext, blocks)
    gk_out[...] = (gp * v[...].astype(F32)).astype(BF16)
    gv_out[...] = (gp * k[...].astype(F32)).astype(BF16)


def backward(gm, later, k, v, table, filled, chunk, chunks):
    rows, width = k.shape
    tiles = width // LANES // chunks
    here = pl.BlockSpec((rows, LANES), lambda i: (0, chunk * tiles + i))
    part = pl.BlockSpec((rows, LANES), lambda i: (0, i))
    args = [gm, later, k, v, table]
    in_specs = [
        part,
        pl.BlockSpec((FILT, LANES), lambda i: (0, i)),
        here,
        here,
        pl.BlockSpec((GPT * FILT, 2 * FILT), lambda i: (chunk * tiles + i, 0)),
    ]
    aliases = {}
    if filled is not None:
        aliases = {len(args): 0, len(args) + 1: 1}
        args += filled
        in_specs += [pl.BlockSpec(memory_space=pl.ANY)] * 2
    shape = jax.ShapeDtypeStruct((rows, width), BF16)
    return pl.pallas_call(
        backward_kernel,
        grid=(tiles,),
        in_specs=in_specs,
        out_specs=[here, here],
        out_shape=[shape, shape],
        input_output_aliases=aliases,
        compiler_params=params(),
        cost_estimate=cost(tiles * rows * 2 * 2**18, tiles * rows * 5 * 256 + tiles * 2**19),
    )(*args)


def gate_kernel(order, *refs):
    out = refs[-1]
    total = jnp.dot(refs[0][0], refs[LINE][...], preferred_element_type=F32)
    for j in range(1, LINE):
        total = total + jnp.dot(refs[j][0], refs[LINE + j][...], preferred_element_type=F32)
    out[...] = total.astype(out.dtype)


def gate_grad(order, cot, weights, dtype):
    _, rows, depth = cot.shape
    width = weights[0].shape[1]
    tile = min(256, rows)

    def cot_spec(j):
        return pl.BlockSpec((1, tile, depth), lambda i, order: (order[j], i, 0))

    weight_spec = pl.BlockSpec((depth, width), lambda i, order: (0, 0))
    return pl.pallas_call(
        gate_kernel,
        grid_spec=pltpu.PrefetchScalarGridSpec(
            num_scalar_prefetch=1,
            grid=(rows // tile,),
            in_specs=[cot_spec(j) for j in range(LINE)] + [weight_spec] * LINE,
            out_specs=pl.BlockSpec((tile, width), lambda i, order: (i, 0)),
        ),
        out_shape=jax.ShapeDtypeStruct((rows, width), dtype),
        compiler_params=params(),
        cost_estimate=cost(
            2 * rows * LINE * depth * width, 2 * LINE * depth * (rows + width) + 4 * rows * width
        ),
    )(order, *([cot] * LINE), *weights)


def shards(seq, ch, queries, keys, values, filters, grad_out, out_weight):
    inner = seq // LINE
    rows, width = queries.shape
    depth = out_weight.shape[0]
    chunks = 2 if width % (2 * LANES) == 0 else 1
    cols = width // chunks
    place = lax.axis_index("seq")
    z, y = place // inner, place % inner

    def send(x, pairs):
        return lax.ppermute(x, "seq", pairs)

    def along_line(x, pairs):
        return send(x, [(a * inner + i, b * inner + i) for a, b in pairs for i in range(inner)])

    def around_inner(x, shift):
        return send(
            x, [(a * inner + i, a * inner + (i + shift) % inner) for a in range(LINE) for i in range(inner)]
        )

    each = range(chunks)
    up_pairs, down_pairs = [(0, 1), (1, 2), (2, 3)], [(1, 0), (2, 1), (3, 2)]

    prior = send(
        product_of(keys[rows - FILT :], values[rows - FILT :]), [(i, i + 1) for i in range(seq - 1)]
    )
    paired = inner == 2 and ch == LINE
    other = grad_out
    if paired:
        kept = lax.dynamic_slice(grad_out, (0, y * depth), (rows, depth))
        other = lax.dynamic_slice(grad_out, (0, (1 - y) * depth), (rows, depth))
        cots = [lax.all_gather(kept, "ch", axis=0, tiled=False)]
    back, ahead = tables(filters)
    halves = [out_weight[:, h * cols : (h + 1) * cols] for h in each]
    prior, other, _, *halves = fence(prior, other, back[:8, :LANES], *halves)

    up1, down1 = [None] * chunks, [None] * chunks
    up1[0], down1[0] = along_line(halves[0], up_pairs), along_line(halves[0], down_pairs)
    if paired:
        swapped = around_inner(other, 1)
    else:
        full = lax.all_gather(other, "ch", axis=1, tiled=True)
        full = full.reshape(rows, LINE, inner, depth).transpose(2, 1, 0, 3)
        cots = []
        for shift in range(inner):
            part = lax.dynamic_index_in_dim(full, (y + shift) % inner, 0, keepdims=False)
            cots.append(part if shift == 0 else around_inner(part, shift))
        swapped = prior
    gateds, mixeds = [], []
    for h in each:
        gated, mixed = forward(queries, keys, values, prior, back, h, chunks)
        gateds.append([gated])
        mixeds.append(mixed)
    up1, down1, swapped, halves, gateds, cots = fence(up1, down1, swapped, halves, gateds, cots)

    def second_step(h):
        return along_line(up1[h], [(1, 2), (2, 3)]), along_line(down1[h], [(2, 1), (1, 0)])

    def swap_gated(h):
        return [around_inner(gateds[h][0], r) for r in range(1, inner)]

    second = [None] * chunks
    second[0] = second_step(0)
    for h in each[1:]:
        up1[h], down1[h] = along_line(halves[h], up_pairs), along_line(halves[h], down_pairs)
    if paired:
        cots.append(lax.all_gather(swapped, "ch", axis=0, tiled=False))
    got = swap_gated(0)
    second[0], got, up1, down1, gateds = fence(second[0], got, up1, down1, gateds)
    gateds[0] = gateds[0] + got

    def merge(pair):
        return jnp.where(z >= 2, *pair)

    def third_step(x):
        return along_line(x, [(2, 3), (1, 0)])

    third = [None] * chunks
    second[0] = merge(second[0])
    third[0] = third_step(second[0])
    for h in each[1:]:
        second[h] = second_step(h)
    got = [swap_gated(h) for h in each[1:]]

    def slots(h, second, third):
        slot_a = jnp.where(z == 0, down1[h], up1[h])
        slot_c = jnp.where((z == 0) | (z == 3), third, down1[h])
        return [halves[h], slot_a, second, slot_c]

    order = jnp.stack(
        [
            z,
            jnp.where(z == 0, 1, z - 1),
            jnp.where(z >= 2, z - 2, z + 2),
            jnp.where(z == 3, 0, jnp.where(z == 1, 2, 3)),
        ]
    ).astype(jnp.int32)

    def partial(block, h):
        total = None
        for cot, gated in zip(cots, gateds[h]):
            lhs = lax.dynamic_index_in_dim(cot, block, 0, keepdims=False)
            term = lax.dot_general(lhs, gated, (((0,), (0,)), ((), ())), preferred_element_type=F32)
            total = term if total is None else total + term
        return total

    second_block = jnp.where(z == 0, 2, jnp.where(z == 1, 3, jnp.where(z == 2, 0, 1)))

    def sum_first(h):
        return partial(jnp.where(z == 0, 3, 0), h).astype(BF16)

    def send_first(x):
        return along_line(x, [(0, 1), (3, 2)])

    def sum_second(h, got):
        return (partial(second_block, h) + got.astype(F32)).astype(BF16)

    def send_second(x):
        return along_line(x, [(0, 1), (3, 2)]), along_line(x, [(1, 2), (2, 1)])

    def sum_third(h, outer_in, inner_in):
        add_up = jnp.where(z == 1, outer_in, inner_in).astype(F32)
        add_down = jnp.where(z == 1, inner_in, outer_in).astype(F32)
        last_up = (partial(jnp.minimum(z + 1, 3), h) + add_up).astype(BF16)
        last_down = (partial(jnp.maximum(z - 1, 0), h) + add_down).astype(BF16)
        return last_up, last_down

    def send_third(last_up, last_down):
        return (
            along_line(last_up, [(0, 1), (1, 2), (2, 3)]),
            along_line(last_down, [(1, 0), (2, 1), (3, 2)]),
        )

    def sum_last(h, from_below, from_above):
        total = partial(z, h) + from_below.astype(F32) + from_above.astype(F32)
        return total.astype(BF16)

    def shares(h, weights):
        return [gate_grad(order, cots[r], weights, BF16) for r in range(1, inner)]

    def send_shares(parts):
        return [around_inner(part, inner - r) for r, part in enumerate(parts, 1)]

    sums = [None] * chunks
    others = [None] * chunks
    weights = [None] * chunks
    latest = sum_first(0)
    sums[0] = send_first(latest)
    middle_share = partial(second_block, 0)
    third[0], sums[0], second, got, middle_share = fence(
        third[0], sums[0], second, got, middle_share
    )
    for h in each[1:]:
        gateds[h] += got[h - 1]

    for h in each[1:]:
        second[h] = merge(second[h])
        third[h] = third_step(second[h])
    latest = (middle_share + sums[0].astype(F32)).astype(BF16)
    sums[0] = send_second(latest)
    weights[0] = slots(0, second[0], third[0])
    parts = shares(0, after(weights[0], latest))
    others[0] = send_shares(parts)
    for h in each[1:]:
        latest = after(sum_first(h), parts)
        sums[h] = send_first(latest)
    for h in each[1:]:
        weights[h] = slots(h, second[h], third[h])
        parts = shares(h, after(weights[h], latest))
        others[h] = send_shares(parts)
    latest = sum_third(0, *after(sums[0], parts))
    sums[0] = send_third(*latest)
    for h in each[1:]:
        latest = sum_second(h, after(sums[h], latest))
        sums[h] = send_second(latest)
    owns = [gate_grad(order, cots[0], after(weights[h], latest), F32) for h in each]
    for h in each[1:]:
        latest = sum_third(h, *sums[h])
        sums[h] = send_third(*latest)

    grad_queries = None
    grad_kv = None
    taps = []
    for h in range(chunks):
        here = slice(h * cols, (h + 1) * cols)
        grad_queries, gm, lag = middle(
            owns[h], others[h], queries, keys, values, mixeds[h], prior, grad_queries, h, chunks
        )
        later = send(gm[:FILT], [(i + 1, i) for i in range(seq - 1)])
        grad_kv = backward(gm, later, keys, values, ahead, grad_kv, h, chunks)
        taps.append(lag)
    grad_weight = jnp.concatenate([sum_last(h, *sums[h]) for h in each], axis=1)
    taps = jnp.concatenate(taps, axis=0)[:, 1 : FILT + 1][:, ::-1]
    taps = taps.T.reshape(seq, FILT // seq, -1)
    taps = jnp.sum(lax.all_to_all(taps, "seq", 0, 0), axis=0)
    return grad_queries, *grad_kv, taps.T, grad_weight


def solution(mesh):
    sizes = dict(mesh.shape)
    return jax.shard_map(
        functools.partial(shards, sizes["seq"], sizes["ch"]),
        mesh=mesh,
        in_specs=(
            P("seq", "ch"),
            P("seq", "ch"),
            P("seq", "ch"),
            P("ch", None),
            P("seq", "ch"),
            P("seq", "ch"),
        ),
        out_specs=(P("seq", "ch"), P("seq", "ch"), P("seq", "ch"), P("ch", "seq"), P("seq", "ch")),
        check_vma=False,
    )
```

```python
import functools

import jax
import jax.numpy as jnp
from jax import lax
from jax.experimental import pallas as pl
from jax.experimental.pallas import tpu as pltpu
from jax.sharding import PartitionSpec as P

GROUP = 16
FILT = 128
LANES = 128
GPT = LANES // GROUP
LINE = 4
F32 = jnp.float32
BF16 = jnp.bfloat16
VMEM_LIMIT = 48 * 1024 * 1024


def params():
    return pltpu.CompilerParams(vmem_limit_bytes=VMEM_LIMIT)


def cost(flops, nbytes):
    return pl.CostEstimate(flops=int(flops) // 64, bytes_accessed=int(nbytes) // 64, transcendentals=0)


def fence(*arrays):
    return lax.optimization_barrier(arrays)


def after(x, *others):
    return lax.optimization_barrier((x, *others))[0]


def table_kernel(back_ref, ahead_ref, back_out, ahead_out):
    for seed, out in ((back_ref, back_out), (ahead_ref, ahead_out)):
        for g in range(GPT):
            rows = jnp.broadcast_to(seed[g : g + 1, :], (FILT, 2 * FILT))
            turned = pltpu.roll(rows, 0, 1, stride=1, stride_axis=0)
            out[g * FILT : (g + 1) * FILT, :] = turned.astype(BF16)


def tables(filters):
    groups = filters.shape[0]
    taps = filters.astype(F32)
    back = jnp.concatenate(
        [jnp.zeros((groups, 1), F32), taps[:, ::-1], jnp.zeros((groups, FILT - 1), F32)], axis=1
    )
    ahead = jnp.concatenate([taps, jnp.zeros((groups, FILT), F32)], axis=1)
    seed = pl.BlockSpec((GPT, 2 * FILT), lambda i: (i, 0))
    full = pl.BlockSpec((GPT * FILT, 2 * FILT), lambda i: (i, 0))
    shape = jax.ShapeDtypeStruct((groups * FILT, 2 * FILT), BF16)
    return pl.pallas_call(
        table_kernel,
        grid=(groups // GPT,),
        in_specs=[seed, seed],
        out_specs=[full, full],
        out_shape=[shape, shape],
        compiler_params=params(),
        cost_estimate=cost(groups * 2**18, groups * 2**17),
    )(back, ahead)


def group_of_lane(rows, cols):
    return (lax.broadcasted_iota(jnp.int32, (rows, cols), 1) % LANES) // GROUP


def windows(ext, b):
    lo = b * FILT
    return jnp.concatenate([ext[lo : lo + 2 * FILT], ext[lo + FILT : lo + 3 * FILT]], axis=1)


def toeplitz(table, ext, blocks):
    group = group_of_lane(FILT, 2 * LANES)
    rows = []
    for b in range(0, blocks, 2):
        out = jnp.dot(table, windows(ext, b), preferred_element_type=F32)
        picked = out[:FILT]
        for g in range(1, GPT):
            picked = jnp.where(group == g, out[g * FILT : (g + 1) * FILT], picked)
        rows += [picked[:, :LANES], picked[:, LANES:]]
    return jnp.concatenate(rows, axis=0)


def product_of(k, v):
    return (k.astype(F32) * v.astype(F32)).astype(BF16)


def forward_kernel(q, k, v, prior, table, gated, mixed_out):
    blocks = q.shape[0] // FILT
    ext = jnp.concatenate([prior[...], product_of(k[...], v[...])], axis=0)
    mixed = toeplitz(table[...], ext, blocks)
    mixed_out[...] = mixed.astype(BF16)
    gated[...] = (q[...].astype(F32) * mixed).astype(BF16)


def forward(q, k, v, prior, table, chunk, chunks):
    rows, width = q.shape
    tiles = width // LANES // chunks
    here = pl.BlockSpec((rows, LANES), lambda i: (0, chunk * tiles + i))
    out = pl.BlockSpec((rows, LANES), lambda i: (0, i))
    shape = jax.ShapeDtypeStruct((rows, width // chunks), BF16)
    return pl.pallas_call(
        forward_kernel,
        grid=(tiles,),
        in_specs=[
            here,
            here,
            here,
            pl.BlockSpec((FILT, LANES), lambda i: (0, i)),
            pl.BlockSpec((GPT * FILT, 2 * FILT), lambda i: (chunk * tiles + i, 0)),
        ],
        out_specs=[out, out],
        out_shape=[shape, shape],
        compiler_params=params(),
        cost_estimate=cost(tiles * rows * 2 * 2**18, tiles * rows * 5 * 256 + tiles * 2**19),
    )(q, k, v, prior, table)


def middle_kernel(own, others, q, k, v, mixed, prior, *rest):
    gq_out, gm_out, taps_out = rest[-3:]
    blocks = q.shape[0] // FILT
    total = own[...].astype(F32)
    for other in others:
        total = total + other[...].astype(F32)
    gg = total.astype(BF16).astype(F32)
    gq_out[...] = (gg * mixed[...].astype(F32)).astype(BF16)
    gm = (gg * q[...].astype(F32)).astype(BF16)
    gm_out[...] = gm
    ext = jnp.concatenate([prior[...], product_of(k[...], v[...])], axis=0)
    group = group_of_lane(FILT, 2 * LANES)
    lag = jnp.zeros((GPT * FILT, 2 * FILT), F32)
    for b in range(0, blocks, 2):
        lo = b * FILT
        pair = jnp.concatenate([gm[lo : lo + FILT], gm[lo + FILT : lo + 2 * FILT]], axis=1)
        stack = jnp.concatenate(
            [jnp.where(group == g, pair, jnp.zeros_like(pair)) for g in range(GPT)], axis=0
        )
        lag = lag + lax.dot_general(
            stack, windows(ext, b), (((1,), (1,)), ((), ())), preferred_element_type=F32
        )
    lag = lag.reshape(GPT, FILT, 2 * FILT)
    half = FILT // 2
    while half >= 8:
        lag = lag[:, :half] + pltpu.roll(lag[:, half:], 2 * FILT - half, 2)
        half //= 2
    while half >= 1:
        lag = lag + pltpu.roll(pltpu.roll(lag, 2 * FILT - half, 2), 8 - half, 1)
        half //= 2
    taps_out[...] = lag[:, 0, :]


def middle(own, others, q, k, v, mixed, prior, filled, chunk, chunks):
    rows, width = q.shape
    tiles = width // LANES // chunks
    groups = width // GROUP // chunks
    here = pl.BlockSpec((rows, LANES), lambda i: (0, chunk * tiles + i))
    part = pl.BlockSpec((rows, LANES), lambda i: (0, i))
    n_other = len(others)

    def kernel(own_ref, *refs):
        middle_kernel(own_ref, refs[:n_other], *refs[n_other:])

    args = [own, *others, q, k, v, mixed, prior]
    in_specs = [part] * (1 + n_other) + [here] * 3 + [part]
    in_specs.append(pl.BlockSpec((FILT, LANES), lambda i: (0, i)))
    aliases = {}
    if filled is not None:
        aliases = {len(args): 0}
        args.append(filled)
        in_specs.append(pl.BlockSpec(memory_space=pl.ANY))
    return pl.pallas_call(
        kernel,
        grid=(tiles,),
        in_specs=in_specs,
        out_specs=[here, part, pl.BlockSpec((GPT, 2 * FILT), lambda i: (i, 0))],
        out_shape=[
            jax.ShapeDtypeStruct((rows, width), BF16),
            jax.ShapeDtypeStruct((rows, width // chunks), BF16),
            jax.ShapeDtypeStruct((groups, 2 * FILT), F32),
        ],
        input_output_aliases=aliases,
        compiler_params=params(),
        cost_estimate=cost(tiles * rows * 2 * 2**18, tiles * rows * 9 * 256),
    )(*args)


def backward_kernel(gm, later, k, v, table, *rest):
    gk_out, gv_out = rest[-2:]
    blocks = gm.shape[0] // FILT
    ext = jnp.concatenate([gm[...], later[...]], axis=0)
    gp = toeplitz(table[...], ext, blocks)
    gk_out[...] = (gp * v[...].astype(F32)).astype(BF16)
    gv_out[...] = (gp * k[...].astype(F32)).astype(BF16)


def backward(gm, later, k, v, table, filled, chunk, chunks):
    rows, width = k.shape
    tiles = width // LANES // chunks
    here = pl.BlockSpec((rows, LANES), lambda i: (0, chunk * tiles + i))
    part = pl.BlockSpec((rows, LANES), lambda i: (0, i))
    args = [gm, later, k, v, table]
    in_specs = [
        part,
        pl.BlockSpec((FILT, LANES), lambda i: (0, i)),
        here,
        here,
        pl.BlockSpec((GPT * FILT, 2 * FILT), lambda i: (chunk * tiles + i, 0)),
    ]
    aliases = {}
    if filled is not None:
        aliases = {len(args): 0, len(args) + 1: 1}
        args += filled
        in_specs += [pl.BlockSpec(memory_space=pl.ANY)] * 2
    shape = jax.ShapeDtypeStruct((rows, width), BF16)
    return pl.pallas_call(
        backward_kernel,
        grid=(tiles,),
        in_specs=in_specs,
        out_specs=[here, here],
        out_shape=[shape, shape],
        input_output_aliases=aliases,
        compiler_params=params(),
        cost_estimate=cost(tiles * rows * 2 * 2**18, tiles * rows * 5 * 256 + tiles * 2**19),
    )(*args)


def gate_kernel(order, *refs):
    out = refs[-1]
    total = jnp.dot(refs[0][0], refs[LINE][...], preferred_element_type=F32)
    for j in range(1, LINE):
        total = total + jnp.dot(refs[j][0], refs[LINE + j][...], preferred_element_type=F32)
    out[...] = total.astype(out.dtype)


def gate_grad(order, cot, weights, dtype):
    _, rows, depth = cot.shape
    width = weights[0].shape[1]
    tile = min(256, rows)

    def cot_spec(j):
        return pl.BlockSpec((1, tile, depth), lambda i, order: (order[j], i, 0))

    weight_spec = pl.BlockSpec((depth, width), lambda i, order: (0, 0))
    return pl.pallas_call(
        gate_kernel,
        grid_spec=pltpu.PrefetchScalarGridSpec(
            num_scalar_prefetch=1,
            grid=(rows // tile,),
            in_specs=[cot_spec(j) for j in range(LINE)] + [weight_spec] * LINE,
            out_specs=pl.BlockSpec((tile, width), lambda i, order: (i, 0)),
        ),
        out_shape=jax.ShapeDtypeStruct((rows, width), dtype),
        compiler_params=params(),
        cost_estimate=cost(
            2 * rows * LINE * depth * width, 2 * LINE * depth * (rows + width) + 4 * rows * width
        ),
    )(order, *([cot] * LINE), *weights)


def rows_kernel(n, pick, *refs):
    out = refs[-1]
    total = None
    for cot, gated in zip(refs[:n], refs[n : 2 * n]):
        term = lax.dot_general(
            cot[0], gated[...], (((0,), (0,)), ((), ())), preferred_element_type=F32
        )
        total = term if total is None else total + term
    for j, came in enumerate(refs[2 * n : -1], 1):
        total = total + came[...].astype(F32) * pick[j].astype(F32)
    out[...] = total.astype(out.dtype)


def weight_rows(pick, cots, gateds, came, dtype):
    _, rows, depth = cots[0].shape
    width = gateds[0].shape[1]
    tile = min(512, width)
    n = len(cots)
    cot_spec = pl.BlockSpec((1, rows, depth), lambda i, pick: (pick[0], 0, 0))
    gated_spec = pl.BlockSpec((rows, tile), lambda i, pick: (0, i))
    out_spec = pl.BlockSpec((depth, tile), lambda i, pick: (0, i))
    return pl.pallas_call(
        functools.partial(rows_kernel, n),
        grid_spec=pltpu.PrefetchScalarGridSpec(
            num_scalar_prefetch=1,
            grid=(width // tile,),
            in_specs=[cot_spec] * n + [gated_spec] * n + [out_spec] * len(came),
            out_specs=out_spec,
        ),
        out_shape=jax.ShapeDtypeStruct((depth, width), dtype),
        compiler_params=params(),
        cost_estimate=cost(2 * n * rows * depth * width, 2 * n * rows * (depth + width)),
    )(pick, *cots, *gateds, *came)


def shards(seq, ch, queries, keys, values, filters, grad_out, out_weight):
    inner = seq // LINE
    rows, width = queries.shape
    depth = out_weight.shape[0]
    chunks = 2 if width % (2 * LANES) == 0 else 1
    cols = width // chunks
    place = lax.axis_index("seq")
    z, y = place // inner, place % inner

    def send(x, pairs):
        return lax.ppermute(x, "seq", pairs)

    def along_line(x, pairs):
        return send(x, [(a * inner + i, b * inner + i) for a, b in pairs for i in range(inner)])

    def around_inner(x, shift):
        return send(
            x, [(a * inner + i, a * inner + (i + shift) % inner) for a in range(LINE) for i in range(inner)]
        )

    each = range(chunks)
    up_pairs, down_pairs = [(0, 1), (1, 2), (2, 3)], [(1, 0), (2, 1), (3, 2)]

    priors = []
    for h in each:
        tail = (slice(rows - FILT, rows), slice(h * cols, (h + 1) * cols))
        priors.append(
            send(product_of(keys[tail], values[tail]), [(i, i + 1) for i in range(seq - 1)])
        )
    paired = inner == 2 and ch == LINE
    other = grad_out
    cots = []
    if paired:
        kept = lax.dynamic_slice(grad_out, (0, y * depth), (rows, depth))
        other = lax.dynamic_slice(grad_out, (0, (1 - y) * depth), (rows, depth))
        cots = [lax.all_gather(kept, "ch", axis=0, tiled=False)]
    back, ahead = tables(filters)
    halves = [out_weight[:, h * cols : (h + 1) * cols] for h in each]
    priors[0], other, halves = fence(priors[0], other, halves)

    up1, down1 = [None] * chunks, [None] * chunks
    up1[0], down1[0] = along_line(halves[0], up_pairs), along_line(halves[0], down_pairs)
    swapped = around_inner(other, 1) if paired else other
    gateds, mixeds = [None] * chunks, [None] * chunks
    gateds[0], mixeds[0] = forward(queries, keys, values, priors[0], back, 0, chunks)
    up1, down1, swapped, halves, gateds, cots, priors = fence(
        up1, down1, swapped, halves, gateds, cots, priors
    )

    def second_step(h):
        return along_line(up1[h], [(1, 2), (2, 3)]), along_line(down1[h], [(2, 1), (1, 0)])

    def swap_gated(h):
        return [around_inner(gateds[h], r) for r in range(1, inner)]

    second = [None] * chunks
    second[0] = second_step(0)
    for h in each[1:]:
        up1[h], down1[h] = along_line(halves[h], up_pairs), along_line(halves[h], down_pairs)
    if paired:
        cots.append(lax.all_gather(swapped, "ch", axis=0, tiled=False))
    else:
        full = lax.all_gather(swapped, "ch", axis=1, tiled=True)
        full = full.reshape(rows, LINE, inner, depth).transpose(2, 1, 0, 3)
        for shift in range(inner):
            part = lax.dynamic_index_in_dim(full, (y + shift) % inner, 0, keepdims=False)
            cots.append(part if shift == 0 else around_inner(part, shift))
    got = [None] * chunks
    got[0] = swap_gated(0)
    for h in each[1:]:
        gateds[h], mixeds[h] = forward(queries, keys, values, priors[h], back, h, chunks)
    second[0], got, up1, down1, gateds = fence(second[0], got, up1, down1, gateds)

    def merge(pair):
        return jnp.where(z >= 2, *pair)

    def third_step(x):
        return along_line(x, [(2, 3), (1, 0)])

    def slots(h):
        slot_a = jnp.where(z == 0, down1[h], up1[h])
        slot_c = jnp.where((z == 0) | (z == 3), third[h], down1[h])
        return [halves[h], slot_a, second[h], slot_c]

    order = jnp.stack(
        [
            z,
            jnp.where(z == 0, 1, z - 1),
            jnp.where(z >= 2, z - 2, z + 2),
            jnp.where(z == 3, 0, jnp.where(z == 1, 2, 3)),
        ]
    ).astype(jnp.int32)

    first_block = jnp.where(z == 0, 3, 0)
    second_block = jnp.where(z == 0, 2, jnp.where(z == 1, 3, jnp.where(z == 2, 0, 1)))
    at_one, at_two = z == 1, z == 2

    def block_rows(block, h, *came):
        pick = [block] + [flag for _, flag in came]
        pick = jnp.stack([jnp.asarray(p, jnp.int32) for p in pick])
        return weight_rows(pick, cots, [gateds[h]] + got[h], [x for x, _ in came], BF16)

    def send_first(x):
        return along_line(x, [(0, 1), (3, 2)])

    def send_second(x):
        return along_line(x, [(0, 1), (3, 2)]), along_line(x, [(1, 2), (2, 1)])

    def sum_third(h, outer_in, inner_in):
        return (
            block_rows(jnp.minimum(z + 1, 3), h, (outer_in, at_one), (inner_in, at_two)),
            block_rows(jnp.maximum(z - 1, 0), h, (inner_in, at_one), (outer_in, at_two)),
        )

    def send_third(last_up, last_down):
        return along_line(last_up, up_pairs), along_line(last_down, down_pairs)

    def shares(h, weights):
        return [gate_grad(order, cots[r], weights, BF16) for r in range(1, inner)]

    def send_shares(parts):
        return [around_inner(part, inner - r) for r, part in enumerate(parts, 1)]

    third, sums, parts, others, owns = ([None] * chunks for _ in range(5))
    second[0] = merge(second[0])
    third[0] = third_step(second[0])
    for h in each[1:]:
        second[h] = second_step(h)
        got[h] = swap_gated(h)
    sums[0] = send_first(block_rows(first_block, 0))
    weights = slots(0)
    parts[0] = shares(0, weights)
    owns[0] = gate_grad(order, cots[0], weights, F32)
    others[0] = send_shares(parts[0])
    sums, second, got, parts, owns = fence(sums, second, got, parts, owns)

    for h in each[1:]:
        second[h] = merge(second[h])
        third[h] = third_step(second[h])
    sums[0] = send_second(block_rows(second_block, 0, (sums[0], 1)))
    for h in each[1:]:
        sums[h] = send_first(block_rows(first_block, h))
    for h in each[1:]:
        weights = slots(h)
        parts[h] = shares(h, weights)
        owns[h] = gate_grad(order, cots[0], weights, F32)
        others[h] = send_shares(parts[h])
    sums, parts, owns = fence(sums, parts, owns)

    ready = [block_rows(second_block, h, (sums[h], 1)) for h in each[1:]]
    last = sum_third(0, *sums[0])
    ready, last, others[0] = fence(ready, last, others[0])
    sums[0] = send_third(*last)
    for h in each[1:]:
        sums[h] = send_second(ready[h - 1])

    grad_queries = None
    grad_kv = None
    taps = [None] * chunks
    for h in each:
        grad_queries, gm, taps[h] = middle(
            owns[h], others[h], queries, keys, values, mixeds[h], priors[h], grad_queries, h, chunks
        )
        later = send(gm[:FILT], [(i + 1, i) for i in range(seq - 1)])
        grad_kv = backward(gm, later, keys, values, ahead, grad_kv, h, chunks)
        if h == 0:
            sums, grad_kv, others = fence(sums, grad_kv, others)
            for g in each[1:]:
                sums[g] = send_third(*sum_third(g, *sums[g]))
    sums[-1], grad_kv = fence(sums[-1], grad_kv)
    done = [block_rows(z, h, *((x, 1) for x in sums[h])) for h in each]
    grad_weight = jnp.concatenate(done, axis=1)
    taps = jnp.concatenate(taps, axis=0)[:, 1 : FILT + 1][:, ::-1]
    taps = taps.T.reshape(seq, FILT // seq, -1)
    taps = jnp.sum(lax.all_to_all(taps, "seq", 0, 0), axis=0)
    return grad_queries, *grad_kv, taps.T, grad_weight


def solution(mesh):
    sizes = dict(mesh.shape)
    return jax.shard_map(
        functools.partial(shards, sizes["seq"], sizes["ch"]),
        mesh=mesh,
        in_specs=(
            P("seq", "ch"),
            P("seq", "ch"),
            P("seq", "ch"),
            P("ch", None),
            P("seq", "ch"),
            P("seq", "ch"),
        ),
        out_specs=(P("seq", "ch"), P("seq", "ch"), P("seq", "ch"), P("ch", "seq"), P("seq", "ch")),
        check_vma=False,
    )
```

```python
import functools

import jax
import jax.numpy as jnp
from jax import lax
from jax.experimental import pallas as pl
from jax.experimental.pallas import tpu as pltpu
from jax.sharding import PartitionSpec as P

GROUP = 16
FILT = 128
LANES = 128
GPT = LANES // GROUP
LINE = 4
F32 = jnp.float32
BF16 = jnp.bfloat16
VMEM_LIMIT = 48 * 1024 * 1024


def params():
    return pltpu.CompilerParams(vmem_limit_bytes=VMEM_LIMIT)


def cost(flops, nbytes):
    return pl.CostEstimate(flops=int(flops) // 64, bytes_accessed=int(nbytes) // 64, transcendentals=0)


def fence(*arrays):
    return lax.optimization_barrier(arrays)


def after(x, *others):
    return lax.optimization_barrier((x, *others))[0]


def table_kernel(back_ref, ahead_ref, back_out, ahead_out):
    for seed, out in ((back_ref, back_out), (ahead_ref, ahead_out)):
        for g in range(GPT):
            rows = jnp.broadcast_to(seed[g : g + 1, :], (FILT, 2 * FILT))
            turned = pltpu.roll(rows, 0, 1, stride=1, stride_axis=0)
            out[g * FILT : (g + 1) * FILT, :] = turned.astype(BF16)


def tables(filters):
    groups = filters.shape[0]
    taps = filters.astype(F32)
    back = jnp.concatenate(
        [jnp.zeros((groups, 1), F32), taps[:, ::-1], jnp.zeros((groups, FILT - 1), F32)], axis=1
    )
    ahead = jnp.concatenate([taps, jnp.zeros((groups, FILT), F32)], axis=1)
    seed = pl.BlockSpec((GPT, 2 * FILT), lambda i: (i, 0))
    full = pl.BlockSpec((GPT * FILT, 2 * FILT), lambda i: (i, 0))
    shape = jax.ShapeDtypeStruct((groups * FILT, 2 * FILT), BF16)
    return pl.pallas_call(
        table_kernel,
        grid=(groups // GPT,),
        in_specs=[seed, seed],
        out_specs=[full, full],
        out_shape=[shape, shape],
        compiler_params=params(),
        cost_estimate=cost(groups * 2**18, groups * 2**17),
    )(back, ahead)


def group_of_lane(rows, cols):
    return (lax.broadcasted_iota(jnp.int32, (rows, cols), 1) % LANES) // GROUP


def windows(ext, b):
    lo = b * FILT
    return jnp.concatenate([ext[lo : lo + 2 * FILT], ext[lo + FILT : lo + 3 * FILT]], axis=1)


def toeplitz(table, ext, blocks):
    group = group_of_lane(FILT, 2 * LANES)
    rows = []
    for b in range(0, blocks, 2):
        out = jnp.dot(table, windows(ext, b), preferred_element_type=F32)
        picked = out[:FILT]
        for g in range(1, GPT):
            picked = jnp.where(group == g, out[g * FILT : (g + 1) * FILT], picked)
        rows += [picked[:, :LANES], picked[:, LANES:]]
    return jnp.concatenate(rows, axis=0)


def product_of(k, v):
    return (k.astype(F32) * v.astype(F32)).astype(BF16)


def forward_kernel(q, k, v, prior, table, gated, mixed_out):
    blocks = q.shape[0] // FILT
    ext = jnp.concatenate([prior[...], product_of(k[...], v[...])], axis=0)
    mixed = toeplitz(table[...], ext, blocks)
    mixed_out[...] = mixed.astype(BF16)
    gated[...] = (q[...].astype(F32) * mixed).astype(BF16)


def forward(q, k, v, prior, table, chunk, chunks):
    rows, width = q.shape
    tiles = width // LANES // chunks
    here = pl.BlockSpec((rows, LANES), lambda i: (0, chunk * tiles + i))
    out = pl.BlockSpec((rows, LANES), lambda i: (0, i))
    shape = jax.ShapeDtypeStruct((rows, width // chunks), BF16)
    return pl.pallas_call(
        forward_kernel,
        grid=(tiles,),
        in_specs=[
            here,
            here,
            here,
            pl.BlockSpec((FILT, LANES), lambda i: (0, chunk * tiles + i)),
            pl.BlockSpec((GPT * FILT, 2 * FILT), lambda i: (chunk * tiles + i, 0)),
        ],
        out_specs=[out, out],
        out_shape=[shape, shape],
        compiler_params=params(),
        cost_estimate=cost(tiles * rows * 2 * 2**18, tiles * rows * 5 * 256 + tiles * 2**19),
    )(q, k, v, prior, table)


def middle_kernel(own, others, q, k, v, mixed, prior, *rest):
    gq_out, gm_out, taps_out = rest[-3:]
    blocks = q.shape[0] // FILT
    total = own[...].astype(F32)
    for other in others:
        total = total + other[...].astype(F32)
    gg = total.astype(BF16).astype(F32)
    gq_out[...] = (gg * mixed[...].astype(F32)).astype(BF16)
    gm = (gg * q[...].astype(F32)).astype(BF16)
    gm_out[...] = gm
    ext = jnp.concatenate([prior[...], product_of(k[...], v[...])], axis=0)
    group = group_of_lane(FILT, 2 * LANES)
    lag = jnp.zeros((GPT * FILT, 2 * FILT), F32)
    for b in range(0, blocks, 2):
        lo = b * FILT
        pair = jnp.concatenate([gm[lo : lo + FILT], gm[lo + FILT : lo + 2 * FILT]], axis=1)
        stack = jnp.concatenate(
            [jnp.where(group == g, pair, jnp.zeros_like(pair)) for g in range(GPT)], axis=0
        )
        lag = lag + lax.dot_general(
            stack, windows(ext, b), (((1,), (1,)), ((), ())), preferred_element_type=F32
        )
    lag = lag.reshape(GPT, FILT, 2 * FILT)
    half = FILT // 2
    while half >= 8:
        lag = lag[:, :half] + pltpu.roll(lag[:, half:], 2 * FILT - half, 2)
        half //= 2
    while half >= 1:
        lag = lag + pltpu.roll(pltpu.roll(lag, 2 * FILT - half, 2), 8 - half, 1)
        half //= 2
    taps_out[...] = lag[:, 0, :]


def middle(own, others, q, k, v, mixed, prior, filled, chunk, chunks):
    rows, width = q.shape
    tiles = width // LANES // chunks
    groups = width // GROUP // chunks
    here = pl.BlockSpec((rows, LANES), lambda i: (0, chunk * tiles + i))
    part = pl.BlockSpec((rows, LANES), lambda i: (0, i))
    n_other = len(others)

    def kernel(own_ref, *refs):
        middle_kernel(own_ref, refs[:n_other], *refs[n_other:])

    args = [own, *others, q, k, v, mixed, prior]
    in_specs = [part] * (1 + n_other) + [here] * 3 + [part]
    in_specs.append(pl.BlockSpec((FILT, LANES), lambda i: (0, chunk * tiles + i)))
    aliases = {}
    if filled is not None:
        aliases = {len(args): 0}
        args.append(filled)
        in_specs.append(pl.BlockSpec(memory_space=pl.ANY))
    return pl.pallas_call(
        kernel,
        grid=(tiles,),
        in_specs=in_specs,
        out_specs=[here, part, pl.BlockSpec((GPT, 2 * FILT), lambda i: (i, 0))],
        out_shape=[
            jax.ShapeDtypeStruct((rows, width), BF16),
            jax.ShapeDtypeStruct((rows, width // chunks), BF16),
            jax.ShapeDtypeStruct((groups, 2 * FILT), F32),
        ],
        input_output_aliases=aliases,
        compiler_params=params(),
        cost_estimate=cost(tiles * rows * 2 * 2**18, tiles * rows * 9 * 256),
    )(*args)


def backward_kernel(gm, later, k, v, table, *rest):
    gk_out, gv_out = rest[-2:]
    blocks = gm.shape[0] // FILT
    ext = jnp.concatenate([gm[...], later[...]], axis=0)
    gp = toeplitz(table[...], ext, blocks)
    gk_out[...] = (gp * v[...].astype(F32)).astype(BF16)
    gv_out[...] = (gp * k[...].astype(F32)).astype(BF16)


def backward(gm, later, k, v, table, filled, chunk, chunks):
    rows, width = k.shape
    tiles = width // LANES // chunks
    here = pl.BlockSpec((rows, LANES), lambda i: (0, chunk * tiles + i))
    part = pl.BlockSpec((rows, LANES), lambda i: (0, i))
    args = [gm, later, k, v, table]
    in_specs = [
        part,
        pl.BlockSpec((FILT, LANES), lambda i: (0, i)),
        here,
        here,
        pl.BlockSpec((GPT * FILT, 2 * FILT), lambda i: (chunk * tiles + i, 0)),
    ]
    aliases = {}
    if filled is not None:
        aliases = {len(args): 0, len(args) + 1: 1}
        args += filled
        in_specs += [pl.BlockSpec(memory_space=pl.ANY)] * 2
    shape = jax.ShapeDtypeStruct((rows, width), BF16)
    return pl.pallas_call(
        backward_kernel,
        grid=(tiles,),
        in_specs=in_specs,
        out_specs=[here, here],
        out_shape=[shape, shape],
        input_output_aliases=aliases,
        compiler_params=params(),
        cost_estimate=cost(tiles * rows * 2 * 2**18, tiles * rows * 5 * 256 + tiles * 2**19),
    )(*args)


def gate_kernel(order, *refs):
    out = refs[-1]
    total = jnp.dot(refs[0][0], refs[LINE][...], preferred_element_type=F32)
    for j in range(1, LINE):
        total = total + jnp.dot(refs[j][0], refs[LINE + j][...], preferred_element_type=F32)
    out[...] = total.astype(out.dtype)


def gate_grad(order, cot, weights, dtype):
    _, rows, depth = cot.shape
    width = weights[0].shape[1]
    tile = min(256, rows)

    def cot_spec(j):
        return pl.BlockSpec((1, tile, depth), lambda i, order: (order[j], i, 0))

    weight_spec = pl.BlockSpec((depth, width), lambda i, order: (0, 0))
    return pl.pallas_call(
        gate_kernel,
        grid_spec=pltpu.PrefetchScalarGridSpec(
            num_scalar_prefetch=1,
            grid=(rows // tile,),
            in_specs=[cot_spec(j) for j in range(LINE)] + [weight_spec] * LINE,
            out_specs=pl.BlockSpec((tile, width), lambda i, order: (i, 0)),
        ),
        out_shape=jax.ShapeDtypeStruct((rows, width), dtype),
        compiler_params=params(),
        cost_estimate=cost(
            2 * rows * LINE * depth * width, 2 * LINE * depth * (rows + width) + 4 * rows * width
        ),
    )(order, *([cot] * LINE), *weights)


def rows_kernel(n, pick, *refs):
    out = refs[-1]
    total = None
    for cot, gated in zip(refs[:n], refs[n : 2 * n]):
        term = lax.dot_general(
            cot[0], gated[...], (((0,), (0,)), ((), ())), preferred_element_type=F32
        )
        total = term if total is None else total + term
    out[...] = total.astype(out.dtype)


def weight_rows(pick, cots, gateds, dtype):
    _, rows, depth = cots[0].shape
    width = gateds[0].shape[1]
    tile = min(512, width)
    n = len(cots)
    cot_spec = pl.BlockSpec((1, rows, depth), lambda i, pick: (pick[0], 0, 0))
    gated_spec = pl.BlockSpec((rows, tile), lambda i, pick: (0, i))
    return pl.pallas_call(
        functools.partial(rows_kernel, n),
        grid_spec=pltpu.PrefetchScalarGridSpec(
            num_scalar_prefetch=1,
            grid=(width // tile,),
            in_specs=[cot_spec] * n + [gated_spec] * n,
            out_specs=pl.BlockSpec((depth, tile), lambda i, pick: (0, i)),
        ),
        out_shape=jax.ShapeDtypeStruct((depth, width), dtype),
        compiler_params=params(),
        cost_estimate=cost(2 * n * rows * depth * width, 2 * n * rows * (depth + width)),
    )(pick, *cots, *gateds)


def shards(seq, ch, queries, keys, values, filters, grad_out, out_weight):
    inner = seq // LINE
    rows, width = queries.shape
    depth = out_weight.shape[0]
    chunks = 2 if width % (2 * LANES) == 0 else 1
    cols = width // chunks
    place = lax.axis_index("seq")
    z, y = place // inner, place % inner

    def send(x, pairs):
        return lax.ppermute(x, "seq", pairs)

    def along_line(x, pairs):
        return send(x, [(a * inner + i, b * inner + i) for a, b in pairs for i in range(inner)])

    def around_inner(x, shift):
        return send(
            x, [(a * inner + i, a * inner + (i + shift) % inner) for a in range(LINE) for i in range(inner)]
        )

    each = range(chunks)
    up_pairs, down_pairs = [(0, 1), (1, 2), (2, 3)], [(1, 0), (2, 1), (3, 2)]

    def second_step(h):
        return along_line(up1[h], [(1, 2), (2, 3)]), along_line(down1[h], [(2, 1), (1, 0)])

    def third_step(x):
        return along_line(x, [(2, 3), (1, 0)])

    def merge(pair):
        return jnp.where(z >= 2, *pair)

    def slots(h):
        slot_a = jnp.where(z == 0, down1[h], up1[h])
        slot_c = jnp.where((z == 0) | (z == 3), third[h], down1[h])
        return [halves[h], slot_a, second[h], slot_c]

    order = jnp.stack(
        [
            z,
            jnp.where(z == 0, 1, z - 1),
            jnp.where(z >= 2, z - 2, z + 2),
            jnp.where(z == 3, 0, jnp.where(z == 1, 2, 3)),
        ]
    ).astype(jnp.int32)

    def swap_gated(h):
        return [around_inner(gateds[h], r) for r in range(1, inner)]

    first_block = jnp.where(z == 0, 3, 0)
    second_block = jnp.where(z == 0, 2, jnp.where(z == 1, 3, jnp.where(z == 2, 0, 1)))

    def block_rows(block, h, dtype=F32):
        pick = jnp.asarray(block, jnp.int32).reshape(1)
        return weight_rows(pick, cots, [gateds[h]] + got[h], dtype)

    def last_rows(h):
        return block_rows(jnp.minimum(z + 1, 3), h), block_rows(jnp.maximum(z - 1, 0), h)

    def send_first(x):
        return along_line(x, [(0, 1), (3, 2)])

    def send_second(rows_here, came):
        x = (rows_here + came.astype(F32)).astype(BF16)
        return along_line(x, [(0, 1), (3, 2)]), along_line(x, [(1, 2), (2, 1)])

    def send_third(rows_here, outer_in, inner_in):
        up, down = rows_here
        outer_in, inner_in = outer_in.astype(F32), inner_in.astype(F32)
        up = (up + jnp.where(z == 1, outer_in, inner_in)).astype(BF16)
        down = (down + jnp.where(z == 1, inner_in, outer_in)).astype(BF16)
        return along_line(up, up_pairs), along_line(down, down_pairs)

    def last_sum(h):
        below, above = sums[h]
        return (finals[h] + below.astype(F32) + above.astype(F32)).astype(BF16)

    def shares(h, weights):
        return [gate_grad(order, cots[r], weights, BF16) for r in range(1, inner)]

    def send_shares(parts):
        return [around_inner(part, inner - r) for r, part in enumerate(parts, 1)]

    up1, down1, gateds, mixeds, got = ([None] * chunks for _ in range(5))
    second, third, sums, parts, others, owns = ([None] * chunks for _ in range(6))
    later_halves = list(each[1:])

    prior = send(
        product_of(keys[rows - FILT :], values[rows - FILT :]), [(i, i + 1) for i in range(seq - 1)]
    )
    paired = inner == 2 and ch == LINE
    other = grad_out
    cots = []
    if paired:
        kept = lax.dynamic_slice(grad_out, (0, y * depth), (rows, depth))
        other = lax.dynamic_slice(grad_out, (0, (1 - y) * depth), (rows, depth))
        cots = [lax.all_gather(kept, "ch", axis=0, tiled=False)]
    back, ahead = tables(filters)
    halves = [out_weight[:, h * cols : (h + 1) * cols] for h in each]
    prior, other, halves = fence(prior, other, halves)

    up1[0], down1[0] = along_line(halves[0], up_pairs), along_line(halves[0], down_pairs)
    swapped = around_inner(other, 1) if paired else other
    for h in later_halves:
        held = after(halves[h], back)
        up1[h], down1[h] = along_line(held, up_pairs), along_line(held, down_pairs)
    gateds[0], mixeds[0] = forward(queries, keys, values, prior, back, 0, chunks)
    up1[0], down1[0], swapped, gateds, cots, prior = fence(
        up1[0], down1[0], swapped, gateds, cots, prior
    )

    second[0] = second_step(0)
    if paired:
        cots.append(lax.all_gather(swapped, "ch", axis=0, tiled=False))
    else:
        full = lax.all_gather(swapped, "ch", axis=1, tiled=True)
        full = full.reshape(rows, LINE, inner, depth).transpose(2, 1, 0, 3)
        for shift in range(inner):
            part = lax.dynamic_index_in_dim(full, (y + shift) % inner, 0, keepdims=False)
            cots.append(part if shift == 0 else around_inner(part, shift))
    got[0] = swap_gated(0)
    for h in later_halves:
        gateds[h], mixeds[h] = forward(queries, keys, values, prior, back, h, chunks)
    up1, down1, gateds = fence(up1, down1, gateds)

    for h in later_halves:
        second[h] = second_step(h)
    second[0], got[0], gateds, cots = fence(second[0], got[0], gateds, cots)

    second[0] = merge(second[0])
    third[0] = third_step(second[0])
    for h in later_halves:
        got[h] = swap_gated(h)
    sums[0] = send_first(block_rows(first_block, 0, BF16))
    mids, lasts, finals = ([None] * chunks for _ in range(3))
    mids[0] = block_rows(second_block, 0)
    second, mids[0] = fence(second, mids[0])

    for h in later_halves:
        second[h] = merge(second[h])
        third[h] = third_step(second[h])
    sums[0] = send_second(mids[0], sums[0])
    lasts[0] = last_rows(0)
    third[0], lasts[0] = fence(third[0], lasts[0])

    weights = slots(0)
    parts[0] = shares(0, weights)
    parts[0], got[1:] = fence(parts[0], got[1:])
    others[0] = send_shares(parts[0])

    for h in later_halves:
        sums[h] = send_first(block_rows(first_block, h, BF16))
    sums[0] = send_third(lasts[0], *sums[0])
    owns[0] = gate_grad(order, cots[0], weights, F32)
    for h in later_halves:
        mids[h] = block_rows(second_block, h)
    third, owns[0], mids = fence(third, owns[0], mids)

    for h in later_halves:
        weights = slots(h)
        parts[h] = shares(h, weights)
        owns[h] = gate_grad(order, cots[0], weights, F32)
    parts[1:], sums = fence(parts[1:], sums)
    for h in later_halves:
        others[h] = send_shares(parts[h])
        sums[h] = send_second(mids[h], sums[h])
        lasts[h] = last_rows(h)
    finals = [block_rows(z, h) for h in each]
    lasts, finals, others[0], owns = fence(lasts, finals, others[0], owns)

    grad_queries = None
    grad_kv = None
    taps = [None] * chunks
    for h in each:
        grad_queries, gm, taps[h] = middle(
            owns[h], others[h], queries, keys, values, mixeds[h], prior, grad_queries, h, chunks
        )
        later = send(gm[:FILT], [(i + 1, i) for i in range(seq - 1)])
        if h == 0:
            for g in later_halves:
                sums[g] = send_third(lasts[g], *after(sums[g], gm))
        grad_kv = backward(gm, later, keys, values, ahead, grad_kv, h, chunks)
        if h == 0:
            done = [last_sum(0)]
            grad_kv, others, owns, done = fence(grad_kv, others, owns, done)
    for h in later_halves:
        sums[h], _ = fence(sums[h], gm)
        done.append(last_sum(h))
    grad_weight = jnp.concatenate(done, axis=1)
    taps = jnp.concatenate(taps, axis=0)[:, 1 : FILT + 1][:, ::-1]
    taps = taps.T.reshape(seq, FILT // seq, -1)
    taps = jnp.sum(lax.all_to_all(taps, "seq", 0, 0), axis=0)
    return grad_queries, *grad_kv, taps.T, grad_weight


def solution(mesh):
    sizes = dict(mesh.shape)
    return jax.shard_map(
        functools.partial(shards, sizes["seq"], sizes["ch"]),
        mesh=mesh,
        in_specs=(
            P("seq", "ch"),
            P("seq", "ch"),
            P("seq", "ch"),
            P("ch", None),
            P("seq", "ch"),
            P("seq", "ch"),
        ),
        out_specs=(P("seq", "ch"), P("seq", "ch"), P("seq", "ch"), P("ch", "seq"), P("seq", "ch")),
        check_vma=False,
    )
```

```python
import functools

import jax
import jax.numpy as jnp
from jax import lax
from jax.experimental import pallas as pl
from jax.experimental.pallas import tpu as pltpu
from jax.sharding import PartitionSpec as P

GROUP = 16
FILT = 128
LANES = 128
GPT = LANES // GROUP
LINE = 4
F32 = jnp.float32
BF16 = jnp.bfloat16
VMEM_LIMIT = 48 * 1024 * 1024


def params():
    return pltpu.CompilerParams(vmem_limit_bytes=VMEM_LIMIT)


def cost(flops, nbytes):
    return pl.CostEstimate(flops=int(flops) // 64, bytes_accessed=int(nbytes) // 64, transcendentals=0)


def fence(*arrays):
    return lax.optimization_barrier(arrays)


def after(x, *others):
    return lax.optimization_barrier((x, *others))[0]


def table_kernel(back_ref, ahead_ref, back_out, ahead_out):
    for seed, out in ((back_ref, back_out), (ahead_ref, ahead_out)):
        for g in range(GPT):
            rows = jnp.broadcast_to(seed[g : g + 1, :], (FILT, 2 * FILT))
            turned = pltpu.roll(rows, 0, 1, stride=1, stride_axis=0)
            out[g * FILT : (g + 1) * FILT, :] = turned.astype(BF16)


def tables(filters):
    groups = filters.shape[0]
    taps = filters.astype(F32)
    back = jnp.concatenate(
        [jnp.zeros((groups, 1), F32), taps[:, ::-1], jnp.zeros((groups, FILT - 1), F32)], axis=1
    )
    ahead = jnp.concatenate([taps, jnp.zeros((groups, FILT), F32)], axis=1)
    seed = pl.BlockSpec((GPT, 2 * FILT), lambda i: (i, 0))
    full = pl.BlockSpec((GPT * FILT, 2 * FILT), lambda i: (i, 0))
    shape = jax.ShapeDtypeStruct((groups * FILT, 2 * FILT), BF16)
    return pl.pallas_call(
        table_kernel,
        grid=(groups // GPT,),
        in_specs=[seed, seed],
        out_specs=[full, full],
        out_shape=[shape, shape],
        compiler_params=params(),
        cost_estimate=cost(groups * 2**18, groups * 2**17),
    )(back, ahead)


def group_of_lane(rows, cols):
    return (lax.broadcasted_iota(jnp.int32, (rows, cols), 1) % LANES) // GROUP


def windows(ext, b):
    lo = b * FILT
    return jnp.concatenate([ext[lo : lo + 2 * FILT], ext[lo + FILT : lo + 3 * FILT]], axis=1)


def toeplitz(table, ext, blocks):
    group = group_of_lane(FILT, 2 * LANES)
    rows = []
    for b in range(0, blocks, 2):
        out = jnp.dot(table, windows(ext, b), preferred_element_type=F32)
        picked = out[:FILT]
        for g in range(1, GPT):
            picked = jnp.where(group == g, out[g * FILT : (g + 1) * FILT], picked)
        rows += [picked[:, :LANES], picked[:, LANES:]]
    return jnp.concatenate(rows, axis=0)


def product_of(k, v):
    return (k.astype(F32) * v.astype(F32)).astype(BF16)


def forward_kernel(q, k, v, prior, table, gated, mixed_out):
    blocks = q.shape[0] // FILT
    ext = jnp.concatenate([prior[...], product_of(k[...], v[...])], axis=0)
    mixed = toeplitz(table[...], ext, blocks)
    mixed_out[...] = mixed.astype(BF16)
    gated[...] = (q[...].astype(F32) * mixed).astype(BF16)


def forward(q, k, v, prior, table, chunk, chunks):
    rows, width = q.shape
    tiles = width // LANES // chunks
    here = pl.BlockSpec((rows, LANES), lambda i: (0, chunk * tiles + i))
    out = pl.BlockSpec((rows, LANES), lambda i: (0, i))
    shape = jax.ShapeDtypeStruct((rows, width // chunks), BF16)
    return pl.pallas_call(
        forward_kernel,
        grid=(tiles,),
        in_specs=[
            here,
            here,
            here,
            pl.BlockSpec((FILT, LANES), lambda i: (0, i)),
            pl.BlockSpec((GPT * FILT, 2 * FILT), lambda i: (chunk * tiles + i, 0)),
        ],
        out_specs=[out, out],
        out_shape=[shape, shape],
        compiler_params=params(),
        cost_estimate=cost(tiles * rows * 2 * 2**18, tiles * rows * 5 * 256 + tiles * 2**19),
    )(q, k, v, prior, table)


def middle_kernel(own, others, q, k, v, mixed, prior, *rest):
    gq_out, gm_out, edge_out, taps_out = rest[-4:]
    blocks = q.shape[0] // FILT
    total = own[...].astype(F32)
    for other in others:
        total = total + other[...].astype(F32)
    gg = total.astype(BF16).astype(F32)
    gq_out[...] = (gg * mixed[...].astype(F32)).astype(BF16)
    gm = (gg * q[...].astype(F32)).astype(BF16)
    gm_out[...] = gm
    edge_out[...] = gm[:FILT]
    ext = jnp.concatenate([prior[...], product_of(k[...], v[...])], axis=0)
    wide = jnp.concatenate([gm[b * FILT : (b + 1) * FILT] for b in range(blocks)], axis=1)
    group = group_of_lane(FILT, blocks * LANES)
    stack = jnp.concatenate(
        [jnp.where(group == g, wide, jnp.zeros_like(wide)) for g in range(GPT)], axis=0
    )
    near = jnp.concatenate([ext[b * FILT : (b + 2) * FILT] for b in range(blocks)], axis=1)
    lag = lax.dot_general(stack, near, (((1,), (1,)), ((), ())), preferred_element_type=F32)
    lag = lag.reshape(GPT, FILT, 2 * FILT)
    half = FILT // 2
    while half >= 8:
        lag = lag[:, :half] + pltpu.roll(lag[:, half:], 2 * FILT - half, 2)
        half //= 2
    while half >= 1:
        lag = lag + pltpu.roll(pltpu.roll(lag, 2 * FILT - half, 2), 8 - half, 1)
        half //= 2
    taps_out[...] = lag[:, 0, :]


def middle(own, others, q, k, v, mixed, prior, filled, chunk, chunks):
    rows, width = q.shape
    tiles = width // LANES // chunks
    groups = width // GROUP // chunks
    here = pl.BlockSpec((rows, LANES), lambda i: (0, chunk * tiles + i))
    part = pl.BlockSpec((rows, LANES), lambda i: (0, i))
    edge = pl.BlockSpec((FILT, LANES), lambda i: (0, i))
    n_other = len(others)

    def kernel(own_ref, *refs):
        middle_kernel(own_ref, refs[:n_other], *refs[n_other:])

    args = [own, *others, q, k, v, mixed, prior]
    in_specs = [part] * (1 + n_other) + [here] * 3 + [part, edge]
    aliases = {}
    if filled is not None:
        aliases = {len(args): 0}
        args.append(filled)
        in_specs.append(pl.BlockSpec(memory_space=pl.ANY))
    return pl.pallas_call(
        kernel,
        grid=(tiles,),
        in_specs=in_specs,
        out_specs=[here, part, edge, pl.BlockSpec((GPT, 2 * FILT), lambda i: (i, 0))],
        out_shape=[
            jax.ShapeDtypeStruct((rows, width), BF16),
            jax.ShapeDtypeStruct((rows, width // chunks), BF16),
            jax.ShapeDtypeStruct((FILT, width // chunks), BF16),
            jax.ShapeDtypeStruct((groups, 2 * FILT), F32),
        ],
        input_output_aliases=aliases,
        compiler_params=params(),
        cost_estimate=cost(tiles * rows * 2 * 2**18, tiles * rows * 9 * 256),
    )(*args)


def backward_kernel(gm, later, k, v, table, *rest):
    gk_out, gv_out = rest[-2:]
    blocks = gm.shape[0] // FILT
    ext = jnp.concatenate([gm[...], later[...]], axis=0)
    gp = toeplitz(table[...], ext, blocks)
    gk_out[...] = (gp * v[...].astype(F32)).astype(BF16)
    gv_out[...] = (gp * k[...].astype(F32)).astype(BF16)


def backward(gm, later, k, v, table, filled, chunk, chunks):
    rows, width = k.shape
    tiles = width // LANES // chunks
    here = pl.BlockSpec((rows, LANES), lambda i: (0, chunk * tiles + i))
    part = pl.BlockSpec((rows, LANES), lambda i: (0, i))
    args = [gm, later, k, v, table]
    in_specs = [
        part,
        pl.BlockSpec((FILT, LANES), lambda i: (0, i)),
        here,
        here,
        pl.BlockSpec((GPT * FILT, 2 * FILT), lambda i: (chunk * tiles + i, 0)),
    ]
    aliases = {}
    if filled is not None:
        aliases = {len(args): 0, len(args) + 1: 1}
        args += filled
        in_specs += [pl.BlockSpec(memory_space=pl.ANY)] * 2
    shape = jax.ShapeDtypeStruct((rows, width), BF16)
    return pl.pallas_call(
        backward_kernel,
        grid=(tiles,),
        in_specs=in_specs,
        out_specs=[here, here],
        out_shape=[shape, shape],
        input_output_aliases=aliases,
        compiler_params=params(),
        cost_estimate=cost(tiles * rows * 2 * 2**18, tiles * rows * 5 * 256 + tiles * 2**19),
    )(*args)


def gate_kernel(pick, *refs):
    own, up, down, second, third, out = refs[LINE:]
    slots = (
        own[...],
        jnp.where(pick[LINE] == 1, down[...], up[...]),
        second[...],
        jnp.where(pick[LINE + 1] == 1, third[...], down[...]),
    )
    total = jnp.dot(refs[0][0], slots[0], preferred_element_type=F32)
    for j in range(1, LINE):
        total = total + jnp.dot(refs[j][0], slots[j], preferred_element_type=F32)
    out[...] = total.astype(out.dtype)


def gate_grad(pick, cot, weights):
    _, rows, depth = cot.shape
    width = weights[0].shape[1]
    tile = min(256, width)

    def cot_spec(j):
        return pl.BlockSpec((1, rows, depth), lambda i, pick: (pick[j], 0, 0))

    return pl.pallas_call(
        gate_kernel,
        grid_spec=pltpu.PrefetchScalarGridSpec(
            num_scalar_prefetch=1,
            grid=(width // tile,),
            in_specs=[cot_spec(j) for j in range(LINE)]
            + [pl.BlockSpec((depth, tile), lambda i, pick: (0, i))] * len(weights),
            out_specs=pl.BlockSpec((rows, tile), lambda i, pick: (0, i)),
        ),
        out_shape=jax.ShapeDtypeStruct((rows, width), BF16),
        compiler_params=params(),
        cost_estimate=cost(
            2 * rows * LINE * depth * width, 2 * LINE * depth * (rows + width) + 2 * rows * width
        ),
    )(pick, *([cot] * LINE), *weights)


def rows_kernel(n, pick, *refs):
    out = refs[-1]
    total = None
    for cot, gated in zip(refs[:n], refs[n : 2 * n]):
        term = lax.dot_general(
            cot[0], gated[...], (((0,), (0,)), ((), ())), preferred_element_type=F32
        )
        total = term if total is None else total + term
    out[0] = total.astype(out.dtype)


def weight_rows(pick, cots, gateds):
    _, rows, depth = cots[0].shape
    width = gateds[0].shape[1]
    blocks = pick.shape[0]
    tile = width if blocks > 1 else min(512, width)
    n = len(cots)
    cot_spec = pl.BlockSpec((1, rows, depth), lambda j, i, pick: (pick[j], 0, 0))
    gated_spec = pl.BlockSpec((rows, tile), lambda j, i, pick: (0, i))
    return pl.pallas_call(
        functools.partial(rows_kernel, n),
        grid_spec=pltpu.PrefetchScalarGridSpec(
            num_scalar_prefetch=1,
            grid=(blocks, width // tile),
            in_specs=[cot_spec] * n + [gated_spec] * n,
            out_specs=pl.BlockSpec((1, depth, tile), lambda j, i, pick: (j, 0, i)),
        ),
        out_shape=jax.ShapeDtypeStruct((blocks, depth, width), BF16),
        compiler_params=params(),
        cost_estimate=cost(2 * n * rows * depth * width, 2 * n * rows * (depth + width)),
    )(pick, *cots, *gateds)


def shards(seq, ch, queries, keys, values, filters, grad_out, out_weight):
    inner = seq // LINE
    rows, width = queries.shape
    depth = out_weight.shape[0]
    chunks = 2 if width % (2 * LANES) == 0 else 1
    cols = width // chunks
    place = lax.axis_index("seq")
    z, y = place // inner, place % inner

    def send(x, pairs):
        return lax.ppermute(x, "seq", pairs)

    def along_line(x, pairs):
        return send(x, [(a * inner + i, b * inner + i) for a, b in pairs for i in range(inner)])

    def around_inner(x, shift):
        return send(
            x, [(a * inner + i, a * inner + (i + shift) % inner) for a in range(LINE) for i in range(inner)]
        )

    each = range(chunks)
    up_pairs, down_pairs = [(0, 1), (1, 2), (2, 3)], [(1, 0), (2, 1), (3, 2)]

    def second_step(h):
        return along_line(up1[h], [(1, 2), (2, 3)]), along_line(down1[h], [(2, 1), (1, 0)])

    def third_step(x):
        return along_line(x, [(2, 3), (1, 0)])

    def merge(pair):
        return jnp.where(z >= 2, *pair)

    pick = jnp.stack(
        [
            z,
            jnp.where(z == 0, 1, z - 1),
            jnp.where(z >= 2, z - 2, z + 2),
            jnp.where(z == 3, 0, jnp.where(z == 1, 2, 3)),
            jnp.where(z == 0, 1, 0),
            jnp.where((z == 0) | (z == 3), 1, 0),
        ]
    ).astype(jnp.int32)

    def weights(h):
        return [halves[h], up1[h], down1[h], second[h], third[h]]

    def swap_gated(h):
        return [around_inner(gateds[h], r) for r in range(1, inner)]

    even = z % 2 == 0
    first_pick = jnp.where(even, 3, 0).astype(jnp.int32).reshape(1)
    rest_pick = jnp.stack(
        [
            jnp.where(z == 0, 2, jnp.where(z == 1, 3, jnp.where(z == 2, 0, 1))),
            jnp.where(even, 1, 2),
            z,
        ]
    ).astype(jnp.int32)

    def rows_of(order, h):
        return weight_rows(order, cots, [gateds[h]] + got[h])

    def send_first(x):
        return along_line(x, [(0, 1), (3, 2)])

    def send_second(h, came):
        x = (rest[h][0].astype(F32) + came.astype(F32)).astype(BF16)
        return along_line(x, [(0, 1), (3, 2)]), along_line(x, [(1, 2), (2, 1)])

    def send_third(h, outer_in, inner_in):
        mine, other = rest[h][1].astype(F32), first[h].astype(F32)
        outer_in, inner_in = outer_in.astype(F32), inner_in.astype(F32)
        up = jnp.where(z == 2, other, mine) + jnp.where(z == 1, outer_in, inner_in)
        down = jnp.where(z == 1, other, mine) + jnp.where(z == 1, inner_in, outer_in)
        return along_line(up.astype(BF16), up_pairs), along_line(down.astype(BF16), down_pairs)

    def last_sum(h):
        below, above = sums[h]
        return (rest[h][2].astype(F32) + below.astype(F32) + above.astype(F32)).astype(BF16)

    def shares(h):
        return [gate_grad(pick, cots[r], weights(h)) for r in range(1, inner)]

    def send_shares(parts):
        return [around_inner(part, inner - r) for r, part in enumerate(parts, 1)]

    up1, down1, gateds, mixeds, got = ([None] * chunks for _ in range(5))
    second, third, sums, parts, others, owns = ([None] * chunks for _ in range(6))
    first, rest = ([None] * chunks for _ in range(2))
    later_halves = list(each[1:])

    priors = []
    for h in each:
        tail = (slice(rows - FILT, rows), slice(h * cols, (h + 1) * cols))
        priors.append(product_of(keys[tail], values[tail]))
    cot_here = after(grad_out, *priors)
    next_pairs = [(i, i + 1) for i in range(seq - 1)]
    priors[0] = send(priors[0], next_pairs)
    paired = inner == 2 and ch == LINE
    other = cot_here
    cots = []
    if paired:
        kept = lax.dynamic_slice(cot_here, (0, y * depth), (rows, depth))
        other = lax.dynamic_slice(cot_here, (0, (1 - y) * depth), (rows, depth))
        cots = [lax.all_gather(kept, "ch", axis=0, tiled=False)]
    back, ahead = tables(filters)
    halves = [out_weight[:, h * cols : (h + 1) * cols] for h in each]
    priors, other, halves = fence(priors, other, halves)
    for h in later_halves:
        priors[h] = send(priors[h], next_pairs)

    up1[0], down1[0] = along_line(halves[0], up_pairs), along_line(halves[0], down_pairs)
    swapped = around_inner(other, 1) if paired else other
    gateds[0], mixeds[0] = forward(queries, keys, values, priors[0], back, 0, chunks)
    up1[0], down1[0], swapped, gateds, cots, priors = fence(
        up1[0], down1[0], swapped, gateds, cots, priors
    )

    for h in later_halves:
        up1[h], down1[h] = along_line(halves[h], up_pairs), along_line(halves[h], down_pairs)
    second[0] = second_step(0)
    if paired:
        cots.append(lax.all_gather(swapped, "ch", axis=0, tiled=False))
    else:
        full = lax.all_gather(swapped, "ch", axis=1, tiled=True)
        full = full.reshape(rows, LINE, inner, depth).transpose(2, 1, 0, 3)
        for shift in range(inner):
            part = lax.dynamic_index_in_dim(full, (y + shift) % inner, 0, keepdims=False)
            cots.append(part if shift == 0 else around_inner(part, shift))
    got[0] = swap_gated(0)
    for h in later_halves:
        gateds[h], mixeds[h] = forward(queries, keys, values, priors[h], back, h, chunks)
    up1, down1, gateds = fence(up1, down1, gateds)

    for h in later_halves:
        second[h] = second_step(h)
    second[0], got[0], gateds, cots = fence(second[0], got[0], gateds, cots)

    second[0] = merge(second[0])
    third[0] = third_step(second[0])
    for h in later_halves:
        got[h] = swap_gated(h)
    first[0] = rows_of(first_pick, 0)[0]
    sums[0] = send_first(first[0])
    rest[0] = rows_of(rest_pick, 0)
    second, rest[0] = fence(second, rest[0])

    for h in later_halves:
        second[h] = merge(second[h])
        third[h] = third_step(second[h])
    sums[0] = send_second(0, sums[0])
    third[0], second = fence(third[0], second)

    parts[0] = shares(0)
    parts[0], got[1:] = fence(parts[0], got[1:])
    others[0] = send_shares(parts[0])

    for h in later_halves:
        first[h] = rows_of(first_pick, h)[0]
        sums[h] = send_first(first[h])
    sums[0] = send_third(0, *sums[0])
    for h in later_halves:
        rest[h] = rows_of(rest_pick, h)
    third, rest[1:] = fence(third, rest[1:])

    for h in later_halves:
        parts[h] = shares(h)
    parts[1:], sums = fence(parts[1:], sums)
    for h in later_halves:
        others[h] = send_shares(parts[h])
        sums[h] = send_second(h, sums[h])
    owns = [gate_grad(pick, cots[0], weights(h)) for h in each]
    others[0], owns = fence(others[0], owns)

    grad_queries = None
    grad_kv = None
    taps = [None] * chunks
    for h in each:
        grad_queries, gm, edge, taps[h] = middle(
            owns[h], others[h], queries, keys, values, mixeds[h], priors[h], grad_queries, h, chunks
        )
        later = send(edge, [(i + 1, i) for i in range(seq - 1)])
        if h == 0:
            for g in later_halves:
                sums[g] = send_third(g, *after(sums[g], later))
        grad_kv = backward(gm, later, keys, values, ahead, grad_kv, h, chunks)
        if h == 0:
            done = [last_sum(0)]
            grad_kv, others, owns, done = fence(grad_kv, others, owns, done)
    for h in later_halves:
        sums[h], _ = fence(sums[h], edge)
        done.append(last_sum(h))
    grad_weight = jnp.concatenate(done, axis=1)
    taps = jnp.concatenate(taps, axis=0)[:, 1 : FILT + 1][:, ::-1]
    taps = taps.T.reshape(seq, FILT // seq, -1)
    taps = jnp.sum(lax.all_to_all(taps, "seq", 0, 0), axis=0)
    return grad_queries, *grad_kv, taps.T, grad_weight


def solution(mesh):
    sizes = dict(mesh.shape)
    return jax.shard_map(
        functools.partial(shards, sizes["seq"], sizes["ch"]),
        mesh=mesh,
        in_specs=(
            P("seq", "ch"),
            P("seq", "ch"),
            P("seq", "ch"),
            P("ch", None),
            P("seq", "ch"),
            P("seq", "ch"),
        ),
        out_specs=(P("seq", "ch"), P("seq", "ch"), P("seq", "ch"), P("ch", "seq"), P("seq", "ch")),
        check_vma=False,
    )
```

```python
import functools

import jax
import jax.numpy as jnp
from jax import lax
from jax.experimental import pallas as pl
from jax.experimental.pallas import tpu as pltpu
from jax.sharding import PartitionSpec as P

GROUP = 16
FILT = 128
LANES = 128
GPT = LANES // GROUP
LINE = 4
F32 = jnp.float32
BF16 = jnp.bfloat16
VMEM_LIMIT = 48 * 1024 * 1024


def params():
    return pltpu.CompilerParams(vmem_limit_bytes=VMEM_LIMIT)


def cost(flops, nbytes):
    return pl.CostEstimate(flops=int(flops) // 64, bytes_accessed=int(nbytes) // 64, transcendentals=0)


def fence(*arrays):
    return lax.optimization_barrier(arrays)


def after(x, *others):
    return lax.optimization_barrier((x, *others))[0]


def table_kernel(back_ref, ahead_ref, back_out, ahead_out):
    for seed, out in ((back_ref, back_out), (ahead_ref, ahead_out)):
        for g in range(GPT):
            rows = jnp.broadcast_to(seed[g : g + 1, :], (FILT, 2 * FILT))
            turned = pltpu.roll(rows, 0, 1, stride=1, stride_axis=0)
            out[g * FILT : (g + 1) * FILT, :] = turned.astype(BF16)


def tables(filters):
    groups = filters.shape[0]
    taps = filters.astype(F32)
    back = jnp.concatenate(
        [jnp.zeros((groups, 1), F32), taps[:, ::-1], jnp.zeros((groups, FILT - 1), F32)], axis=1
    )
    ahead = jnp.concatenate([taps, jnp.zeros((groups, FILT), F32)], axis=1)
    seed = pl.BlockSpec((GPT, 2 * FILT), lambda i: (i, 0))
    full = pl.BlockSpec((GPT * FILT, 2 * FILT), lambda i: (i, 0))
    shape = jax.ShapeDtypeStruct((groups * FILT, 2 * FILT), BF16)
    return pl.pallas_call(
        table_kernel,
        grid=(groups // GPT,),
        in_specs=[seed, seed],
        out_specs=[full, full],
        out_shape=[shape, shape],
        compiler_params=params(),
        cost_estimate=cost(groups * 2**18, groups * 2**17),
    )(back, ahead)


def group_of_lane(rows, cols):
    return (lax.broadcasted_iota(jnp.int32, (rows, cols), 1) % LANES) // GROUP


def windows(ext, b):
    lo = b * FILT
    return jnp.concatenate([ext[lo : lo + 2 * FILT], ext[lo + FILT : lo + 3 * FILT]], axis=1)


def toeplitz(table, ext, blocks):
    group = group_of_lane(FILT, 2 * LANES)
    rows = []
    for b in range(0, blocks, 2):
        out = jnp.dot(table, windows(ext, b), preferred_element_type=F32)
        picked = out[:FILT]
        for g in range(1, GPT):
            picked = jnp.where(group == g, out[g * FILT : (g + 1) * FILT], picked)
        rows += [picked[:, :LANES], picked[:, LANES:]]
    return jnp.concatenate(rows, axis=0)


def product_of(k, v):
    return (k.astype(F32) * v.astype(F32)).astype(BF16)


def forward_kernel(q, k, v, prior, table, gated, mixed_out):
    blocks = q.shape[0] // FILT
    ext = jnp.concatenate([prior[...], product_of(k[...], v[...])], axis=0)
    mixed = toeplitz(table[...], ext, blocks)
    mixed_out[...] = mixed.astype(BF16)
    gated[...] = (q[...].astype(F32) * mixed).astype(BF16)


def forward(q, k, v, prior, table, chunk, chunks):
    rows, width = q.shape
    tiles = width // LANES // chunks
    here = pl.BlockSpec((rows, LANES), lambda i: (0, chunk * tiles + i))
    out = pl.BlockSpec((rows, LANES), lambda i: (0, i))
    shape = jax.ShapeDtypeStruct((rows, width // chunks), BF16)
    return pl.pallas_call(
        forward_kernel,
        grid=(tiles,),
        in_specs=[
            here,
            here,
            here,
            pl.BlockSpec((FILT, LANES), lambda i: (0, i)),
            pl.BlockSpec((GPT * FILT, 2 * FILT), lambda i: (chunk * tiles + i, 0)),
        ],
        out_specs=[out, out],
        out_shape=[shape, shape],
        compiler_params=params(),
        cost_estimate=cost(tiles * rows * 2 * 2**18, tiles * rows * 5 * 256 + tiles * 2**19),
    )(q, k, v, prior, table)


def middle_kernel(own, others, q, k, v, mixed, prior, *rest):
    gq_out, gm_out, edge_out, taps_out = rest[-4:]
    blocks = q.shape[0] // FILT
    total = own[...].astype(F32)
    for other in others:
        total = total + other[...].astype(F32)
    gg = total.astype(BF16).astype(F32)
    gq_out[...] = (gg * mixed[...].astype(F32)).astype(BF16)
    gm = (gg * q[...].astype(F32)).astype(BF16)
    gm_out[...] = gm
    edge_out[...] = gm[:FILT]
    ext = jnp.concatenate([prior[...], product_of(k[...], v[...])], axis=0)
    wide = jnp.concatenate([gm[b * FILT : (b + 1) * FILT] for b in range(blocks)], axis=1)
    group = group_of_lane(FILT, blocks * LANES)
    stack = jnp.concatenate(
        [jnp.where(group == g, wide, jnp.zeros_like(wide)) for g in range(GPT)], axis=0
    )
    near = jnp.concatenate([ext[b * FILT : (b + 2) * FILT] for b in range(blocks)], axis=1)
    lag = lax.dot_general(stack, near, (((1,), (1,)), ((), ())), preferred_element_type=F32)
    lag = lag.reshape(GPT, FILT, 2 * FILT)
    half = FILT // 2
    while half >= 8:
        lag = lag[:, :half] + pltpu.roll(lag[:, half:], 2 * FILT - half, 2)
        half //= 2
    while half >= 1:
        lag = lag + pltpu.roll(pltpu.roll(lag, 2 * FILT - half, 2), 8 - half, 1)
        half //= 2
    taps_out[...] = lag[:, 0, :]


def middle(own, others, q, k, v, mixed, prior, filled, chunk, chunks):
    rows, width = q.shape
    tiles = width // LANES // chunks
    groups = width // GROUP // chunks
    here = pl.BlockSpec((rows, LANES), lambda i: (0, chunk * tiles + i))
    part = pl.BlockSpec((rows, LANES), lambda i: (0, i))
    edge = pl.BlockSpec((FILT, LANES), lambda i: (0, i))
    n_other = len(others)

    def kernel(own_ref, *refs):
        middle_kernel(own_ref, refs[:n_other], *refs[n_other:])

    args = [own, *others, q, k, v, mixed, prior]
    in_specs = [part] * (1 + n_other) + [here] * 3 + [part, edge]
    aliases = {}
    if filled is not None:
        aliases = {len(args): 0}
        args.append(filled)
        in_specs.append(pl.BlockSpec(memory_space=pl.ANY))
    return pl.pallas_call(
        kernel,
        grid=(tiles,),
        in_specs=in_specs,
        out_specs=[here, part, edge, pl.BlockSpec((GPT, 2 * FILT), lambda i: (i, 0))],
        out_shape=[
            jax.ShapeDtypeStruct((rows, width), BF16),
            jax.ShapeDtypeStruct((rows, width // chunks), BF16),
            jax.ShapeDtypeStruct((FILT, width // chunks), BF16),
            jax.ShapeDtypeStruct((groups, 2 * FILT), F32),
        ],
        input_output_aliases=aliases,
        compiler_params=params(),
        cost_estimate=cost(tiles * rows * 2 * 2**18, tiles * rows * 9 * 256),
    )(*args)


def backward_kernel(gm, later, k, v, table, *rest):
    gk_out, gv_out = rest[-2:]
    blocks = gm.shape[0] // FILT
    ext = jnp.concatenate([gm[...], later[...]], axis=0)
    gp = toeplitz(table[...], ext, blocks)
    gk_out[...] = (gp * v[...].astype(F32)).astype(BF16)
    gv_out[...] = (gp * k[...].astype(F32)).astype(BF16)


def backward(gm, later, k, v, table, filled, chunk, chunks):
    rows, width = k.shape
    tiles = width // LANES // chunks
    here = pl.BlockSpec((rows, LANES), lambda i: (0, chunk * tiles + i))
    part = pl.BlockSpec((rows, LANES), lambda i: (0, i))
    args = [gm, later, k, v, table]
    in_specs = [
        part,
        pl.BlockSpec((FILT, LANES), lambda i: (0, i)),
        here,
        here,
        pl.BlockSpec((GPT * FILT, 2 * FILT), lambda i: (chunk * tiles + i, 0)),
    ]
    aliases = {}
    if filled is not None:
        aliases = {len(args): 0, len(args) + 1: 1}
        args += filled
        in_specs += [pl.BlockSpec(memory_space=pl.ANY)] * 2
    shape = jax.ShapeDtypeStruct((rows, width), BF16)
    return pl.pallas_call(
        backward_kernel,
        grid=(tiles,),
        in_specs=in_specs,
        out_specs=[here, here],
        out_shape=[shape, shape],
        input_output_aliases=aliases,
        compiler_params=params(),
        cost_estimate=cost(tiles * rows * 2 * 2**18, tiles * rows * 5 * 256 + tiles * 2**19),
    )(*args)


def gate_kernel(pick, *refs):
    own, up, down, second, third, out = refs[LINE:]
    slots = (
        own[...],
        jnp.where(pick[LINE] == 1, down[...], up[...]),
        second[...],
        jnp.where(pick[LINE + 1] == 1, third[...], down[...]),
    )
    cot = jnp.concatenate([ref[0] for ref in refs[:LINE]], axis=1)
    total = jnp.dot(cot, jnp.concatenate(slots, axis=0), preferred_element_type=F32)
    out[...] = total.astype(out.dtype)


def gate_grad(pick, cot, weights, chunk, chunks):
    _, rows, depth = cot.shape
    width = weights[0].shape[1] // chunks
    tile = min(256, width)
    tiles = width // tile

    def cot_spec(j):
        return pl.BlockSpec((1, rows, depth), lambda i, pick: (pick[j], 0, 0))

    return pl.pallas_call(
        gate_kernel,
        grid_spec=pltpu.PrefetchScalarGridSpec(
            num_scalar_prefetch=1,
            grid=(tiles,),
            in_specs=[cot_spec(j) for j in range(LINE)]
            + [pl.BlockSpec((depth, tile), lambda i, pick: (0, chunk * tiles + i))] * len(weights),
            out_specs=pl.BlockSpec((rows, tile), lambda i, pick: (0, i)),
        ),
        out_shape=jax.ShapeDtypeStruct((rows, width), BF16),
        compiler_params=params(),
        cost_estimate=cost(
            2 * rows * LINE * depth * width, 2 * LINE * depth * (rows + width) + 2 * rows * width
        ),
    )(pick, *([cot] * LINE), *weights)


def rows_kernel(n, pick, *refs):
    out = refs[-1]
    cot = jnp.concatenate([ref[0] for ref in refs[:n]], axis=0)
    gated = jnp.concatenate([ref[...] for ref in refs[n : 2 * n]], axis=0)
    total = lax.dot_general(cot, gated, (((0,), (0,)), ((), ())), preferred_element_type=F32)
    out[0] = total.astype(out.dtype)


def weight_rows(pick, cots, gateds):
    _, rows, depth = cots[0].shape
    width = gateds[0].shape[1]
    blocks = pick.shape[0]
    tile = width if blocks > 1 else min(512, width)
    n = len(cots)
    cot_spec = pl.BlockSpec((1, rows, depth), lambda j, i, pick: (pick[j], 0, 0))
    gated_spec = pl.BlockSpec((rows, tile), lambda j, i, pick: (0, i))
    return pl.pallas_call(
        functools.partial(rows_kernel, n),
        grid_spec=pltpu.PrefetchScalarGridSpec(
            num_scalar_prefetch=1,
            grid=(blocks, width // tile),
            in_specs=[cot_spec] * n + [gated_spec] * n,
            out_specs=pl.BlockSpec((1, depth, tile), lambda j, i, pick: (j, 0, i)),
        ),
        out_shape=jax.ShapeDtypeStruct((blocks, depth, width), BF16),
        compiler_params=params(),
        cost_estimate=cost(2 * n * rows * depth * width, 2 * n * rows * (depth + width)),
    )(pick, *cots, *gateds)


def shards(seq, ch, queries, keys, values, filters, grad_out, out_weight):
    inner = seq // LINE
    rows, width = queries.shape
    depth = out_weight.shape[0]
    chunks = 2 if width % (2 * LANES) == 0 else 1
    cols = width // chunks
    place = lax.axis_index("seq")
    z, y = place // inner, place % inner

    def send(x, pairs):
        return lax.ppermute(x, "seq", pairs)

    def along_line(x, pairs):
        return send(x, [(a * inner + i, b * inner + i) for a, b in pairs for i in range(inner)])

    def around_inner(x, shift):
        return send(
            x, [(a * inner + i, a * inner + (i + shift) % inner) for a in range(LINE) for i in range(inner)]
        )

    each = range(chunks)
    up_pairs, down_pairs = [(0, 1), (1, 2), (2, 3)], [(1, 0), (2, 1), (3, 2)]

    def merge(up, down):
        return jnp.where(z >= 2, up, down)

    pick = jnp.stack(
        [
            z,
            jnp.where(z == 0, 1, z - 1),
            jnp.where(z >= 2, z - 2, z + 2),
            jnp.where(z == 3, 0, jnp.where(z == 1, 2, 3)),
            jnp.where(z == 0, 1, 0),
            jnp.where((z == 0) | (z == 3), 1, 0),
        ]
    ).astype(jnp.int32)

    def swap_gated(h):
        return [around_inner(gateds[h], r) for r in range(1, inner)]

    even = z % 2 == 0
    first_pick = jnp.where(even, 3, 0).astype(jnp.int32).reshape(1)
    rest_pick = jnp.stack(
        [
            jnp.where(z == 0, 2, jnp.where(z == 1, 3, jnp.where(z == 2, 0, 1))),
            jnp.where(even, 1, 2),
            z,
        ]
    ).astype(jnp.int32)

    def rows_of(order, h):
        return weight_rows(order, cots, [gateds[h]] + got[h])

    def send_first(x):
        return along_line(x, [(0, 1), (3, 2)])

    def send_second(h, came):
        x = (rest[h][0].astype(F32) + came.astype(F32)).astype(BF16)
        return along_line(x, [(0, 1), (3, 2)]), along_line(x, [(1, 2), (2, 1)])

    def send_third(h, outer_in, inner_in):
        mine, other = rest[h][1].astype(F32), first[h].astype(F32)
        outer_in, inner_in = outer_in.astype(F32), inner_in.astype(F32)
        up = jnp.where(z == 2, other, mine) + jnp.where(z == 1, outer_in, inner_in)
        down = jnp.where(z == 1, other, mine) + jnp.where(z == 1, inner_in, outer_in)
        return along_line(up.astype(BF16), up_pairs), along_line(down.astype(BF16), down_pairs)

    def last_sum(h):
        below, above = sums[h]
        return (rest[h][2].astype(F32) + below.astype(F32) + above.astype(F32)).astype(BF16)

    def shares(h):
        return [gate_grad(pick, cots[r], weights, h, chunks) for r in range(1, inner)]

    def send_shares(parts):
        return [around_inner(part, inner - r) for r, part in enumerate(parts, 1)]

    gateds, mixeds, got, sums, parts, others, first, rest = ([None] * chunks for _ in range(8))
    later_halves = list(each[1:])

    priors = []
    for h in each:
        tail = (slice(rows - FILT, rows), slice(h * cols, (h + 1) * cols))
        priors.append(product_of(keys[tail], values[tail]))
    cot_here = after(grad_out, *priors)
    next_pairs = [(i, i + 1) for i in range(seq - 1)]
    priors[0] = send(priors[0], next_pairs)
    paired = inner == 2 and ch == LINE
    other = cot_here
    cots = []
    if paired:
        kept = lax.dynamic_slice(cot_here, (0, y * depth), (rows, depth))
        other = lax.dynamic_slice(cot_here, (0, (1 - y) * depth), (rows, depth))
        cots = [lax.all_gather(kept, "ch", axis=0, tiled=False)]
    back, ahead = tables(filters)
    priors, other, weight = fence(priors, other, out_weight)
    for h in later_halves:
        priors[h] = send(priors[h], next_pairs)

    up1, down1 = along_line(weight, up_pairs), along_line(weight, down_pairs)
    swapped = around_inner(other, 1) if paired else other
    gateds[0], mixeds[0] = forward(queries, keys, values, priors[0], back, 0, chunks)
    swapped, gateds, cots, priors = fence(swapped, gateds, cots, priors)
    if paired:
        cots.append(lax.all_gather(swapped, "ch", axis=0, tiled=False))
    else:
        full = lax.all_gather(swapped, "ch", axis=1, tiled=True)
        full = full.reshape(rows, LINE, inner, depth).transpose(2, 1, 0, 3)
        for shift in range(inner):
            part = lax.dynamic_index_in_dim(full, (y + shift) % inner, 0, keepdims=False)
            cots.append(part if shift == 0 else around_inner(part, shift))
    got[0] = swap_gated(0)
    for h in later_halves:
        gateds[h], mixeds[h] = forward(queries, keys, values, priors[h], back, h, chunks)
    up1, down1, gateds = fence(up1, down1, gateds)

    up2 = along_line(up1, [(1, 2), (2, 3)])
    down2 = along_line(down1, [(2, 1), (1, 0)])
    for h in later_halves:
        got[h] = swap_gated(h)
    got[0], cots, gateds = fence(got[0], cots, gateds)
    first[0] = rows_of(first_pick, 0)[0]
    sums[0] = send_first(first[0])
    up2, down2, first[0] = fence(up2, down2, first[0])

    second = merge(up2, down2)
    third = along_line(second, [(2, 3), (1, 0)])
    rest[0] = rows_of(rest_pick, 0)
    sums[0], rest[0], got[1:] = fence(sums[0], rest[0], got[1:])
    sums[0] = send_second(0, sums[0])

    for h in later_halves:
        first[h] = rows_of(first_pick, h)[0]
        sums[h] = send_first(first[h])
    for h in later_halves:
        rest[h] = rows_of(rest_pick, h)
    third, rest = fence(third, rest)
    weights = [weight, up1, down1, second, third]

    parts[0] = shares(0)
    others[0] = send_shares(parts[0])
    sums[0], parts[0], third = fence(sums[0], parts[0], third)
    sums[0] = send_third(0, *sums[0])
    weights = [weight, up1, down1, second, third]
    for h in later_halves:
        parts[h] = shares(h)
        others[h] = send_shares(parts[h])
    sums[1:], parts = fence(sums[1:], parts)
    for h in later_halves:
        sums[h] = send_second(h, sums[h])
    third, _ = fence(third, parts)
    weights = [weight, up1, down1, second, third]
    owns = [gate_grad(pick, cots[0], weights, h, chunks) for h in each]
    others[0], owns, sums[0] = fence(others[0], owns, sums[0])

    grad_queries = None
    grad_kv = None
    taps, gms, laters = ([None] * chunks for _ in range(3))
    for h in each:
        grad_queries, gms[h], edge, taps[h] = middle(
            owns[h], others[h], queries, keys, values, mixeds[h], priors[h], grad_queries, h, chunks
        )
        laters[h] = send(edge, [(i + 1, i) for i in range(seq - 1)])
        if h == 0:
            for g in later_halves:
                sums[g] = send_third(g, *after(sums[g], edge))
            done = [last_sum(0)]
            others, owns, done = fence(others, owns, done)
    for h in later_halves:
        sums[h], gms[0], _ = fence(sums[h], gms[0], edge)
        done.append(last_sum(h))
    for h in each:
        grad_kv = backward(gms[h], laters[h], keys, values, ahead, grad_kv, h, chunks)
    grad_weight = jnp.concatenate(done, axis=1)
    taps = jnp.concatenate(taps, axis=0)[:, 1 : FILT + 1][:, ::-1]
    taps = taps.T.reshape(seq, FILT // seq, -1)
    taps = jnp.sum(lax.all_to_all(taps, "seq", 0, 0), axis=0)
    return grad_queries, *grad_kv, taps.T, grad_weight


def solution(mesh):
    sizes = dict(mesh.shape)
    return jax.shard_map(
        functools.partial(shards, sizes["seq"], sizes["ch"]),
        mesh=mesh,
        in_specs=(
            P("seq", "ch"),
            P("seq", "ch"),
            P("seq", "ch"),
            P("ch", None),
            P("seq", "ch"),
            P("seq", "ch"),
        ),
        out_specs=(P("seq", "ch"), P("seq", "ch"), P("seq", "ch"), P("ch", "seq"), P("seq", "ch")),
        check_vma=False,
    )
```

```python
import functools

import jax
import jax.numpy as jnp
from jax import lax
from jax.experimental import pallas as pl
from jax.experimental.pallas import tpu as pltpu
from jax.sharding import PartitionSpec as P

GROUP = 16
FILT = 128
LANES = 128
GPT = LANES // GROUP
LINE = 4
F32 = jnp.float32
BF16 = jnp.bfloat16
VMEM_LIMIT = 48 * 1024 * 1024


def params():
    return pltpu.CompilerParams(vmem_limit_bytes=VMEM_LIMIT)


def cost(flops, nbytes):
    return pl.CostEstimate(flops=int(flops) // 64, bytes_accessed=int(nbytes) // 64, transcendentals=0)


def fence(*arrays):
    return lax.optimization_barrier(arrays)


def after(x, *others):
    return lax.optimization_barrier((x, *others))[0]


def table_kernel(back_ref, ahead_ref, back_out, ahead_out):
    for seed, out in ((back_ref, back_out), (ahead_ref, ahead_out)):
        for g in range(GPT):
            rows = jnp.broadcast_to(seed[g : g + 1, :], (FILT, 2 * FILT))
            turned = pltpu.roll(rows, 0, 1, stride=1, stride_axis=0)
            out[g * FILT : (g + 1) * FILT, :] = turned.astype(BF16)


def tables(filters):
    groups = filters.shape[0]
    taps = filters.astype(F32)
    back = jnp.concatenate(
        [jnp.zeros((groups, 1), F32), taps[:, ::-1], jnp.zeros((groups, FILT - 1), F32)], axis=1
    )
    ahead = jnp.concatenate([taps, jnp.zeros((groups, FILT), F32)], axis=1)
    seed = pl.BlockSpec((GPT, 2 * FILT), lambda i: (i, 0))
    full = pl.BlockSpec((GPT * FILT, 2 * FILT), lambda i: (i, 0))
    shape = jax.ShapeDtypeStruct((groups * FILT, 2 * FILT), BF16)
    return pl.pallas_call(
        table_kernel,
        grid=(groups // GPT,),
        in_specs=[seed, seed],
        out_specs=[full, full],
        out_shape=[shape, shape],
        compiler_params=params(),
        cost_estimate=cost(groups * 2**18, groups * 2**17),
    )(back, ahead)


def group_of_lane(rows, cols):
    return (lax.broadcasted_iota(jnp.int32, (rows, cols), 1) % LANES) // GROUP


def windows(ext, b):
    lo = b * FILT
    return jnp.concatenate([ext[lo : lo + 2 * FILT], ext[lo + FILT : lo + 3 * FILT]], axis=1)


def toeplitz(table, ext, blocks):
    group = group_of_lane(FILT, 2 * LANES)
    rows = []
    for b in range(0, blocks, 2):
        out = jnp.dot(table, windows(ext, b), preferred_element_type=F32)
        picked = out[:FILT]
        for g in range(1, GPT):
            picked = jnp.where(group == g, out[g * FILT : (g + 1) * FILT], picked)
        rows += [picked[:, :LANES], picked[:, LANES:]]
    return jnp.concatenate(rows, axis=0)


def product_of(k, v):
    return (k.astype(F32) * v.astype(F32)).astype(BF16)


def forward_kernel(q, k, v, prior, table, gated, mixed_out):
    blocks = q.shape[0] // FILT
    ext = jnp.concatenate([prior[...], product_of(k[...], v[...])], axis=0)
    mixed = toeplitz(table[...], ext, blocks)
    mixed_out[...] = mixed.astype(BF16)
    gated[...] = (q[...].astype(F32) * mixed).astype(BF16)


def forward(q, k, v, prior, table, chunk, chunks):
    rows, width = q.shape
    tiles = width // LANES // chunks
    here = pl.BlockSpec((rows, LANES), lambda i: (0, chunk * tiles + i))
    out = pl.BlockSpec((rows, LANES), lambda i: (0, i))
    shape = jax.ShapeDtypeStruct((rows, width // chunks), BF16)
    return pl.pallas_call(
        forward_kernel,
        grid=(tiles,),
        in_specs=[
            here,
            here,
            here,
            pl.BlockSpec((FILT, LANES), lambda i: (0, i)),
            pl.BlockSpec((GPT * FILT, 2 * FILT), lambda i: (chunk * tiles + i, 0)),
        ],
        out_specs=[out, out],
        out_shape=[shape, shape],
        compiler_params=params(),
        cost_estimate=cost(tiles * rows * 2 * 2**18, tiles * rows * 5 * 256 + tiles * 2**19),
    )(q, k, v, prior, table)


def middle_kernel(own, others, q, k, v, mixed, prior, *rest):
    gq_out, gm_out, edge_out, taps_out = rest[-4:]
    blocks = q.shape[0] // FILT
    total = own[...].astype(F32)
    for other in others:
        total = total + other[...].astype(F32)
    gg = total.astype(BF16).astype(F32)
    gq_out[...] = (gg * mixed[...].astype(F32)).astype(BF16)
    gm = (gg * q[...].astype(F32)).astype(BF16)
    gm_out[...] = gm
    edge_out[...] = gm[:FILT]
    ext = jnp.concatenate([prior[...], product_of(k[...], v[...])], axis=0)
    wide = jnp.concatenate([gm[b * FILT : (b + 1) * FILT] for b in range(blocks)], axis=1)
    group = group_of_lane(FILT, blocks * LANES)
    stack = jnp.concatenate(
        [jnp.where(group == g, wide, jnp.zeros_like(wide)) for g in range(GPT)], axis=0
    )
    near = jnp.concatenate([ext[b * FILT : (b + 2) * FILT] for b in range(blocks)], axis=1)
    lag = lax.dot_general(stack, near, (((1,), (1,)), ((), ())), preferred_element_type=F32)
    lag = lag.reshape(GPT, FILT, 2 * FILT)
    half = FILT // 2
    while half >= 8:
        lag = lag[:, :half] + pltpu.roll(lag[:, half:], 2 * FILT - half, 2)
        half //= 2
    while half >= 1:
        lag = lag + pltpu.roll(pltpu.roll(lag, 2 * FILT - half, 2), 8 - half, 1)
        half //= 2
    taps_out[...] = lag[:, 0, :]


def middle(own, others, q, k, v, mixed, prior, filled, span):
    rows, width = q.shape
    _, local, cols, first = span
    tiles = cols // LANES
    here = pl.BlockSpec((rows, LANES), lambda i: (0, first // LANES + i))
    part = pl.BlockSpec((rows, LANES), lambda i: (0, i))
    edge = pl.BlockSpec((FILT, LANES), lambda i: (0, i))
    n_other = len(others)

    def kernel(own_ref, *refs):
        middle_kernel(own_ref, refs[:n_other], *refs[n_other:])

    args = [own, *others, q, k, v, mixed, prior]
    in_specs = [part] * (1 + n_other) + [here] * 3
    in_specs.append(pl.BlockSpec((rows, LANES), lambda i: (0, local // LANES + i)))
    in_specs.append(pl.BlockSpec((FILT, LANES), lambda i: (0, local // LANES + i)))
    aliases = {}
    if filled is not None:
        aliases = {len(args): 0}
        args.append(filled)
        in_specs.append(pl.BlockSpec(memory_space=pl.ANY))
    return pl.pallas_call(
        kernel,
        grid=(tiles,),
        in_specs=in_specs,
        out_specs=[here, part, edge, pl.BlockSpec((GPT, 2 * FILT), lambda i: (i, 0))],
        out_shape=[
            jax.ShapeDtypeStruct((rows, width), BF16),
            jax.ShapeDtypeStruct((rows, cols), BF16),
            jax.ShapeDtypeStruct((FILT, cols), BF16),
            jax.ShapeDtypeStruct((cols // GROUP, 2 * FILT), F32),
        ],
        input_output_aliases=aliases,
        compiler_params=params(),
        cost_estimate=cost(tiles * rows * 2 * 2**18, tiles * rows * 9 * 256),
    )(*args)


def backward_kernel(gm, later, k, v, table, *rest):
    gk_out, gv_out = rest[-2:]
    blocks = gm.shape[0] // FILT
    ext = jnp.concatenate([gm[...], later[...]], axis=0)
    gp = toeplitz(table[...], ext, blocks)
    gk_out[...] = (gp * v[...].astype(F32)).astype(BF16)
    gv_out[...] = (gp * k[...].astype(F32)).astype(BF16)


def backward(gm, later, k, v, table, filled, span):
    rows, width = k.shape
    _, _, cols, first = span
    tiles = cols // LANES
    here = pl.BlockSpec((rows, LANES), lambda i: (0, first // LANES + i))
    part = pl.BlockSpec((rows, LANES), lambda i: (0, i))
    args = [gm, later, k, v, table]
    in_specs = [
        part,
        pl.BlockSpec((FILT, LANES), lambda i: (0, i)),
        here,
        here,
        pl.BlockSpec((GPT * FILT, 2 * FILT), lambda i: (first // LANES + i, 0)),
    ]
    aliases = {}
    if filled is not None:
        aliases = {len(args): 0, len(args) + 1: 1}
        args += filled
        in_specs += [pl.BlockSpec(memory_space=pl.ANY)] * 2
    shape = jax.ShapeDtypeStruct((rows, width), BF16)
    return pl.pallas_call(
        backward_kernel,
        grid=(tiles,),
        in_specs=in_specs,
        out_specs=[here, here],
        out_shape=[shape, shape],
        input_output_aliases=aliases,
        compiler_params=params(),
        cost_estimate=cost(tiles * rows * 2 * 2**18, tiles * rows * 5 * 256 + tiles * 2**19),
    )(*args)


def gate_kernel(pick, *refs):
    own, up, down, second, third, out = refs[LINE:]
    slots = (
        own[...],
        jnp.where(pick[LINE] == 1, down[...], up[...]),
        second[...],
        jnp.where(pick[LINE + 1] == 1, third[...], down[...]),
    )
    cot = jnp.concatenate([ref[0] for ref in refs[:LINE]], axis=1)
    total = jnp.dot(cot, jnp.concatenate(slots, axis=0), preferred_element_type=F32)
    out[...] = total.astype(out.dtype)


def gate_grad(pick, cot, weights, span):
    _, rows, depth = cot.shape
    _, _, width, first = span
    tile = min(256, width)
    tiles = width // tile

    def cot_spec(j):
        return pl.BlockSpec((1, rows, depth), lambda i, pick: (pick[j], 0, 0))

    return pl.pallas_call(
        gate_kernel,
        grid_spec=pltpu.PrefetchScalarGridSpec(
            num_scalar_prefetch=1,
            grid=(tiles,),
            in_specs=[cot_spec(j) for j in range(LINE)]
            + [pl.BlockSpec((depth, tile), lambda i, pick: (0, first // tile + i))] * len(weights),
            out_specs=pl.BlockSpec((rows, tile), lambda i, pick: (0, i)),
        ),
        out_shape=jax.ShapeDtypeStruct((rows, width), BF16),
        compiler_params=params(),
        cost_estimate=cost(
            2 * rows * LINE * depth * width, 2 * LINE * depth * (rows + width) + 2 * rows * width
        ),
    )(pick, *([cot] * LINE), *weights)


def rows_kernel(n, pick, *refs):
    out = refs[-1]
    cot, gated = refs[0][0], refs[n][...]
    if n > 1:
        cot = jnp.concatenate([ref[0] for ref in refs[:n]], axis=0)
        gated = jnp.concatenate([ref[...] for ref in refs[n : 2 * n]], axis=0)
    total = lax.dot_general(cot, gated, (((0,), (0,)), ((), ())), preferred_element_type=F32)
    if len(refs) > 2 * n + 1:
        total = total + refs[2 * n][0]
    out[0] = total.astype(out.dtype)


def weight_rows(pick, cots, gateds, dtype, base=None, skip=0):
    _, rows, depth = cots[0].shape
    width = gateds[0].shape[1]
    blocks = pick.shape[0]
    tile = width if blocks > 1 else min(512, width)
    n = len(cots)
    in_specs = [pl.BlockSpec((1, rows, depth), lambda j, i, pick: (pick[j], 0, 0))] * n
    in_specs += [pl.BlockSpec((rows, tile), lambda j, i, pick: (0, i))] * n
    args = [*cots, *gateds]
    if base is not None:
        in_specs.append(pl.BlockSpec((1, depth, tile), lambda j, i, pick: (j + skip, 0, i)))
        args.append(base)
    return pl.pallas_call(
        functools.partial(rows_kernel, n),
        grid_spec=pltpu.PrefetchScalarGridSpec(
            num_scalar_prefetch=1,
            grid=(blocks, width // tile),
            in_specs=in_specs,
            out_specs=pl.BlockSpec((1, depth, tile), lambda j, i, pick: (j, 0, i)),
        ),
        out_shape=jax.ShapeDtypeStruct((blocks, depth, width), dtype),
        compiler_params=params(),
        cost_estimate=cost(2 * n * rows * depth * width, 2 * n * rows * (depth + width)),
    )(pick, *args)


def shards(seq, ch, queries, keys, values, filters, grad_out, out_weight):
    inner = seq // LINE
    rows, width = queries.shape
    depth = out_weight.shape[0]
    chunks = 2 if width % (2 * LANES) == 0 else 1
    cols = width // chunks
    place = lax.axis_index("seq")
    z, y = place // inner, place % inner

    def send(x, pairs):
        return lax.ppermute(x, "seq", pairs)

    def along_line(x, pairs):
        return send(x, [(a * inner + i, b * inner + i) for a, b in pairs for i in range(inner)])

    def around_inner(x, shift):
        return send(
            x, [(a * inner + i, a * inner + (i + shift) % inner) for a in range(LINE) for i in range(inner)]
        )

    each = range(chunks)
    up_pairs, down_pairs = [(0, 1), (1, 2), (2, 3)], [(1, 0), (2, 1), (3, 2)]

    def merge(up, down):
        return jnp.where(z >= 2, up, down)

    pick = jnp.stack(
        [
            z,
            jnp.where(z == 0, 1, z - 1),
            jnp.where(z >= 2, z - 2, z + 2),
            jnp.where(z == 3, 0, jnp.where(z == 1, 2, 3)),
            jnp.where(z == 0, 1, 0),
            jnp.where((z == 0) | (z == 3), 1, 0),
        ]
    ).astype(jnp.int32)

    def swap_gated(h):
        return [around_inner(gateds[h], r) for r in range(1, inner)]

    even = z % 2 == 0
    first_pick = jnp.where(even, 3, 0).astype(jnp.int32).reshape(1)
    rest_pick = jnp.stack(
        [
            jnp.where(z == 0, 2, jnp.where(z == 1, 3, jnp.where(z == 2, 0, 1))),
            jnp.where(even, 1, 2),
            z,
        ]
    ).astype(jnp.int32)

    def rows_own(h):
        return weight_rows(jnp.concatenate([first_pick, rest_pick]), cots[:1], [gateds[h]], F32)

    def rows_first(h):
        return weight_rows(first_pick, cots[1:], got[h], BF16, base[h])[0]

    def rows_rest(h):
        return weight_rows(rest_pick, cots[1:], got[h], BF16, base[h], 1)

    def send_first(x):
        return along_line(x, [(0, 1), (3, 2)])

    def send_second(h, came):
        x = (rest[h][0].astype(F32) + came.astype(F32)).astype(BF16)
        return along_line(x, [(0, 1), (3, 2)]), along_line(x, [(1, 2), (2, 1)])

    def send_third(h, outer_in, inner_in):
        mine, other = rest[h][1].astype(F32), first[h].astype(F32)
        outer_in, inner_in = outer_in.astype(F32), inner_in.astype(F32)
        up = jnp.where(z == 2, other, mine) + jnp.where(z == 1, outer_in, inner_in)
        down = jnp.where(z == 1, other, mine) + jnp.where(z == 1, inner_in, outer_in)
        return along_line(up.astype(BF16), up_pairs), along_line(down.astype(BF16), down_pairs)

    def last_sum(h):
        below, above = sums[h]
        return (rest[h][2].astype(F32) + below.astype(F32) + above.astype(F32)).astype(BF16)

    def shares(span):
        return [gate_grad(pick, cots[r], weights, span) for r in range(1, inner)]

    def send_shares(parts):
        return [around_inner(part, inner - r) for r, part in enumerate(parts, 1)]

    gateds, mixeds, got, sums, first, rest, base = ([None] * chunks for _ in range(7))
    later_halves = list(each[1:])
    spans = [(0, 0, cols, 0)]
    for h in later_halves:
        spans += [(h, lo, cols // 2, h * cols + lo) for lo in (0, cols // 2)]
    parts, others, owns, gms, laters, taps = ([None] * len(spans) for _ in range(6))

    priors = []
    for h in each:
        tail = (slice(rows - FILT, rows), slice(h * cols, (h + 1) * cols))
        priors.append(product_of(keys[tail], values[tail]))
    cot_here = after(grad_out, *priors)
    next_pairs = [(i, i + 1) for i in range(seq - 1)]
    priors[0] = send(priors[0], next_pairs)
    paired = inner == 2 and ch == LINE
    other = cot_here
    cots = []
    if paired:
        kept = lax.dynamic_slice(cot_here, (0, y * depth), (rows, depth))
        other = lax.dynamic_slice(cot_here, (0, (1 - y) * depth), (rows, depth))
        cots = [lax.all_gather(kept, "ch", axis=0, tiled=False)]
    back, ahead = tables(filters)
    priors, other, weight = fence(priors, other, out_weight)
    for h in later_halves:
        priors[h] = send(priors[h], next_pairs)

    up1, down1 = along_line(weight, up_pairs), along_line(weight, down_pairs)
    swapped = around_inner(other, 1) if paired else other
    for h in each:
        gateds[h], mixeds[h] = forward(queries, keys, values, priors[h], back, h, chunks)
    if paired:
        base[0] = rows_own(0)
    up1, down1, swapped, gateds, cots, priors, base = fence(
        up1, down1, swapped, gateds, cots, priors, base
    )

    up2 = along_line(up1, [(1, 2), (2, 3)])
    down2 = along_line(down1, [(2, 1), (1, 0)])
    if paired:
        cots.append(lax.all_gather(swapped, "ch", axis=0, tiled=False))
    else:
        full = lax.all_gather(swapped, "ch", axis=1, tiled=True)
        full = full.reshape(rows, LINE, inner, depth).transpose(2, 1, 0, 3)
        for shift in range(inner):
            part = lax.dynamic_index_in_dim(full, (y + shift) % inner, 0, keepdims=False)
            cots.append(part if shift == 0 else around_inner(part, shift))
        base[0] = rows_own(0)
    for h in each:
        got[h] = swap_gated(h)

    got[0], cots, gateds, base = fence(got[0], cots, gateds, base)
    first[0] = rows_first(0)
    sums[0] = send_first(first[0])
    up2, down2, first[0] = fence(up2, down2, first[0])

    second = merge(up2, down2)
    third = along_line(second, [(2, 3), (1, 0)])
    rest[0] = rows_rest(0)
    sums[0], rest[0], gateds = fence(sums[0], rest[0], gateds)
    sums[0] = send_second(0, sums[0])
    for h in later_halves:
        base[h] = rows_own(h)
    got[1:], base = fence(got[1:], base)

    for h in later_halves:
        first[h] = rows_first(h)
        sums[h] = send_first(first[h])
    third, first = fence(third, first)
    weights = [weight, up1, down1, second, third]
    parts[0] = shares(spans[0])
    others[0] = send_shares(parts[0])

    sums[0], parts[0], third, base = fence(sums[0], parts[0], third, base)
    sums[0] = send_third(0, *sums[0])
    for h in later_halves:
        rest[h] = rows_rest(h)
    weights = [weight, up1, down1, second, third]
    for n, span in enumerate(spans[1:], 1):
        parts[n] = shares(span)
    for n in range(1, len(spans), 2):
        others[n] = send_shares(parts[n])
    sums[1:], parts, rest = fence(sums[1:], parts, rest)
    for h in later_halves:
        sums[h] = send_second(h, sums[h])
    third, _ = fence(third, parts)
    weights = [weight, up1, down1, second, third]
    owns = [gate_grad(pick, cots[0], weights, span) for span in spans]
    others[0], owns, sums[0] = fence(others[0], owns, sums[0])

    grad_queries = None
    grad_kv = None
    back_pairs = [(i + 1, i) for i in range(seq - 1)]
    done = []
    for n, span in enumerate(spans):
        half = span[0]
        grad_queries, gms[n], edge, taps[n] = middle(
            owns[n], others[n], queries, keys, values, mixeds[half], priors[half], grad_queries, span
        )
        laters[n] = send(edge, back_pairs)
        if n == 0:
            for m in range(2, len(spans), 2):
                others[m] = send_shares(after(parts[m], laters[0]))
            for g in later_halves:
                sums[g] = send_third(g, *after(sums[g], laters[0]))
            done.append(last_sum(0))
            others[1:2], owns, done = fence(others[1:2], owns, done)
        if n == 1:
            gms[0], _ = fence(gms[0], edge)
            grad_kv = backward(gms[0], laters[0], keys, values, ahead, grad_kv, spans[0])
            others[2:], grad_kv = fence(others[2:], grad_kv)
    for h in later_halves:
        sums[h], gms[1], _ = fence(sums[h], gms[1], edge)
        done.append(last_sum(h))
    for n in range(1 if len(spans) > 1 else 0, len(spans)):
        grad_kv = backward(gms[n], laters[n], keys, values, ahead, grad_kv, spans[n])
    grad_weight = jnp.concatenate(done, axis=1)
    taps = jnp.concatenate(taps, axis=0)[:, 1 : FILT + 1][:, ::-1]
    taps = taps.T.reshape(seq, FILT // seq, -1)
    taps = jnp.sum(lax.all_to_all(taps, "seq", 0, 0), axis=0)
    return grad_queries, *grad_kv, taps.T, grad_weight


def solution(mesh):
    sizes = dict(mesh.shape)
    return jax.shard_map(
        functools.partial(shards, sizes["seq"], sizes["ch"]),
        mesh=mesh,
        in_specs=(
            P("seq", "ch"),
            P("seq", "ch"),
            P("seq", "ch"),
            P("ch", None),
            P("seq", "ch"),
            P("seq", "ch"),
        ),
        out_specs=(P("seq", "ch"), P("seq", "ch"), P("seq", "ch"), P("ch", "seq"), P("seq", "ch")),
        check_vma=False,
    )
```

```python
import functools

import jax
import jax.numpy as jnp
from jax import lax
from jax.experimental import pallas as pl
from jax.experimental.pallas import tpu as pltpu
from jax.sharding import PartitionSpec as P

GROUP = 16
FILT = 128
LANES = 128
GPT = LANES // GROUP
LINE = 4
F32 = jnp.float32
BF16 = jnp.bfloat16
VMEM_LIMIT = 48 * 1024 * 1024


def params():
    return pltpu.CompilerParams(vmem_limit_bytes=VMEM_LIMIT)


def cost(flops, nbytes):
    return pl.CostEstimate(flops=int(flops) // 64, bytes_accessed=int(nbytes) // 64, transcendentals=0)


def fence(*arrays):
    return lax.optimization_barrier(arrays)


def after(x, *others):
    return lax.optimization_barrier((x, *others))[0]


def table_kernel(back_ref, ahead_ref, back_out, ahead_out):
    for seed, out in ((back_ref, back_out), (ahead_ref, ahead_out)):
        for g in range(GPT):
            rows = jnp.broadcast_to(seed[g : g + 1, :], (FILT, 2 * FILT))
            turned = pltpu.roll(rows, 0, 1, stride=1, stride_axis=0)
            out[g * FILT : (g + 1) * FILT, :] = turned.astype(BF16)


def tables(filters):
    groups = filters.shape[0]
    taps = filters.astype(F32)
    back = jnp.concatenate(
        [jnp.zeros((groups, 1), F32), taps[:, ::-1], jnp.zeros((groups, FILT - 1), F32)], axis=1
    )
    ahead = jnp.concatenate([taps, jnp.zeros((groups, FILT), F32)], axis=1)
    seed = pl.BlockSpec((GPT, 2 * FILT), lambda i: (i, 0))
    full = pl.BlockSpec((GPT * FILT, 2 * FILT), lambda i: (i, 0))
    shape = jax.ShapeDtypeStruct((groups * FILT, 2 * FILT), BF16)
    return pl.pallas_call(
        table_kernel,
        grid=(groups // GPT,),
        in_specs=[seed, seed],
        out_specs=[full, full],
        out_shape=[shape, shape],
        compiler_params=params(),
        cost_estimate=cost(groups * 2**18, groups * 2**17),
    )(back, ahead)


def group_of_lane(rows, cols):
    return (lax.broadcasted_iota(jnp.int32, (rows, cols), 1) % LANES) // GROUP


def windows(ext, b):
    lo = b * FILT
    return jnp.concatenate([ext[lo : lo + 2 * FILT], ext[lo + FILT : lo + 3 * FILT]], axis=1)


def toeplitz(table, ext, blocks):
    group = group_of_lane(FILT, 2 * LANES)
    rows = []
    for b in range(0, blocks, 2):
        out = jnp.dot(table, windows(ext, b), preferred_element_type=F32)
        picked = out[:FILT]
        for g in range(1, GPT):
            picked = jnp.where(group == g, out[g * FILT : (g + 1) * FILT], picked)
        rows += [picked[:, :LANES], picked[:, LANES:]]
    return jnp.concatenate(rows, axis=0)


def product_of(k, v):
    return (k.astype(F32) * v.astype(F32)).astype(BF16)


def forward_kernel(q, k, v, prior, table, gated, mixed_out):
    blocks = q.shape[0] // FILT
    ext = jnp.concatenate([prior[...], product_of(k[...], v[...])], axis=0)
    mixed = toeplitz(table[...], ext, blocks)
    mixed_out[...] = mixed.astype(BF16)
    gated[...] = (q[...].astype(F32) * mixed).astype(BF16)


def forward(q, k, v, prior, table, chunk, chunks):
    rows, width = q.shape
    tiles = width // LANES // chunks
    here = pl.BlockSpec((rows, LANES), lambda i: (0, chunk * tiles + i))
    out = pl.BlockSpec((rows, LANES), lambda i: (0, i))
    shape = jax.ShapeDtypeStruct((rows, width // chunks), BF16)
    return pl.pallas_call(
        forward_kernel,
        grid=(tiles,),
        in_specs=[
            here,
            here,
            here,
            pl.BlockSpec((FILT, LANES), lambda i: (0, chunk * tiles + i)),
            pl.BlockSpec((GPT * FILT, 2 * FILT), lambda i: (chunk * tiles + i, 0)),
        ],
        out_specs=[out, out],
        out_shape=[shape, shape],
        compiler_params=params(),
        cost_estimate=cost(tiles * rows * 2 * 2**18, tiles * rows * 5 * 256 + tiles * 2**19),
    )(q, k, v, prior, table)


def middle_kernel(own, others, q, k, v, mixed, prior, *rest):
    gq_out, gm_out, edge_out, taps_out = rest[-4:]
    blocks = q.shape[0] // FILT
    total = own[...].astype(F32)
    for other in others:
        total = total + other[...].astype(F32)
    gg = total.astype(BF16).astype(F32)
    gq_out[...] = (gg * mixed[...].astype(F32)).astype(BF16)
    gm = (gg * q[...].astype(F32)).astype(BF16)
    gm_out[...] = gm
    edge_out[...] = gm[:FILT]
    ext = jnp.concatenate([prior[...], product_of(k[...], v[...])], axis=0)
    wide = jnp.concatenate([gm[b * FILT : (b + 1) * FILT] for b in range(blocks)], axis=1)
    group = group_of_lane(FILT, blocks * LANES)
    stack = jnp.concatenate(
        [jnp.where(group == g, wide, jnp.zeros_like(wide)) for g in range(GPT)], axis=0
    )
    near = jnp.concatenate([ext[b * FILT : (b + 2) * FILT] for b in range(blocks)], axis=1)
    lag = lax.dot_general(stack, near, (((1,), (1,)), ((), ())), preferred_element_type=F32)
    lag = lag.reshape(GPT, FILT, 2 * FILT)
    half = FILT // 2
    while half >= 8:
        lag = lag[:, :half] + pltpu.roll(lag[:, half:], 2 * FILT - half, 2)
        half //= 2
    while half >= 1:
        lag = lag + pltpu.roll(pltpu.roll(lag, 2 * FILT - half, 2), 8 - half, 1)
        half //= 2
    taps_out[...] = lag[:, 0, :]


def middle(own, others, q, k, v, mixed, prior, filled, span):
    rows, width = q.shape
    _, local, cols, first = span
    tiles = cols // LANES
    here = pl.BlockSpec((rows, LANES), lambda i: (0, first // LANES + i))
    part = pl.BlockSpec((rows, LANES), lambda i: (0, i))
    edge = pl.BlockSpec((FILT, LANES), lambda i: (0, i))
    n_other = len(others)

    def kernel(own_ref, *refs):
        middle_kernel(own_ref, refs[:n_other], *refs[n_other:])

    args = [own, *others, q, k, v, mixed, prior]
    in_specs = [part] * (1 + n_other) + [here] * 3
    in_specs.append(pl.BlockSpec((rows, LANES), lambda i: (0, local // LANES + i)))
    in_specs.append(pl.BlockSpec((FILT, LANES), lambda i: (0, first // LANES + i)))
    aliases = {}
    if filled is not None:
        aliases = {len(args): 0}
        args.append(filled)
        in_specs.append(pl.BlockSpec(memory_space=pl.ANY))
    return pl.pallas_call(
        kernel,
        grid=(tiles,),
        in_specs=in_specs,
        out_specs=[here, part, edge, pl.BlockSpec((GPT, 2 * FILT), lambda i: (i, 0))],
        out_shape=[
            jax.ShapeDtypeStruct((rows, width), BF16),
            jax.ShapeDtypeStruct((rows, cols), BF16),
            jax.ShapeDtypeStruct((FILT, cols), BF16),
            jax.ShapeDtypeStruct((cols // GROUP, 2 * FILT), F32),
        ],
        input_output_aliases=aliases,
        compiler_params=params(),
        cost_estimate=cost(tiles * rows * 2 * 2**18, tiles * rows * 9 * 256),
    )(*args)


def backward_kernel(gm, later, k, v, table, *rest):
    gk_out, gv_out = rest[-2:]
    blocks = gm.shape[0] // FILT
    ext = jnp.concatenate([gm[...], later[...]], axis=0)
    gp = toeplitz(table[...], ext, blocks)
    gk_out[...] = (gp * v[...].astype(F32)).astype(BF16)
    gv_out[...] = (gp * k[...].astype(F32)).astype(BF16)


def backward(gm, later, k, v, table, filled, span):
    rows, width = k.shape
    _, _, cols, first = span
    tiles = cols // LANES
    here = pl.BlockSpec((rows, LANES), lambda i: (0, first // LANES + i))
    part = pl.BlockSpec((rows, LANES), lambda i: (0, i))
    args = [gm, later, k, v, table]
    in_specs = [
        part,
        pl.BlockSpec((FILT, LANES), lambda i: (0, i)),
        here,
        here,
        pl.BlockSpec((GPT * FILT, 2 * FILT), lambda i: (first // LANES + i, 0)),
    ]
    aliases = {}
    if filled is not None:
        aliases = {len(args): 0, len(args) + 1: 1}
        args += filled
        in_specs += [pl.BlockSpec(memory_space=pl.ANY)] * 2
    shape = jax.ShapeDtypeStruct((rows, width), BF16)
    return pl.pallas_call(
        backward_kernel,
        grid=(tiles,),
        in_specs=in_specs,
        out_specs=[here, here],
        out_shape=[shape, shape],
        input_output_aliases=aliases,
        compiler_params=params(),
        cost_estimate=cost(tiles * rows * 2 * 2**18, tiles * rows * 5 * 256 + tiles * 2**19),
    )(*args)


def gate_kernel(pick, *refs):
    own, up, down, second, third, out = refs[LINE:]
    slots = (
        own[...],
        jnp.where(pick[LINE] == 1, down[...], up[...]),
        second[...],
        jnp.where(pick[LINE + 1] == 1, third[...], down[...]),
    )
    cot = jnp.concatenate([ref[0] for ref in refs[:LINE]], axis=1)
    total = jnp.dot(cot, jnp.concatenate(slots, axis=0), preferred_element_type=F32)
    out[...] = total.astype(out.dtype)


def gate_grad(pick, cot, weights, span):
    _, rows, depth = cot.shape
    _, _, width, first = span
    tile = min(256, width)
    tiles = width // tile

    def cot_spec(j):
        return pl.BlockSpec((1, rows, depth), lambda i, pick: (pick[j], 0, 0))

    return pl.pallas_call(
        gate_kernel,
        grid_spec=pltpu.PrefetchScalarGridSpec(
            num_scalar_prefetch=1,
            grid=(tiles,),
            in_specs=[cot_spec(j) for j in range(LINE)]
            + [pl.BlockSpec((depth, tile), lambda i, pick: (0, first // tile + i))] * len(weights),
            out_specs=pl.BlockSpec((rows, tile), lambda i, pick: (0, i)),
        ),
        out_shape=jax.ShapeDtypeStruct((rows, width), BF16),
        compiler_params=params(),
        cost_estimate=cost(
            2 * rows * LINE * depth * width, 2 * LINE * depth * (rows + width) + 2 * rows * width
        ),
    )(pick, *([cot] * LINE), *weights)


def rows_kernel(n, halves, pick, *refs):
    out = refs[-1]
    cot = refs[0][0]
    if n > 1:
        cot = jnp.concatenate([ref[0] for ref in refs[:n]], axis=0)

    def write(gated_refs):
        gated = gated_refs[0][...]
        if n > 1:
            gated = jnp.concatenate([ref[...] for ref in gated_refs], axis=0)
        total = lax.dot_general(cot, gated, (((0,), (0,)), ((), ())), preferred_element_type=F32)
        if len(refs) > n + n * halves + 1:
            total = total + refs[-2][0]
        out[0] = total.astype(out.dtype)

    for h in range(halves):
        pl.when(pl.program_id(1) == h)(
            functools.partial(write, refs[n + n * h : n + n * (h + 1)])
        )


def weight_rows(pick, cots, gateds, dtype, base=None, skip=0, lead=0):
    _, rows, depth = cots[0].shape
    width = gateds[0][0].shape[1]
    blocks = pick.shape[0]
    n, halves = len(cots), len(gateds)
    in_specs = [pl.BlockSpec((1, rows, depth), lambda j, i, pick: (pick[j], 0, 0))] * n
    in_specs += [pl.BlockSpec((rows, width), lambda j, i, pick: (0, 0))] * (n * halves)
    args = [*cots, *(x for half in gateds for x in half)]
    if base is not None:
        in_specs.append(
            pl.BlockSpec((1, depth, width), lambda j, i, pick: (j + skip, 0, lead + i))
        )
        args.append(base)
    return pl.pallas_call(
        functools.partial(rows_kernel, n, halves),
        grid_spec=pltpu.PrefetchScalarGridSpec(
            num_scalar_prefetch=1,
            grid=(blocks, halves),
            in_specs=in_specs,
            out_specs=pl.BlockSpec((1, depth, width), lambda j, i, pick: (j, 0, i)),
        ),
        out_shape=jax.ShapeDtypeStruct((blocks, depth, halves * width), dtype),
        compiler_params=params(),
        cost_estimate=cost(2 * n * rows * depth * width, 2 * n * rows * (depth + width)),
    )(pick, *args)


def second_kernel(halves, rows_ref, *refs):
    out = refs[-1]

    def write(came):
        out[...] = (rows_ref[0].astype(F32) + came[...].astype(F32)).astype(out.dtype)

    for h in range(halves):
        pl.when(pl.program_id(0) == h)(functools.partial(write, refs[h]))


def second_sums(rows, came):
    _, depth, width = rows.shape
    halves = len(came)
    cols = width // halves
    return pl.pallas_call(
        functools.partial(second_kernel, halves),
        grid=(halves, 2),
        in_specs=[pl.BlockSpec((1, depth // 2, cols), lambda h, i: (0, i, h))]
        + [pl.BlockSpec((depth // 2, cols), lambda h, i: (i, 0))] * halves,
        out_specs=pl.BlockSpec((depth // 2, cols), lambda h, i: (i, h)),
        out_shape=jax.ShapeDtypeStruct((depth, width), BF16),
        compiler_params=params(),
        cost_estimate=cost(depth * width, 6 * depth * width),
    )(rows, *came)


def third_kernel(halves, at, rows_ref, outer_ref, inner_ref, *refs):
    up_out, down_out = refs[halves:]
    mine = rows_ref[0].astype(F32)
    outer, inner = outer_ref[...].astype(F32), inner_ref[...].astype(F32)
    add_up = jnp.where(at[0] == 1, outer, inner)
    add_down = jnp.where(at[0] == 1, inner, outer)

    def write(first):
        other = first[...].astype(F32)
        up_out[...] = (jnp.where(at[1] == 1, other, mine) + add_up).astype(BF16)
        down_out[...] = (jnp.where(at[0] == 1, other, mine) + add_down).astype(BF16)

    for h in range(halves):
        pl.when(pl.program_id(0) == h)(functools.partial(write, refs[h]))


def third_sums(at, rows, outer, inner, first):
    _, depth, width = rows.shape
    halves = len(first)
    cols = width // halves
    whole = pl.BlockSpec((depth // 2, cols), lambda h, i, at: (i, h))
    shape = jax.ShapeDtypeStruct((depth, width), BF16)
    return pl.pallas_call(
        functools.partial(third_kernel, halves),
        grid_spec=pltpu.PrefetchScalarGridSpec(
            num_scalar_prefetch=1,
            grid=(halves, 2),
            in_specs=[pl.BlockSpec((1, depth // 2, cols), lambda h, i, at: (1, i, h)), whole, whole]
            + [pl.BlockSpec((depth // 2, cols), lambda h, i, at: (i, 0))] * halves,
            out_specs=[whole, whole],
        ),
        out_shape=[shape, shape],
        compiler_params=params(),
        cost_estimate=cost(4 * depth * width, 12 * depth * width),
    )(at, rows, outer, inner, *first)


def last_kernel(rows_ref, below, above, out):
    total = rows_ref[0].astype(F32) + below[...].astype(F32) + above[...].astype(F32)
    out[...] = total.astype(out.dtype)


def last_sums(rows, below, above):
    _, depth, width = rows.shape
    tile = depth // 4
    whole = pl.BlockSpec((tile, width), lambda i: (i, 0))
    return pl.pallas_call(
        last_kernel,
        grid=(4,),
        in_specs=[pl.BlockSpec((1, tile, width), lambda i: (2, i, 0)), whole, whole],
        out_specs=whole,
        out_shape=jax.ShapeDtypeStruct((depth, width), BF16),
        compiler_params=params(),
        cost_estimate=cost(2 * depth * width, 8 * depth * width),
    )(rows, below, above)


def shards(seq, ch, queries, keys, values, filters, grad_out, out_weight):
    inner = seq // LINE
    rows, width = queries.shape
    depth = out_weight.shape[0]
    chunks = 2 if width % (2 * LANES) == 0 else 1
    cols = width // chunks
    place = lax.axis_index("seq")
    z, y = place // inner, place % inner

    def send(x, pairs):
        return lax.ppermute(x, "seq", pairs)

    def along_line(x, pairs):
        return send(x, [(a * inner + i, b * inner + i) for a, b in pairs for i in range(inner)])

    def around_inner(x, shift):
        return send(
            x, [(a * inner + i, a * inner + (i + shift) % inner) for a in range(LINE) for i in range(inner)]
        )

    each = range(chunks)
    up_pairs, down_pairs = [(0, 1), (1, 2), (2, 3)], [(1, 0), (2, 1), (3, 2)]

    def merge(up, down):
        return jnp.where(z >= 2, up, down)

    pick = jnp.stack(
        [
            z,
            jnp.where(z == 0, 1, z - 1),
            jnp.where(z >= 2, z - 2, z + 2),
            jnp.where(z == 3, 0, jnp.where(z == 1, 2, 3)),
            jnp.where(z == 0, 1, 0),
            jnp.where((z == 0) | (z == 3), 1, 0),
        ]
    ).astype(jnp.int32)

    def swap_gated(h):
        return [around_inner(gateds[h], r) for r in range(1, inner)]

    even = z % 2 == 0
    first_pick = jnp.where(even, 3, 0).astype(jnp.int32).reshape(1)
    rest_pick = jnp.stack(
        [
            jnp.where(z == 0, 2, jnp.where(z == 1, 3, jnp.where(z == 2, 0, 1))),
            jnp.where(even, 1, 2),
            z,
        ]
    ).astype(jnp.int32)

    places = jnp.stack([z == 1, z == 2]).astype(jnp.int32)

    def rows_first(h):
        return weight_rows(first_pick, cots[1:], got[h : h + 1], BF16, base, 0, h)[0]

    def send_first(x):
        return along_line(x, [(0, 1), (3, 2)])

    def send_second(x):
        return along_line(x, [(0, 1), (3, 2)]), along_line(x, [(1, 2), (2, 1)])

    def send_third(up, down):
        return along_line(up, up_pairs), along_line(down, down_pairs)

    def shares(span):
        return [gate_grad(pick, cots[r], weights, span) for r in range(1, inner)]

    def send_shares(parts):
        return [around_inner(part, inner - r) for r, part in enumerate(parts, 1)]

    gateds, mixeds, got, sums, first = ([None] * chunks for _ in range(5))
    later_halves = list(each[1:])
    spans = [(h, 0, cols, h * cols) for h in each]
    parts, others, gms, laters, taps = ([None] * chunks for _ in range(5))

    prior = product_of(keys[rows - FILT :], values[rows - FILT :])
    cot_here = after(grad_out, prior)
    prior = send(prior, [(i, i + 1) for i in range(seq - 1)])
    paired = inner == 2 and ch == LINE
    other = cot_here
    cots = []
    if paired:
        kept = lax.dynamic_slice(cot_here, (0, y * depth), (rows, depth))
        other = lax.dynamic_slice(cot_here, (0, (1 - y) * depth), (rows, depth))
        cots = [lax.all_gather(kept, "ch", axis=0, tiled=False)]
    back, ahead = tables(filters)
    prior, other, weight = fence(prior, other, out_weight)

    up1, down1 = along_line(weight, up_pairs), along_line(weight, down_pairs)
    swapped = around_inner(other, 1) if paired else other
    for h in each:
        gateds[h], mixeds[h] = forward(queries, keys, values, prior, back, h, chunks)
    up1, down1, swapped, gateds, cots, prior = fence(up1, down1, swapped, gateds, cots, prior)

    up2 = along_line(up1, [(1, 2), (2, 3)])
    down2 = along_line(down1, [(2, 1), (1, 0)])
    if paired:
        cots.append(lax.all_gather(swapped, "ch", axis=0, tiled=False))
    else:
        full = lax.all_gather(swapped, "ch", axis=1, tiled=True)
        full = full.reshape(rows, LINE, inner, depth).transpose(2, 1, 0, 3)
        for shift in range(inner):
            part = lax.dynamic_index_in_dim(full, (y + shift) % inner, 0, keepdims=False)
            cots.append(part if shift == 0 else around_inner(part, shift))
    for h in each:
        got[h] = swap_gated(h)
    all_pick = jnp.concatenate([first_pick, rest_pick])
    base = weight_rows(all_pick, cots[:1], [[x] for x in gateds], F32)

    got[0], cots, base = fence(got[0], cots, base)
    first[0] = rows_first(0)
    sums[0] = send_first(first[0])
    up2, down2, first[0] = fence(up2, down2, first[0])

    second = merge(up2, down2)
    third = along_line(second, [(2, 3), (1, 0)])
    got, second, sums[0] = fence(got, second, sums[0])
    for h in later_halves:
        first[h] = rows_first(h)
        sums[h] = send_first(first[h])
    third, first = fence(third, first)

    weights = [weight, up1, down1, second, third]
    parts[0] = shares(spans[0])
    others[0] = send_shares(parts[0])
    parts[0], got, third = fence(parts[0], got, third)
    rest = weight_rows(rest_pick, cots[1:], got, BF16, base, 1)
    rest, third = fence(rest, third)
    weights = [weight, up1, down1, second, third]
    for h in later_halves:
        parts[h] = shares(spans[h])
        others[h] = send_shares(parts[h])
    sums, rest, parts, third = fence(sums, rest, parts, third)
    sums = send_second(second_sums(rest, sums))
    weights = [weight, up1, down1, second, third]
    owns = [gate_grad(pick, cots[0], weights, span) for span in spans]
    others[0], owns = fence(others[0], owns)

    grad_queries = None
    grad_kv = None
    back_pairs = [(i + 1, i) for i in range(seq - 1)]
    for h, span in enumerate(spans):
        grad_queries, gms[h], edge, taps[h] = middle(
            owns[h], others[h], queries, keys, values, mixeds[h], prior, grad_queries, span
        )
        laters[h] = send(edge, back_pairs)
        if h == 0:
            sums = send_third(*third_sums(places, rest, *after(sums, edge), first))
            others, owns, edge = fence(others, owns, edge)
    gms, _ = fence(gms, edge)
    for h, span in enumerate(spans):
        grad_kv = backward(gms[h], laters[h], keys, values, ahead, grad_kv, span)
        if h == 0:
            sums, grad_kv = fence(sums, grad_kv)
    grad_weight = last_sums(rest, *sums)
    taps = jnp.concatenate(taps, axis=0)[:, 1 : FILT + 1][:, ::-1]
    taps = taps.T.reshape(seq, FILT // seq, -1)
    taps = jnp.sum(lax.all_to_all(taps, "seq", 0, 0), axis=0)
    return grad_queries, *grad_kv, taps.T, grad_weight


def solution(mesh):
    sizes = dict(mesh.shape)
    return jax.shard_map(
        functools.partial(shards, sizes["seq"], sizes["ch"]),
        mesh=mesh,
        in_specs=(
            P("seq", "ch"),
            P("seq", "ch"),
            P("seq", "ch"),
            P("ch", None),
            P("seq", "ch"),
            P("seq", "ch"),
        ),
        out_specs=(P("seq", "ch"), P("seq", "ch"), P("seq", "ch"), P("ch", "seq"), P("seq", "ch")),
        check_vma=False,
    )
```

```python
import functools

import jax
import jax.numpy as jnp
from jax import lax
from jax.experimental import pallas as pl
from jax.experimental.pallas import tpu as pltpu
from jax.sharding import PartitionSpec as P

GROUP = 16
FILT = 128
LANES = 128
GPT = LANES // GROUP
LINE = 4
F32 = jnp.float32
BF16 = jnp.bfloat16
VMEM_LIMIT = 48 * 1024 * 1024


def params():
    return pltpu.CompilerParams(vmem_limit_bytes=VMEM_LIMIT)


def cost(flops, nbytes):
    return pl.CostEstimate(flops=int(flops) // 64, bytes_accessed=int(nbytes) // 64, transcendentals=0)


def fence(*arrays):
    return lax.optimization_barrier(arrays)


def after(x, *others):
    return lax.optimization_barrier((x, *others))[0]


def table_kernel(back_ref, ahead_ref, back_out, ahead_out):
    for seed, out in ((back_ref, back_out), (ahead_ref, ahead_out)):
        for g in range(GPT):
            rows = jnp.broadcast_to(seed[g : g + 1, :], (FILT, 2 * FILT))
            turned = pltpu.roll(rows, 0, 1, stride=1, stride_axis=0)
            out[g * FILT : (g + 1) * FILT, :] = turned.astype(BF16)


def tables(filters):
    groups = filters.shape[0]
    taps = filters.astype(F32)
    back = jnp.concatenate(
        [jnp.zeros((groups, 1), F32), taps[:, ::-1], jnp.zeros((groups, FILT - 1), F32)], axis=1
    )
    ahead = jnp.concatenate([taps, jnp.zeros((groups, FILT), F32)], axis=1)
    seed = pl.BlockSpec((GPT, 2 * FILT), lambda i: (i, 0))
    full = pl.BlockSpec((GPT * FILT, 2 * FILT), lambda i: (i, 0))
    shape = jax.ShapeDtypeStruct((groups * FILT, 2 * FILT), BF16)
    return pl.pallas_call(
        table_kernel,
        grid=(groups // GPT,),
        in_specs=[seed, seed],
        out_specs=[full, full],
        out_shape=[shape, shape],
        compiler_params=params(),
        cost_estimate=cost(groups * 2**18, groups * 2**17),
    )(back, ahead)


def group_of_lane(rows, cols):
    return (lax.broadcasted_iota(jnp.int32, (rows, cols), 1) % LANES) // GROUP


def windows(ext, b):
    lo = b * FILT
    return jnp.concatenate([ext[lo : lo + 2 * FILT], ext[lo + FILT : lo + 3 * FILT]], axis=1)


def toeplitz(table, ext, blocks):
    group = group_of_lane(FILT, 2 * LANES)
    rows = []
    for b in range(0, blocks, 2):
        out = jnp.dot(table, windows(ext, b), preferred_element_type=F32)
        picked = out[:FILT]
        for g in range(1, GPT):
            picked = jnp.where(group == g, out[g * FILT : (g + 1) * FILT], picked)
        rows += [picked[:, :LANES], picked[:, LANES:]]
    return jnp.concatenate(rows, axis=0)


def product_of(k, v):
    return (k.astype(F32) * v.astype(F32)).astype(BF16)


def forward_kernel(q, k, v, prior, table, gated, mixed_out):
    blocks = q.shape[0] // FILT
    ext = jnp.concatenate([prior[...], product_of(k[...], v[...])], axis=0)
    mixed = toeplitz(table[...], ext, blocks)
    mixed_out[...] = mixed.astype(BF16)
    gated[...] = (q[...].astype(F32) * mixed).astype(BF16)


def forward(q, k, v, prior, table, chunk, chunks):
    rows, width = q.shape
    tiles = width // LANES // chunks
    here = pl.BlockSpec((rows, LANES), lambda i: (0, chunk * tiles + i))
    out = pl.BlockSpec((rows, LANES), lambda i: (0, i))
    shape = jax.ShapeDtypeStruct((rows, width // chunks), BF16)
    return pl.pallas_call(
        forward_kernel,
        grid=(tiles,),
        in_specs=[
            here,
            here,
            here,
            pl.BlockSpec((FILT, LANES), lambda i: (0, chunk * tiles + i)),
            pl.BlockSpec((GPT * FILT, 2 * FILT), lambda i: (chunk * tiles + i, 0)),
        ],
        out_specs=[out, out],
        out_shape=[shape, shape],
        compiler_params=params(),
        cost_estimate=cost(tiles * rows * 2 * 2**18, tiles * rows * 5 * 256 + tiles * 2**19),
    )(q, k, v, prior, table)


def middle_kernel(own, others, q, k, v, mixed, prior, *rest):
    gq_out, gm_out, edge_out, taps_out = rest[-4:]
    blocks = q.shape[0] // FILT
    total = own[...].astype(F32)
    for other in others:
        total = total + other[...].astype(F32)
    gg = total.astype(BF16).astype(F32)
    gq_out[...] = (gg * mixed[...].astype(F32)).astype(BF16)
    gm = (gg * q[...].astype(F32)).astype(BF16)
    gm_out[...] = gm
    edge_out[...] = gm[:FILT]
    ext = jnp.concatenate([prior[...], product_of(k[...], v[...])], axis=0)
    wide = jnp.concatenate([gm[b * FILT : (b + 1) * FILT] for b in range(blocks)], axis=1)
    group = group_of_lane(FILT, blocks * LANES)
    stack = jnp.concatenate(
        [jnp.where(group == g, wide, jnp.zeros_like(wide)) for g in range(GPT)], axis=0
    )
    near = jnp.concatenate([ext[b * FILT : (b + 2) * FILT] for b in range(blocks)], axis=1)
    lag = lax.dot_general(stack, near, (((1,), (1,)), ((), ())), preferred_element_type=F32)
    lag = lag.reshape(GPT, FILT, 2 * FILT)
    half = FILT // 2
    while half >= 8:
        lag = lag[:, :half] + pltpu.roll(lag[:, half:], 2 * FILT - half, 2)
        half //= 2
    while half >= 1:
        lag = lag + pltpu.roll(pltpu.roll(lag, 2 * FILT - half, 2), 8 - half, 1)
        half //= 2
    taps_out[...] = lag[:, 0, :]


def middle(own, others, q, k, v, mixed, prior, filled, span):
    rows, width = q.shape
    _, local, cols, first = span
    tiles = cols // LANES
    here = pl.BlockSpec((rows, LANES), lambda i: (0, first // LANES + i))
    part = pl.BlockSpec((rows, LANES), lambda i: (0, i))
    edge = pl.BlockSpec((FILT, LANES), lambda i: (0, i))
    n_other = len(others)

    def kernel(own_ref, *refs):
        middle_kernel(own_ref, refs[:n_other], *refs[n_other:])

    args = [own, *others, q, k, v, mixed, prior]
    in_specs = [part] * (1 + n_other) + [here] * 3
    in_specs.append(pl.BlockSpec((rows, LANES), lambda i: (0, local // LANES + i)))
    in_specs.append(pl.BlockSpec((FILT, LANES), lambda i: (0, first // LANES + i)))
    aliases = {}
    if filled is not None:
        aliases = {len(args): 0}
        args.append(filled)
        in_specs.append(pl.BlockSpec(memory_space=pl.ANY))
    return pl.pallas_call(
        kernel,
        grid=(tiles,),
        in_specs=in_specs,
        out_specs=[here, part, edge, pl.BlockSpec((GPT, 2 * FILT), lambda i: (i, 0))],
        out_shape=[
            jax.ShapeDtypeStruct((rows, width), BF16),
            jax.ShapeDtypeStruct((rows, cols), BF16),
            jax.ShapeDtypeStruct((FILT, cols), BF16),
            jax.ShapeDtypeStruct((cols // GROUP, 2 * FILT), F32),
        ],
        input_output_aliases=aliases,
        compiler_params=params(),
        cost_estimate=cost(tiles * rows * 2 * 2**18, tiles * rows * 9 * 256),
    )(*args)


def backward_kernel(gm, later, k, v, table, *rest):
    gk_out, gv_out = rest[-2:]
    blocks = gm.shape[0] // FILT
    ext = jnp.concatenate([gm[...], later[...]], axis=0)
    gp = toeplitz(table[...], ext, blocks)
    gk_out[...] = (gp * v[...].astype(F32)).astype(BF16)
    gv_out[...] = (gp * k[...].astype(F32)).astype(BF16)


def backward(gm, later, k, v, table, filled, span):
    rows, width = k.shape
    _, _, cols, first = span
    tiles = cols // LANES
    here = pl.BlockSpec((rows, LANES), lambda i: (0, first // LANES + i))
    part = pl.BlockSpec((rows, LANES), lambda i: (0, i))
    args = [gm, later, k, v, table]
    in_specs = [
        part,
        pl.BlockSpec((FILT, LANES), lambda i: (0, i)),
        here,
        here,
        pl.BlockSpec((GPT * FILT, 2 * FILT), lambda i: (first // LANES + i, 0)),
    ]
    aliases = {}
    if filled is not None:
        aliases = {len(args): 0, len(args) + 1: 1}
        args += filled
        in_specs += [pl.BlockSpec(memory_space=pl.ANY)] * 2
    shape = jax.ShapeDtypeStruct((rows, width), BF16)
    return pl.pallas_call(
        backward_kernel,
        grid=(tiles,),
        in_specs=in_specs,
        out_specs=[here, here],
        out_shape=[shape, shape],
        input_output_aliases=aliases,
        compiler_params=params(),
        cost_estimate=cost(tiles * rows * 2 * 2**18, tiles * rows * 5 * 256 + tiles * 2**19),
    )(*args)


def gate_kernel(slots, pick, *refs):
    out = refs[-1]
    cots, refs = refs[: len(slots)], list(refs[len(slots) :])
    blocks = []
    for slot in slots:
        block = refs.pop(0)[...]
        if slot in (1, 3):
            block = jnp.where(pick[LINE + slot // 2] == 1, block, refs.pop(0)[...])
        blocks.append(block)
    cot, block = cots[0][0], blocks[0]
    if len(slots) > 1:
        cot = jnp.concatenate([ref[0] for ref in cots], axis=1)
        block = jnp.concatenate(blocks, axis=0)
    total = jnp.dot(cot, block, preferred_element_type=F32)
    if len(refs) > 1:
        total = total + refs[0][...]
    out[...] = total.astype(out.dtype)


def gate_grad(pick, cot, weights, span, slots, dtype, base=None):
    _, rows, depth = cot.shape
    _, _, width, first = span
    tile = min(256, width)
    tiles = width // tile

    def cot_spec(j):
        return pl.BlockSpec((1, rows, depth), lambda i, pick: (pick[j], 0, 0))

    blocks = [x for slot in slots for x in weights[slot]]
    in_specs = [cot_spec(j) for j in slots]
    in_specs += [pl.BlockSpec((depth, tile), lambda i, pick: (0, first // tile + i))] * len(blocks)
    args = [cot] * len(slots) + blocks
    if base is not None:
        in_specs.append(pl.BlockSpec((rows, tile), lambda i, pick: (0, first // tile + i)))
        args.append(base)
    return pl.pallas_call(
        functools.partial(gate_kernel, slots),
        grid_spec=pltpu.PrefetchScalarGridSpec(
            num_scalar_prefetch=1,
            grid=(tiles,),
            in_specs=in_specs,
            out_specs=pl.BlockSpec((rows, tile), lambda i, pick: (0, i)),
        ),
        out_shape=jax.ShapeDtypeStruct((rows, width), dtype),
        compiler_params=params(),
        cost_estimate=cost(
            2 * rows * len(slots) * depth * width, 2 * len(slots) * depth * (rows + width)
        ),
    )(pick, *args)


def rows_kernel(n, halves, pick, *refs):
    out = refs[-1]
    cot = refs[0][0]
    if n > 1:
        cot = jnp.concatenate([ref[0] for ref in refs[:n]], axis=0)

    def write(gated_refs):
        gated = gated_refs[0][...]
        if n > 1:
            gated = jnp.concatenate([ref[...] for ref in gated_refs], axis=0)
        total = lax.dot_general(cot, gated, (((0,), (0,)), ((), ())), preferred_element_type=F32)
        if len(refs) > n + n * halves + 1:
            total = total + refs[-2][0]
        out[0] = total.astype(out.dtype)

    for h in range(halves):
        pl.when(pl.program_id(1) == h)(
            functools.partial(write, refs[n + n * h : n + n * (h + 1)])
        )


def weight_rows(pick, cots, gateds, dtype, base=None, skip=0, lead=0):
    _, rows, depth = cots[0].shape
    width = gateds[0][0].shape[1]
    blocks = pick.shape[0]
    n, halves = len(cots), len(gateds)
    in_specs = [pl.BlockSpec((1, rows, depth), lambda j, i, pick: (pick[j], 0, 0))] * n
    in_specs += [pl.BlockSpec((rows, width), lambda j, i, pick: (0, 0))] * (n * halves)
    args = [*cots, *(x for half in gateds for x in half)]
    if base is not None:
        in_specs.append(
            pl.BlockSpec((1, depth, width), lambda j, i, pick: (j + skip, 0, lead + i))
        )
        args.append(base)
    return pl.pallas_call(
        functools.partial(rows_kernel, n, halves),
        grid_spec=pltpu.PrefetchScalarGridSpec(
            num_scalar_prefetch=1,
            grid=(blocks, halves),
            in_specs=in_specs,
            out_specs=pl.BlockSpec((1, depth, width), lambda j, i, pick: (j, 0, i)),
        ),
        out_shape=jax.ShapeDtypeStruct((blocks, depth, halves * width), dtype),
        compiler_params=params(),
        cost_estimate=cost(2 * n * rows * depth * width, 2 * n * rows * (depth + width)),
    )(pick, *args)


STEPS = 4


def half_spec(k, block, depth, cols):
    def place(h, i, *_):
        row = jnp.where(h == k, i, jnp.where(h < k, 0, STEPS - 1))
        return (row, 0) if block is None else (block, row, 0)

    shape = (depth // STEPS, cols)
    return pl.BlockSpec(shape if block is None else (1, *shape), place)


def whole_spec(depth, cols):
    return pl.BlockSpec((depth // STEPS, cols), lambda h, i, *_: (i, h))


def by_half(halves, write):
    for h in range(halves):
        pl.when(pl.program_id(0) == h)(functools.partial(write, h))


def second_kernel(halves, *refs):
    out = refs[-1]

    def write(h):
        out[...] = (refs[h][0].astype(F32) + refs[halves + h][...].astype(F32)).astype(out.dtype)

    by_half(halves, write)


def second_sums(rows, came):
    _, depth, cols = rows[0].shape
    halves = len(rows)
    return pl.pallas_call(
        functools.partial(second_kernel, halves),
        grid=(halves, STEPS),
        in_specs=[half_spec(k, 0, depth, cols) for k in range(halves)]
        + [half_spec(k, None, depth, cols) for k in range(halves)],
        out_specs=whole_spec(depth, cols),
        out_shape=jax.ShapeDtypeStruct((depth, halves * cols), BF16),
        compiler_params=params(),
        cost_estimate=cost(depth * cols, 6 * depth * cols),
    )(*rows, *came)


def third_kernel(halves, at, outer, inner, *refs):
    up_out, down_out = refs[-2:]

    def write(h):
        mine, other = refs[h][0].astype(F32), refs[halves + h][...].astype(F32)
        from_outer, from_inner = outer[...].astype(F32), inner[...].astype(F32)
        up = jnp.where(at[1] == 1, other, mine) + jnp.where(at[0] == 1, from_outer, from_inner)
        down = jnp.where(at[0] == 1, other, mine) + jnp.where(at[0] == 1, from_inner, from_outer)
        up_out[...] = up.astype(BF16)
        down_out[...] = down.astype(BF16)

    by_half(halves, write)


def third_sums(at, rows, outer, inner, first):
    _, depth, cols = rows[0].shape
    halves = len(rows)
    whole = whole_spec(depth, cols)
    shape = jax.ShapeDtypeStruct((depth, halves * cols), BF16)
    return pl.pallas_call(
        functools.partial(third_kernel, halves),
        grid_spec=pltpu.PrefetchScalarGridSpec(
            num_scalar_prefetch=1,
            grid=(halves, STEPS),
            in_specs=[whole, whole]
            + [half_spec(k, 1, depth, cols) for k in range(halves)]
            + [half_spec(k, None, depth, cols) for k in range(halves)],
            out_specs=[whole, whole],
        ),
        out_shape=[shape, shape],
        compiler_params=params(),
        cost_estimate=cost(4 * depth * cols, 12 * depth * cols),
    )(at, outer, inner, *rows, *first)


def last_kernel(halves, below, above, *refs):
    out = refs[-1]

    def write(h):
        total = refs[h][0].astype(F32) + below[...].astype(F32) + above[...].astype(F32)
        out[...] = total.astype(out.dtype)

    by_half(halves, write)


def last_sums(rows, below, above):
    _, depth, cols = rows[0].shape
    halves = len(rows)
    whole = whole_spec(depth, cols)
    return pl.pallas_call(
        functools.partial(last_kernel, halves),
        grid=(halves, STEPS),
        in_specs=[whole, whole] + [half_spec(k, 2, depth, cols) for k in range(halves)],
        out_specs=whole,
        out_shape=jax.ShapeDtypeStruct((depth, halves * cols), BF16),
        compiler_params=params(),
        cost_estimate=cost(2 * depth * cols, 8 * depth * cols),
    )(below, above, *rows)


def shards(seq, ch, queries, keys, values, filters, grad_out, out_weight):
    inner = seq // LINE
    rows, width = queries.shape
    depth = out_weight.shape[0]
    chunks = 2 if width % (2 * LANES) == 0 else 1
    cols = width // chunks
    place = lax.axis_index("seq")
    z, y = place // inner, place % inner

    def send(x, pairs):
        return lax.ppermute(x, "seq", pairs)

    def along_line(x, pairs):
        return send(x, [(a * inner + i, b * inner + i) for a, b in pairs for i in range(inner)])

    def around_inner(x, shift):
        return send(
            x, [(a * inner + i, a * inner + (i + shift) % inner) for a in range(LINE) for i in range(inner)]
        )

    each = range(chunks)
    up_pairs, down_pairs = [(0, 1), (1, 2), (2, 3)], [(1, 0), (2, 1), (3, 2)]

    def merge(up, down):
        return jnp.where(z >= 2, up, down)

    pick = jnp.stack(
        [
            z,
            jnp.where(z == 0, 1, z - 1),
            jnp.where(z >= 2, z - 2, z + 2),
            jnp.where(z == 3, 0, jnp.where(z == 1, 2, 3)),
            jnp.where(z == 0, 1, 0),
            jnp.where((z == 0) | (z == 3), 1, 0),
        ]
    ).astype(jnp.int32)

    def swap_gated(h):
        return [around_inner(gateds[h], r) for r in range(1, inner)]

    even = z % 2 == 0
    first_pick = jnp.where(even, 3, 0).astype(jnp.int32).reshape(1)
    rest_pick = jnp.stack(
        [
            jnp.where(z == 0, 2, jnp.where(z == 1, 3, jnp.where(z == 2, 0, 1))),
            jnp.where(even, 1, 2),
            z,
        ]
    ).astype(jnp.int32)

    places = jnp.stack([z == 1, z == 2]).astype(jnp.int32)

    def rows_first(h):
        return weight_rows(first_pick, cots[1:], got[h : h + 1], BF16, base, 0, h)[0]

    def rows_rest(h):
        return weight_rows(rest_pick, cots[1:], got[h : h + 1], BF16, base, 1, h)

    def send_first(x):
        return along_line(x, [(0, 1), (3, 2)])

    def send_second(x):
        return along_line(x, [(0, 1), (3, 2)]), along_line(x, [(1, 2), (2, 1)])

    def send_third(up, down):
        return along_line(up, up_pairs), along_line(down, down_pairs)

    def shares(span):
        return [
            gate_grad(pick, cot, weights, span, (3,), BF16, begun)
            for cot, begun in zip(cots[1:], other_begun)
        ]

    def send_shares(parts):
        return [around_inner(part, inner - r) for r, part in enumerate(parts, 1)]

    gateds, mixeds, got, sums, first = ([None] * chunks for _ in range(5))
    later_halves = list(each[1:])
    spans = [(h, 0, cols, h * cols) for h in each]
    parts, others, gms, laters, taps = ([None] * chunks for _ in range(5))

    prior = product_of(keys[rows - FILT :], values[rows - FILT :])
    cot_here = after(grad_out, prior)
    prior = send(prior, [(i, i + 1) for i in range(seq - 1)])
    paired = inner == 2 and ch == LINE
    other = cot_here
    cots = []
    if paired:
        kept = lax.dynamic_slice(cot_here, (0, y * depth), (rows, depth))
        other = lax.dynamic_slice(cot_here, (0, (1 - y) * depth), (rows, depth))
        cots = [lax.all_gather(kept, "ch", axis=0, tiled=False)]
    back, ahead = tables(filters)
    prior, other, weight, back = fence(prior, other, out_weight, back)

    up1, down1 = along_line(weight, up_pairs), along_line(weight, down_pairs)
    swapped = around_inner(other, 1) if paired else other
    for h in each:
        gateds[h], mixeds[h] = forward(queries, keys, values, prior, back, h, chunks)
    swapped, gateds, cots, prior = fence(swapped, gateds, cots, prior)

    for h in each:
        got[h] = swap_gated(h)
    if paired:
        cots.append(lax.all_gather(swapped, "ch", axis=0, tiled=False))
    else:
        full = lax.all_gather(swapped, "ch", axis=1, tiled=True)
        full = full.reshape(rows, LINE, inner, depth).transpose(2, 1, 0, 3)
        for shift in range(inner):
            part = lax.dynamic_index_in_dim(full, (y + shift) % inner, 0, keepdims=False)
            cots.append(part if shift == 0 else around_inner(part, shift))
    up1, down1, gateds, cots[0] = fence(up1, down1, gateds, cots[0])

    up2 = along_line(up1, [(1, 2), (2, 3)])
    down2 = along_line(down1, [(2, 1), (1, 0)])
    all_pick = jnp.concatenate([first_pick, rest_pick])
    base = weight_rows(all_pick, cots[:1], [[x] for x in gateds], F32)
    full_span = (0, 0, width, 0)
    weights = [[weight], [down1, up1]]
    own_begun = gate_grad(pick, cots[0], weights, full_span, (0, 1), F32)
    got[0], cots, base, own_begun = fence(got[0], cots, base, own_begun)

    first[0] = rows_first(0)
    sums[0] = send_first(first[0])
    up2, down2, first[0] = fence(up2, down2, first[0])
    second = merge(up2, down2)
    third = along_line(second, [(2, 3), (1, 0)])
    rest = [None] * chunks
    rest[0] = rows_rest(0)
    got, second, sums[0], rest[0] = fence(got, second, sums[0], rest[0])
    for h in later_halves:
        first[h] = rows_first(h)
        sums[h] = send_first(first[h])
    held, first = fence(second, first)
    weights = [[weight], [down1, up1], [held]]
    other_begun = [gate_grad(pick, cot, weights, full_span, (0, 1, 2), F32) for cot in cots[1:]]
    third, other_begun = fence(third, other_begun)

    weights = [[weight], [down1, up1], [second], [third, down1]]
    parts[0] = shares(spans[0])
    others[0] = send_shares(parts[0])
    parts[0], got = fence(parts[0], got)
    for h in later_halves:
        rest[h] = rows_rest(h)
    for h in later_halves:
        parts[h] = shares(spans[h])
        others[h] = send_shares(parts[h])
    sums, rest, parts = fence(sums, rest, parts)
    sums = send_second(second_sums(rest, sums))
    held, _ = fence(own_begun, parts)
    owns = [gate_grad(pick, cots[0], weights, span, (2, 3), BF16, held) for span in spans]
    others[0], owns = fence(others[0], owns)

    grad_queries = None
    grad_kv = None
    back_pairs = [(i + 1, i) for i in range(seq - 1)]
    for h, span in enumerate(spans):
        grad_queries, gms[h], edge, taps[h] = middle(
            owns[h], others[h], queries, keys, values, mixeds[h], prior, grad_queries, span
        )
        laters[h] = send(edge, back_pairs)
        if h == 0:
            sums = send_third(*third_sums(places, rest, *after(sums, edge), first))
            others, owns, edge = fence(others, owns, edge)
    gms, _ = fence(gms, edge)
    for h, span in enumerate(spans):
        grad_kv = backward(gms[h], laters[h], keys, values, ahead, grad_kv, span)
        if h == 0:
            sums, grad_kv = fence(sums, grad_kv)
    grad_weight = last_sums(rest, *sums)
    taps = jnp.concatenate(taps, axis=0)[:, 1 : FILT + 1][:, ::-1]
    taps = taps.T.reshape(seq, FILT // seq, -1)
    taps = jnp.sum(lax.all_to_all(taps, "seq", 0, 0), axis=0)
    return grad_queries, *grad_kv, taps.T, grad_weight


def solution(mesh):
    sizes = dict(mesh.shape)
    return jax.shard_map(
        functools.partial(shards, sizes["seq"], sizes["ch"]),
        mesh=mesh,
        in_specs=(
            P("seq", "ch"),
            P("seq", "ch"),
            P("seq", "ch"),
            P("ch", None),
            P("seq", "ch"),
            P("seq", "ch"),
        ),
        out_specs=(P("seq", "ch"), P("seq", "ch"), P("seq", "ch"), P("ch", "seq"), P("seq", "ch")),
        check_vma=False,
    )
```

```python
import functools

import jax
import jax.numpy as jnp
from jax import lax
from jax.experimental import pallas as pl
from jax.experimental.pallas import tpu as pltpu
from jax.sharding import PartitionSpec as P

GROUP = 16
FILT = 128
LANES = 128
GPT = LANES // GROUP
LINE = 4
F32 = jnp.float32
BF16 = jnp.bfloat16
VMEM_LIMIT = 48 * 1024 * 1024


def params():
    return pltpu.CompilerParams(vmem_limit_bytes=VMEM_LIMIT)


def cost(flops, nbytes):
    return pl.CostEstimate(flops=int(flops) // 64, bytes_accessed=int(nbytes) // 64, transcendentals=0)


def fence(*arrays):
    return lax.optimization_barrier(arrays)


def after(x, *others):
    return lax.optimization_barrier((x, *others))[0]


def table_kernel(back_ref, ahead_ref, back_out, ahead_out):
    for seed, out in ((back_ref, back_out), (ahead_ref, ahead_out)):
        for g in range(GPT):
            rows = jnp.broadcast_to(seed[g : g + 1, :], (FILT, 2 * FILT))
            turned = pltpu.roll(rows, 0, 1, stride=1, stride_axis=0)
            out[g * FILT : (g + 1) * FILT, :] = turned.astype(BF16)


def tables(filters):
    groups = filters.shape[0]
    taps = filters.astype(F32)
    back = jnp.concatenate(
        [jnp.zeros((groups, 1), F32), taps[:, ::-1], jnp.zeros((groups, FILT - 1), F32)], axis=1
    )
    ahead = jnp.concatenate([taps, jnp.zeros((groups, FILT), F32)], axis=1)
    seed = pl.BlockSpec((GPT, 2 * FILT), lambda i: (i, 0))
    full = pl.BlockSpec((GPT * FILT, 2 * FILT), lambda i: (i, 0))
    shape = jax.ShapeDtypeStruct((groups * FILT, 2 * FILT), BF16)
    return pl.pallas_call(
        table_kernel,
        grid=(groups // GPT,),
        in_specs=[seed, seed],
        out_specs=[full, full],
        out_shape=[shape, shape],
        compiler_params=params(),
        cost_estimate=cost(groups * 2**18, groups * 2**17),
    )(back, ahead)


def group_of_lane(rows, cols):
    return (lax.broadcasted_iota(jnp.int32, (rows, cols), 1) % LANES) // GROUP


def windows(ext, b):
    lo = b * FILT
    return jnp.concatenate([ext[lo : lo + 2 * FILT], ext[lo + FILT : lo + 3 * FILT]], axis=1)


def toeplitz(table, ext, blocks):
    group = group_of_lane(FILT, 2 * LANES)
    rows = []
    for b in range(0, blocks, 2):
        out = jnp.dot(table, windows(ext, b), preferred_element_type=F32)
        picked = out[:FILT]
        for g in range(1, GPT):
            picked = jnp.where(group == g, out[g * FILT : (g + 1) * FILT], picked)
        rows += [picked[:, :LANES], picked[:, LANES:]]
    return jnp.concatenate(rows, axis=0)


def product_of(k, v):
    return (k.astype(F32) * v.astype(F32)).astype(BF16)


def forward_kernel(q, k, v, prior, table, gated, mixed_out):
    blocks = q.shape[0] // FILT
    ext = jnp.concatenate([prior[...], product_of(k[...], v[...])], axis=0)
    mixed = toeplitz(table[...], ext, blocks)
    mixed_out[...] = mixed.astype(BF16)
    gated[...] = (q[...].astype(F32) * mixed).astype(BF16)


def forward(q, k, v, prior, table, chunk, chunks):
    rows, width = q.shape
    tiles = width // LANES // chunks
    here = pl.BlockSpec((rows, LANES), lambda i: (0, chunk * tiles + i))
    out = pl.BlockSpec((rows, LANES), lambda i: (0, i))
    shape = jax.ShapeDtypeStruct((rows, width // chunks), BF16)
    return pl.pallas_call(
        forward_kernel,
        grid=(tiles,),
        in_specs=[
            here,
            here,
            here,
            pl.BlockSpec((FILT, LANES), lambda i: (0, i)),
            pl.BlockSpec((GPT * FILT, 2 * FILT), lambda i: (chunk * tiles + i, 0)),
        ],
        out_specs=[out, out],
        out_shape=[shape, shape],
        compiler_params=params(),
        cost_estimate=cost(tiles * rows * 2 * 2**18, tiles * rows * 5 * 256 + tiles * 2**19),
    )(q, k, v, prior, table)


def middle_kernel(own, others, q, k, v, mixed, prior, *rest):
    gq_out, gm_out, edge_out, taps_out = rest[-4:]
    blocks = q.shape[0] // FILT
    total = own[...].astype(F32)
    for other in others:
        total = total + other[...].astype(F32)
    gg = total.astype(BF16).astype(F32)
    gq_out[...] = (gg * mixed[...].astype(F32)).astype(BF16)
    gm = (gg * q[...].astype(F32)).astype(BF16)
    gm_out[...] = gm
    edge_out[...] = gm[:FILT]
    ext = jnp.concatenate([prior[...], product_of(k[...], v[...])], axis=0)
    wide = jnp.concatenate([gm[b * FILT : (b + 1) * FILT] for b in range(blocks)], axis=1)
    group = group_of_lane(FILT, blocks * LANES)
    stack = jnp.concatenate(
        [jnp.where(group == g, wide, jnp.zeros_like(wide)) for g in range(GPT)], axis=0
    )
    near = jnp.concatenate([ext[b * FILT : (b + 2) * FILT] for b in range(blocks)], axis=1)
    lag = lax.dot_general(stack, near, (((1,), (1,)), ((), ())), preferred_element_type=F32)
    lag = lag.reshape(GPT, FILT, 2 * FILT)
    half = FILT // 2
    while half >= 8:
        lag = lag[:, :half] + pltpu.roll(lag[:, half:], 2 * FILT - half, 2)
        half //= 2
    while half >= 1:
        lag = lag + pltpu.roll(pltpu.roll(lag, 2 * FILT - half, 2), 8 - half, 1)
        half //= 2
    taps_out[...] = lag[:, 0, :]


def middle(own, others, q, k, v, mixed, prior, filled, chunk, chunks):
    rows, width = q.shape
    tiles = width // LANES // chunks
    groups = width // GROUP // chunks
    here = pl.BlockSpec((rows, LANES), lambda i: (0, chunk * tiles + i))
    part = pl.BlockSpec((rows, LANES), lambda i: (0, i))
    edge = pl.BlockSpec((FILT, LANES), lambda i: (0, i))
    n_other = len(others)

    def kernel(own_ref, *refs):
        middle_kernel(own_ref, refs[:n_other], *refs[n_other:])

    args = [own, *others, q, k, v, mixed, prior]
    in_specs = [part] * (1 + n_other) + [here] * 3 + [part, edge]
    aliases = {}
    if filled is not None:
        aliases = {len(args): 0}
        args.append(filled)
        in_specs.append(pl.BlockSpec(memory_space=pl.ANY))
    return pl.pallas_call(
        kernel,
        grid=(tiles,),
        in_specs=in_specs,
        out_specs=[here, part, edge, pl.BlockSpec((GPT, 2 * FILT), lambda i: (i, 0))],
        out_shape=[
            jax.ShapeDtypeStruct((rows, width), BF16),
            jax.ShapeDtypeStruct((rows, width // chunks), BF16),
            jax.ShapeDtypeStruct((FILT, width // chunks), BF16),
            jax.ShapeDtypeStruct((groups, 2 * FILT), F32),
        ],
        input_output_aliases=aliases,
        compiler_params=params(),
        cost_estimate=cost(tiles * rows * 2 * 2**18, tiles * rows * 9 * 256),
    )(*args)


def backward_kernel(gm, later, k, v, table, *rest):
    gk_out, gv_out = rest[-2:]
    blocks = gm.shape[0] // FILT
    ext = jnp.concatenate([gm[...], later[...]], axis=0)
    gp = toeplitz(table[...], ext, blocks)
    gk_out[...] = (gp * v[...].astype(F32)).astype(BF16)
    gv_out[...] = (gp * k[...].astype(F32)).astype(BF16)


def backward(gm, later, k, v, table, filled, chunk, chunks):
    rows, width = k.shape
    tiles = width // LANES // chunks
    here = pl.BlockSpec((rows, LANES), lambda i: (0, chunk * tiles + i))
    part = pl.BlockSpec((rows, LANES), lambda i: (0, i))
    args = [gm, later, k, v, table]
    in_specs = [
        part,
        pl.BlockSpec((FILT, LANES), lambda i: (0, i)),
        here,
        here,
        pl.BlockSpec((GPT * FILT, 2 * FILT), lambda i: (chunk * tiles + i, 0)),
    ]
    aliases = {}
    if filled is not None:
        aliases = {len(args): 0, len(args) + 1: 1}
        args += filled
        in_specs += [pl.BlockSpec(memory_space=pl.ANY)] * 2
    shape = jax.ShapeDtypeStruct((rows, width), BF16)
    return pl.pallas_call(
        backward_kernel,
        grid=(tiles,),
        in_specs=in_specs,
        out_specs=[here, here],
        out_shape=[shape, shape],
        input_output_aliases=aliases,
        compiler_params=params(),
        cost_estimate=cost(tiles * rows * 2 * 2**18, tiles * rows * 5 * 256 + tiles * 2**19),
    )(*args)


def gate_kernel(pick, *refs):
    own, up, down, second, third, out = refs[LINE:]
    slots = (
        own[...],
        jnp.where(pick[LINE] == 1, down[...], up[...]),
        second[...],
        jnp.where(pick[LINE + 1] == 1, third[...], down[...]),
    )
    cot = jnp.concatenate([ref[0] for ref in refs[:LINE]], axis=1)
    total = jnp.dot(cot, jnp.concatenate(slots, axis=0), preferred_element_type=F32)
    out[...] = total.astype(out.dtype)


def gate_grad(pick, cot, weights):
    _, rows, depth = cot.shape
    width = weights[0].shape[1]
    tile = min(256, width)

    def cot_spec(j):
        return pl.BlockSpec((1, rows, depth), lambda i, pick: (pick[j], 0, 0))

    return pl.pallas_call(
        gate_kernel,
        grid_spec=pltpu.PrefetchScalarGridSpec(
            num_scalar_prefetch=1,
            grid=(width // tile,),
            in_specs=[cot_spec(j) for j in range(LINE)]
            + [pl.BlockSpec((depth, tile), lambda i, pick: (0, i))] * len(weights),
            out_specs=pl.BlockSpec((rows, tile), lambda i, pick: (0, i)),
        ),
        out_shape=jax.ShapeDtypeStruct((rows, width), BF16),
        compiler_params=params(),
        cost_estimate=cost(
            2 * rows * LINE * depth * width, 2 * LINE * depth * (rows + width) + 2 * rows * width
        ),
    )(pick, *([cot] * LINE), *weights)


def rows_kernel(n, pick, *refs):
    out = refs[-1]
    cot, gated = refs[0][0], refs[n][...]
    if n > 1:
        cot = jnp.concatenate([ref[0] for ref in refs[:n]], axis=0)
        gated = jnp.concatenate([ref[...] for ref in refs[n : 2 * n]], axis=0)
    total = lax.dot_general(cot, gated, (((0,), (0,)), ((), ())), preferred_element_type=F32)
    if len(refs) > 2 * n + 1:
        total = total + refs[2 * n][0]
    out[0] = total.astype(out.dtype)


def weight_rows(pick, cots, gateds, dtype, base=None, skip=0):
    _, rows, depth = cots[0].shape
    width = gateds[0].shape[1]
    blocks = pick.shape[0]
    tile = width if blocks > 1 else min(512, width)
    n = len(cots)
    in_specs = [pl.BlockSpec((1, rows, depth), lambda j, i, pick: (pick[j], 0, 0))] * n
    in_specs += [pl.BlockSpec((rows, tile), lambda j, i, pick: (0, i))] * n
    args = [*cots, *gateds]
    if base is not None:
        in_specs.append(pl.BlockSpec((1, depth, tile), lambda j, i, pick: (j + skip, 0, i)))
        args.append(base)
    return pl.pallas_call(
        functools.partial(rows_kernel, n),
        grid_spec=pltpu.PrefetchScalarGridSpec(
            num_scalar_prefetch=1,
            grid=(blocks, width // tile),
            in_specs=in_specs,
            out_specs=pl.BlockSpec((1, depth, tile), lambda j, i, pick: (j, 0, i)),
        ),
        out_shape=jax.ShapeDtypeStruct((blocks, depth, width), dtype),
        compiler_params=params(),
        cost_estimate=cost(2 * n * rows * depth * width, 2 * n * rows * (depth + width)),
    )(pick, *args)


def shards(seq, ch, queries, keys, values, filters, grad_out, out_weight):
    inner = seq // LINE
    rows, width = queries.shape
    depth = out_weight.shape[0]
    chunks = 2 if width % (2 * LANES) == 0 else 1
    cols = width // chunks
    place = lax.axis_index("seq")
    z, y = place // inner, place % inner

    def send(x, pairs):
        return lax.ppermute(x, "seq", pairs)

    def along_line(x, pairs):
        return send(x, [(a * inner + i, b * inner + i) for a, b in pairs for i in range(inner)])

    def around_inner(x, shift):
        return send(
            x, [(a * inner + i, a * inner + (i + shift) % inner) for a in range(LINE) for i in range(inner)]
        )

    each = range(chunks)
    up_pairs, down_pairs = [(0, 1), (1, 2), (2, 3)], [(1, 0), (2, 1), (3, 2)]

    def second_step(h):
        return along_line(up1[h], [(1, 2), (2, 3)]), along_line(down1[h], [(2, 1), (1, 0)])

    def third_step(x):
        return along_line(x, [(2, 3), (1, 0)])

    def merge(pair):
        return jnp.where(z >= 2, *pair)

    pick = jnp.stack(
        [
            z,
            jnp.where(z == 0, 1, z - 1),
            jnp.where(z >= 2, z - 2, z + 2),
            jnp.where(z == 3, 0, jnp.where(z == 1, 2, 3)),
            jnp.where(z == 0, 1, 0),
            jnp.where((z == 0) | (z == 3), 1, 0),
        ]
    ).astype(jnp.int32)

    def weights(h):
        return [halves[h], up1[h], down1[h], second[h], third[h]]

    def swap_gated(h):
        return [around_inner(gateds[h], r) for r in range(1, inner)]

    even = z % 2 == 0
    first_pick = jnp.where(even, 3, 0).astype(jnp.int32).reshape(1)
    rest_pick = jnp.stack(
        [
            jnp.where(z == 0, 2, jnp.where(z == 1, 3, jnp.where(z == 2, 0, 1))),
            jnp.where(even, 1, 2),
            z,
        ]
    ).astype(jnp.int32)

    def rows_own(h):
        return weight_rows(jnp.concatenate([first_pick, rest_pick]), cots[:1], [gateds[h]], F32)

    def rows_first(h):
        return weight_rows(first_pick, cots[1:], got[h], BF16, base[h])[0]

    def rows_rest(h):
        return weight_rows(rest_pick, cots[1:], got[h], BF16, base[h], 1)

    def send_first(x):
        return along_line(x, [(0, 1), (3, 2)])

    def send_second(h, came):
        x = (rest[h][0].astype(F32) + came.astype(F32)).astype(BF16)
        return along_line(x, [(0, 1), (3, 2)]), along_line(x, [(1, 2), (2, 1)])

    def send_third(h, outer_in, inner_in):
        mine, other = rest[h][1].astype(F32), first[h].astype(F32)
        outer_in, inner_in = outer_in.astype(F32), inner_in.astype(F32)
        up = jnp.where(z == 2, other, mine) + jnp.where(z == 1, outer_in, inner_in)
        down = jnp.where(z == 1, other, mine) + jnp.where(z == 1, inner_in, outer_in)
        return along_line(up.astype(BF16), up_pairs), along_line(down.astype(BF16), down_pairs)

    def last_sum(h):
        below, above = sums[h]
        return (rest[h][2].astype(F32) + below.astype(F32) + above.astype(F32)).astype(BF16)

    def shares(h):
        return [gate_grad(pick, cots[r], weights(h)) for r in range(1, inner)]

    def send_shares(parts):
        return [around_inner(part, inner - r) for r, part in enumerate(parts, 1)]

    up1, down1, gateds, mixeds, got = ([None] * chunks for _ in range(5))
    second, third, sums, parts, others, owns = ([None] * chunks for _ in range(6))
    first, rest = ([None] * chunks for _ in range(2))
    later_halves = list(each[1:])

    priors = []
    for h in each:
        tail = (slice(rows - FILT, rows), slice(h * cols, (h + 1) * cols))
        priors.append(product_of(keys[tail], values[tail]))
    cot_here = after(grad_out, *priors)
    next_pairs = [(i, i + 1) for i in range(seq - 1)]
    priors[0] = send(priors[0], next_pairs)
    paired = inner == 2 and ch == LINE
    other = cot_here
    cots = []
    if paired:
        kept = lax.dynamic_slice(cot_here, (0, y * depth), (rows, depth))
        other = lax.dynamic_slice(cot_here, (0, (1 - y) * depth), (rows, depth))
        cots = [lax.all_gather(kept, "ch", axis=0, tiled=False)]
    back, ahead = tables(filters)
    halves = [out_weight[:, h * cols : (h + 1) * cols] for h in each]
    priors, other, halves, back = fence(priors, other, halves, back)
    for h in later_halves:
        priors[h] = send(priors[h], next_pairs)

    up1[0], down1[0] = along_line(halves[0], up_pairs), along_line(halves[0], down_pairs)
    swapped = around_inner(other, 1) if paired else other
    gateds[0], mixeds[0] = forward(queries, keys, values, priors[0], back, 0, chunks)
    up1[0], down1[0], swapped, gateds, cots, priors = fence(
        up1[0], down1[0], swapped, gateds, cots, priors
    )

    for h in later_halves:
        up1[h], down1[h] = along_line(halves[h], up_pairs), along_line(halves[h], down_pairs)
    second[0] = second_step(0)
    if paired:
        cots.append(lax.all_gather(swapped, "ch", axis=0, tiled=False))
    else:
        full = lax.all_gather(swapped, "ch", axis=1, tiled=True)
        full = full.reshape(rows, LINE, inner, depth).transpose(2, 1, 0, 3)
        for shift in range(inner):
            part = lax.dynamic_index_in_dim(full, (y + shift) % inner, 0, keepdims=False)
            cots.append(part if shift == 0 else around_inner(part, shift))
    got[0] = swap_gated(0)
    for h in later_halves:
        gateds[h], mixeds[h] = forward(queries, keys, values, priors[h], back, h, chunks)
    up1, down1, gateds, cots[0] = fence(up1, down1, gateds, cots[0])

    for h in later_halves:
        second[h] = second_step(h)
    base = [rows_own(h) for h in each]
    second[0], got[0], gateds, cots, base = fence(second[0], got[0], gateds, cots, base)

    second[0] = merge(second[0])
    third[0] = third_step(second[0])
    for h in later_halves:
        got[h] = swap_gated(h)
    first[0] = rows_first(0)
    sums[0] = send_first(first[0])
    rest[0] = rows_rest(0)
    second, rest[0] = fence(second, rest[0])

    for h in later_halves:
        second[h] = merge(second[h])
        third[h] = third_step(second[h])
    sums[0] = send_second(0, sums[0])
    third[0], second = fence(third[0], second)

    parts[0] = shares(0)
    parts[0], got[1:] = fence(parts[0], got[1:])
    others[0] = send_shares(parts[0])

    for h in later_halves:
        first[h] = rows_first(h)
        sums[h] = send_first(first[h])
    sums[0] = send_third(0, *sums[0])
    for h in later_halves:
        rest[h] = rows_rest(h)
    third, rest[1:] = fence(third, rest[1:])

    for h in later_halves:
        parts[h] = shares(h)
    parts[1:], sums = fence(parts[1:], sums)
    for h in later_halves:
        others[h] = send_shares(parts[h])
        sums[h] = send_second(h, sums[h])
    owns = [gate_grad(pick, cots[0], weights(h)) for h in each]
    others[0], owns = fence(others[0], owns)

    grad_queries = None
    grad_kv = None
    taps, gms, laters = ([None] * chunks for _ in range(3))
    for h in each:
        grad_queries, gms[h], edge, taps[h] = middle(
            owns[h], others[h], queries, keys, values, mixeds[h], priors[h], grad_queries, h, chunks
        )
        laters[h] = send(edge, [(i + 1, i) for i in range(seq - 1)])
        if h == 0:
            for g in later_halves:
                sums[g] = send_third(g, *after(sums[g], edge))
            done = [last_sum(0)]
            others, owns, done = fence(others, owns, done)
    for h in later_halves:
        sums[h], gms[0], _ = fence(sums[h], gms[0], edge)
        done.append(last_sum(h))
    for h in each:
        grad_kv = backward(gms[h], laters[h], keys, values, ahead, grad_kv, h, chunks)
    grad_weight = jnp.concatenate(done, axis=1)
    taps = jnp.concatenate(taps, axis=0)[:, 1 : FILT + 1][:, ::-1]
    taps = taps.T.reshape(seq, FILT // seq, -1)
    taps = jnp.sum(lax.all_to_all(taps, "seq", 0, 0), axis=0)
    return grad_queries, *grad_kv, taps.T, grad_weight


def solution(mesh):
    sizes = dict(mesh.shape)
    return jax.shard_map(
        functools.partial(shards, sizes["seq"], sizes["ch"]),
        mesh=mesh,
        in_specs=(
            P("seq", "ch"),
            P("seq", "ch"),
            P("seq", "ch"),
            P("ch", None),
            P("seq", "ch"),
            P("seq", "ch"),
        ),
        out_specs=(P("seq", "ch"), P("seq", "ch"), P("seq", "ch"), P("ch", "seq"), P("seq", "ch")),
        check_vma=False,
    )
```

```python
import functools

import jax
import jax.numpy as jnp
from jax import lax
from jax.experimental import pallas as pl
from jax.experimental.pallas import tpu as pltpu
from jax.sharding import PartitionSpec as P

GROUP = 16
FILT = 128
LANES = 128
GPT = LANES // GROUP
LINE = 4
F32 = jnp.float32
BF16 = jnp.bfloat16
VMEM_LIMIT = 48 * 1024 * 1024


def params():
    return pltpu.CompilerParams(vmem_limit_bytes=VMEM_LIMIT)


def cost(flops, nbytes):
    return pl.CostEstimate(flops=int(flops) // 64, bytes_accessed=int(nbytes) // 64, transcendentals=0)


def fence(*arrays):
    return lax.optimization_barrier(arrays)


def after(x, *others):
    return lax.optimization_barrier((x, *others))[0]


def table_kernel(back_ref, ahead_ref, back_out, ahead_out):
    for seed, out in ((back_ref, back_out), (ahead_ref, ahead_out)):
        for g in range(GPT):
            rows = jnp.broadcast_to(seed[g : g + 1, :], (FILT, 2 * FILT))
            turned = pltpu.roll(rows, 0, 1, stride=1, stride_axis=0)
            out[g * FILT : (g + 1) * FILT, :] = turned.astype(BF16)


def tables(filters):
    groups = filters.shape[0]
    taps = filters.astype(F32)
    back = jnp.concatenate(
        [jnp.zeros((groups, 1), F32), taps[:, ::-1], jnp.zeros((groups, FILT - 1), F32)], axis=1
    )
    ahead = jnp.concatenate([taps, jnp.zeros((groups, FILT), F32)], axis=1)
    seed = pl.BlockSpec((GPT, 2 * FILT), lambda i: (i, 0))
    full = pl.BlockSpec((GPT * FILT, 2 * FILT), lambda i: (i, 0))
    shape = jax.ShapeDtypeStruct((groups * FILT, 2 * FILT), BF16)
    return pl.pallas_call(
        table_kernel,
        grid=(groups // GPT,),
        in_specs=[seed, seed],
        out_specs=[full, full],
        out_shape=[shape, shape],
        compiler_params=params(),
        cost_estimate=cost(groups * 2**18, groups * 2**17),
    )(back, ahead)


def group_of_lane(rows, cols):
    return (lax.broadcasted_iota(jnp.int32, (rows, cols), 1) % LANES) // GROUP


def windows(ext, b):
    lo = b * FILT
    return jnp.concatenate([ext[lo : lo + 2 * FILT], ext[lo + FILT : lo + 3 * FILT]], axis=1)


def toeplitz(table, ext, blocks):
    group = group_of_lane(FILT, 2 * LANES)
    rows = []
    for b in range(0, blocks, 2):
        out = jnp.dot(table, windows(ext, b), preferred_element_type=F32)
        picked = out[:FILT]
        for g in range(1, GPT):
            picked = jnp.where(group == g, out[g * FILT : (g + 1) * FILT], picked)
        rows += [picked[:, :LANES], picked[:, LANES:]]
    return jnp.concatenate(rows, axis=0)


def product_of(k, v):
    return (k.astype(F32) * v.astype(F32)).astype(BF16)


def forward_kernel(q, k, v, prior, table, gated, mixed_out):
    blocks = q.shape[0] // FILT
    ext = jnp.concatenate([prior[...], product_of(k[...], v[...])], axis=0)
    mixed = toeplitz(table[...], ext, blocks)
    mixed_out[...] = mixed.astype(BF16)
    gated[...] = (q[...].astype(F32) * mixed).astype(BF16)


def forward(q, k, v, prior, table, chunk, chunks):
    rows, width = q.shape
    tiles = width // LANES // chunks
    here = pl.BlockSpec((rows, LANES), lambda i: (0, chunk * tiles + i))
    out = pl.BlockSpec((rows, LANES), lambda i: (0, i))
    shape = jax.ShapeDtypeStruct((rows, width // chunks), BF16)
    return pl.pallas_call(
        forward_kernel,
        grid=(tiles,),
        in_specs=[
            here,
            here,
            here,
            pl.BlockSpec((FILT, LANES), lambda i: (0, chunk * tiles + i)),
            pl.BlockSpec((GPT * FILT, 2 * FILT), lambda i: (chunk * tiles + i, 0)),
        ],
        out_specs=[out, out],
        out_shape=[shape, shape],
        compiler_params=params(),
        cost_estimate=cost(tiles * rows * 2 * 2**18, tiles * rows * 5 * 256 + tiles * 2**19),
    )(q, k, v, prior, table)


def middle_kernel(own, others, q, k, v, mixed, prior, *rest):
    gq_out, gm_out, edge_out, taps_out = rest[-4:]
    blocks = q.shape[0] // FILT
    total = own[...].astype(F32)
    for other in others:
        total = total + other[...].astype(F32)
    gg = total.astype(BF16).astype(F32)
    gq_out[...] = (gg * mixed[...].astype(F32)).astype(BF16)
    gm = (gg * q[...].astype(F32)).astype(BF16)
    gm_out[...] = gm
    edge_out[...] = gm[:FILT]
    ext = jnp.concatenate([prior[...], product_of(k[...], v[...])], axis=0)
    wide = jnp.concatenate([gm[b * FILT : (b + 1) * FILT] for b in range(blocks)], axis=1)
    group = group_of_lane(FILT, blocks * LANES)
    stack = jnp.concatenate(
        [jnp.where(group == g, wide, jnp.zeros_like(wide)) for g in range(GPT)], axis=0
    )
    near = jnp.concatenate([ext[b * FILT : (b + 2) * FILT] for b in range(blocks)], axis=1)
    lag = lax.dot_general(stack, near, (((1,), (1,)), ((), ())), preferred_element_type=F32)
    lag = lag.reshape(GPT, FILT, 2 * FILT)
    half = FILT // 2
    while half >= 8:
        lag = lag[:, :half] + pltpu.roll(lag[:, half:], 2 * FILT - half, 2)
        half //= 2
    while half >= 1:
        lag = lag + pltpu.roll(pltpu.roll(lag, 2 * FILT - half, 2), 8 - half, 1)
        half //= 2
    taps_out[...] = lag[:, 0, :]


def middle(own, others, q, k, v, mixed, prior, filled, chunk, chunks):
    rows, width = q.shape
    tiles = width // LANES // chunks
    groups = width // GROUP // chunks
    here = pl.BlockSpec((rows, LANES), lambda i: (0, chunk * tiles + i))
    part = pl.BlockSpec((rows, LANES), lambda i: (0, i))
    edge = pl.BlockSpec((FILT, LANES), lambda i: (0, i))
    n_other = len(others)

    def kernel(own_ref, *refs):
        middle_kernel(own_ref, refs[:n_other], *refs[n_other:])

    args = [own, *others, q, k, v, mixed, prior]
    in_specs = [part] * (1 + n_other) + [here] * 3 + [part]
    in_specs.append(pl.BlockSpec((FILT, LANES), lambda i: (0, chunk * tiles + i)))
    aliases = {}
    if filled is not None:
        aliases = {len(args): 0}
        args.append(filled)
        in_specs.append(pl.BlockSpec(memory_space=pl.ANY))
    return pl.pallas_call(
        kernel,
        grid=(tiles,),
        in_specs=in_specs,
        out_specs=[here, part, edge, pl.BlockSpec((GPT, 2 * FILT), lambda i: (i, 0))],
        out_shape=[
            jax.ShapeDtypeStruct((rows, width), BF16),
            jax.ShapeDtypeStruct((rows, width // chunks), BF16),
            jax.ShapeDtypeStruct((FILT, width // chunks), BF16),
            jax.ShapeDtypeStruct((groups, 2 * FILT), F32),
        ],
        input_output_aliases=aliases,
        compiler_params=params(),
        cost_estimate=cost(tiles * rows * 2 * 2**18, tiles * rows * 9 * 256),
    )(*args)


def backward_kernel(gm, later, k, v, table, *rest):
    gk_out, gv_out = rest[-2:]
    blocks = gm.shape[0] // FILT
    ext = jnp.concatenate([gm[...], later[...]], axis=0)
    gp = toeplitz(table[...], ext, blocks)
    gk_out[...] = (gp * v[...].astype(F32)).astype(BF16)
    gv_out[...] = (gp * k[...].astype(F32)).astype(BF16)


def backward(gm, later, k, v, table, filled, chunk, chunks):
    rows, width = k.shape
    tiles = width // LANES // chunks
    here = pl.BlockSpec((rows, LANES), lambda i: (0, chunk * tiles + i))
    part = pl.BlockSpec((rows, LANES), lambda i: (0, i))
    args = [gm, later, k, v, table]
    in_specs = [
        part,
        pl.BlockSpec((FILT, LANES), lambda i: (0, i)),
        here,
        here,
        pl.BlockSpec((GPT * FILT, 2 * FILT), lambda i: (chunk * tiles + i, 0)),
    ]
    aliases = {}
    if filled is not None:
        aliases = {len(args): 0, len(args) + 1: 1}
        args += filled
        in_specs += [pl.BlockSpec(memory_space=pl.ANY)] * 2
    shape = jax.ShapeDtypeStruct((rows, width), BF16)
    return pl.pallas_call(
        backward_kernel,
        grid=(tiles,),
        in_specs=in_specs,
        out_specs=[here, here],
        out_shape=[shape, shape],
        input_output_aliases=aliases,
        compiler_params=params(),
        cost_estimate=cost(tiles * rows * 2 * 2**18, tiles * rows * 5 * 256 + tiles * 2**19),
    )(*args)


def gate_kernel(pick, *refs):
    own, up, down, up2, down2, third, out = refs[LINE:]
    slots = (
        own[...],
        jnp.where(pick[LINE] == 1, down[...], up[...]),
        jnp.where(pick[LINE + 1] == 1, up2[...], down2[...]),
        jnp.where(pick[LINE + 2] == 1, third[...], down[...]),
    )
    cot = jnp.concatenate([ref[0] for ref in refs[:LINE]], axis=1)
    total = jnp.dot(cot, jnp.concatenate(slots, axis=0), preferred_element_type=F32)
    out[...] = total.astype(out.dtype)


def gate_grad(pick, cot, weights):
    _, rows, depth = cot.shape
    width = weights[0].shape[1]
    tile = min(256, width)

    def cot_spec(j):
        return pl.BlockSpec((1, rows, depth), lambda i, pick: (pick[j], 0, 0))

    return pl.pallas_call(
        gate_kernel,
        grid_spec=pltpu.PrefetchScalarGridSpec(
            num_scalar_prefetch=1,
            grid=(width // tile,),
            in_specs=[cot_spec(j) for j in range(LINE)]
            + [pl.BlockSpec((depth, tile), lambda i, pick: (0, i))] * len(weights),
            out_specs=pl.BlockSpec((rows, tile), lambda i, pick: (0, i)),
        ),
        out_shape=jax.ShapeDtypeStruct((rows, width), BF16),
        compiler_params=params(),
        cost_estimate=cost(
            2 * rows * LINE * depth * width, 2 * LINE * depth * (rows + width) + 2 * rows * width
        ),
    )(pick, *([cot] * LINE), *weights)


def rows_kernel(n, pick, *refs):
    out = refs[-1]
    cot, gated = refs[0][0], refs[n][...]
    if n > 1:
        cot = jnp.concatenate([ref[0] for ref in refs[:n]], axis=0)
        gated = jnp.concatenate([ref[...] for ref in refs[n : 2 * n]], axis=0)
    total = lax.dot_general(cot, gated, (((0,), (0,)), ((), ())), preferred_element_type=F32)
    if len(refs) > 2 * n + 1:
        total = total + refs[2 * n][0]
    out[0] = total.astype(out.dtype)


def weight_rows(pick, cots, gateds, dtype, base=None, skip=0):
    _, rows, depth = cots[0].shape
    width = gateds[0].shape[1]
    blocks = pick.shape[0]
    tile = width if blocks > 1 else min(512, width)
    n = len(cots)
    in_specs = [pl.BlockSpec((1, rows, depth), lambda j, i, pick: (pick[j], 0, 0))] * n
    in_specs += [pl.BlockSpec((rows, tile), lambda j, i, pick: (0, i))] * n
    args = [*cots, *gateds]
    if base is not None:
        in_specs.append(pl.BlockSpec((1, depth, tile), lambda j, i, pick: (j + skip, 0, i)))
        args.append(base)
    return pl.pallas_call(
        functools.partial(rows_kernel, n),
        grid_spec=pltpu.PrefetchScalarGridSpec(
            num_scalar_prefetch=1,
            grid=(blocks, width // tile),
            in_specs=in_specs,
            out_specs=pl.BlockSpec((1, depth, tile), lambda j, i, pick: (j, 0, i)),
        ),
        out_shape=jax.ShapeDtypeStruct((blocks, depth, width), dtype),
        compiler_params=params(),
        cost_estimate=cost(2 * n * rows * depth * width, 2 * n * rows * (depth + width)),
    )(pick, *args)


def packet_kernel(n, pick, *refs):
    base, up, down, first_out, packet_out = refs[2 * n :]
    cot, gated = refs[0][0], refs[n][...]
    if n > 1:
        cot = jnp.concatenate([ref[0] for ref in refs[:n]], axis=0)
        gated = jnp.concatenate([ref[...] for ref in refs[n : 2 * n]], axis=0)
    total = lax.dot_general(cot, gated, (((0,), (0,)), ((), ())), preferred_element_type=F32)
    rows = (total + base[0]).astype(BF16)
    first_out[...] = rows
    passed = jnp.where(pick[2] == 1, up[...], down[...])
    packet_out[...] = jnp.where(pick[1] == 1, rows, passed)


def packet_rows(pick, cots, gateds, base, up, down):
    _, rows, depth = cots[0].shape
    width = gateds[0].shape[1]
    tile = min(512, width)
    n = len(cots)
    part = pl.BlockSpec((depth, tile), lambda i, pick: (0, i))
    shape = jax.ShapeDtypeStruct((depth, width), BF16)
    return pl.pallas_call(
        functools.partial(packet_kernel, n),
        grid_spec=pltpu.PrefetchScalarGridSpec(
            num_scalar_prefetch=1,
            grid=(width // tile,),
            in_specs=[pl.BlockSpec((1, rows, depth), lambda i, pick: (pick[0], 0, 0))] * n
            + [pl.BlockSpec((rows, tile), lambda i, pick: (0, i))] * n
            + [pl.BlockSpec((1, depth, tile), lambda i, pick: (0, 0, i)), part, part],
            out_specs=[part, part],
        ),
        out_shape=[shape, shape],
        compiler_params=params(),
        cost_estimate=cost(2 * n * rows * depth * width, 2 * n * rows * (depth + width)),
    )(pick, *cots, *gateds, base, up, down)


def shards(seq, ch, queries, keys, values, filters, grad_out, out_weight):
    inner = seq // LINE
    rows, width = queries.shape
    depth = out_weight.shape[0]
    chunks = 2 if width % (2 * LANES) == 0 else 1
    cols = width // chunks
    place = lax.axis_index("seq")
    z, y = place // inner, place % inner

    def send(x, pairs):
        return lax.ppermute(x, "seq", pairs)

    def along_line(x, pairs):
        return send(x, [(a * inner + i, b * inner + i) for a, b in pairs for i in range(inner)])

    def around_inner(x, shift):
        return send(
            x, [(a * inner + i, a * inner + (i + shift) % inner) for a in range(LINE) for i in range(inner)]
        )

    each = range(chunks)
    up_pairs, down_pairs = [(0, 1), (1, 2), (2, 3)], [(1, 0), (2, 1), (3, 2)]

    def second_step(h):
        return along_line(up1[h], [(1, 2), (2, 3)]), along_line(down1[h], [(2, 1), (1, 0)])

    at_end = (z == 0) | (z == 3)
    pick = jnp.stack(
        [
            z,
            jnp.where(z == 0, 1, z - 1),
            jnp.where(z >= 2, z - 2, z + 2),
            jnp.where(z == 3, 0, jnp.where(z == 1, 2, 3)),
            z == 0,
            z >= 2,
            at_end,
        ]
    ).astype(jnp.int32)

    def weights(h):
        return [halves[h], up1[h], down1[h], *second[h], third[h]]

    def swap_gated(h):
        return [around_inner(gateds[h], r) for r in range(1, inner)]

    even = z % 2 == 0
    first_pick = jnp.where(even, 3, 0).astype(jnp.int32).reshape(1)
    rest_pick = jnp.stack(
        [
            jnp.where(z == 0, 2, jnp.where(z == 1, 3, jnp.where(z == 2, 0, 1))),
            jnp.where(even, 1, 2),
            z,
        ]
    ).astype(jnp.int32)

    def rows_own(h):
        return weight_rows(jnp.concatenate([first_pick, rest_pick]), cots[:1], [gateds[h]], F32)

    packet_pick = jnp.concatenate([first_pick, jnp.stack([at_end, z >= 2]).astype(jnp.int32)])

    def packet(h):
        return packet_rows(packet_pick, cots[1:], got[h], base[h], *second[h])

    def rows_rest(h):
        return weight_rows(rest_pick, cots[1:], got[h], BF16, base[h], 1)

    def send_packet(x):
        return along_line(x, [(0, 1), (3, 2), (2, 3), (1, 0)])

    def send_second(h, came):
        came = jnp.where(at_end, 0.0, came.astype(F32))
        x = (rest[h][0].astype(F32) + came).astype(BF16)
        return along_line(x, [(0, 1), (3, 2)]), along_line(x, [(1, 2), (2, 1)])

    def send_third(h, outer_in, inner_in):
        mine, other = rest[h][1].astype(F32), first[h].astype(F32)
        outer_in, inner_in = outer_in.astype(F32), inner_in.astype(F32)
        up = jnp.where(z == 2, other, mine) + jnp.where(z == 1, outer_in, inner_in)
        down = jnp.where(z == 1, other, mine) + jnp.where(z == 1, inner_in, outer_in)
        return along_line(up.astype(BF16), up_pairs), along_line(down.astype(BF16), down_pairs)

    def last_sum(h):
        below, above = sums[h]
        return (rest[h][2].astype(F32) + below.astype(F32) + above.astype(F32)).astype(BF16)

    def shares(h):
        return [gate_grad(pick, cots[r], weights(h)) for r in range(1, inner)]

    def send_shares(parts):
        return [around_inner(part, inner - r) for r, part in enumerate(parts, 1)]

    up1, down1, gateds, mixeds, got = ([None] * chunks for _ in range(5))
    second, third, sums, parts, others, owns = ([None] * chunks for _ in range(6))
    first, rest = ([None] * chunks for _ in range(2))
    later_halves = list(each[1:])

    prior = product_of(keys[rows - FILT :], values[rows - FILT :])
    cot_here = after(grad_out, prior)
    prior = send(prior, [(i, i + 1) for i in range(seq - 1)])
    paired = inner == 2 and ch == LINE
    other = cot_here
    cots = []
    if paired:
        kept = lax.dynamic_slice(cot_here, (0, y * depth), (rows, depth))
        other = lax.dynamic_slice(cot_here, (0, (1 - y) * depth), (rows, depth))
        cots = [lax.all_gather(kept, "ch", axis=0, tiled=False)]
    back, ahead = tables(filters)
    halves = [out_weight[:, h * cols : (h + 1) * cols] for h in each]
    prior, other, halves, back = fence(prior, other, halves, back)

    up1[0], down1[0] = along_line(halves[0], up_pairs), along_line(halves[0], down_pairs)
    swapped = around_inner(other, 1) if paired else other
    gateds[0], mixeds[0] = forward(queries, keys, values, prior, back, 0, chunks)
    up1[0], down1[0], swapped, gateds, cots = fence(up1[0], down1[0], swapped, gateds, cots)

    for h in later_halves:
        up1[h], down1[h] = along_line(halves[h], up_pairs), along_line(halves[h], down_pairs)
    second[0] = second_step(0)
    if paired:
        cots.append(lax.all_gather(swapped, "ch", axis=0, tiled=False))
    else:
        full = lax.all_gather(swapped, "ch", axis=1, tiled=True)
        full = full.reshape(rows, LINE, inner, depth).transpose(2, 1, 0, 3)
        for shift in range(inner):
            part = lax.dynamic_index_in_dim(full, (y + shift) % inner, 0, keepdims=False)
            cots.append(part if shift == 0 else around_inner(part, shift))
    got[0] = swap_gated(0)
    for h in later_halves:
        gateds[h], mixeds[h] = forward(queries, keys, values, prior, back, h, chunks)
    up1, down1, gateds, cots[0] = fence(up1, down1, gateds, cots[0])

    for h in later_halves:
        second[h] = second_step(h)
    base = [None] * chunks
    base[0] = rows_own(0)
    second[0], got[0], gateds, cots, base = fence(second[0], got[0], gateds, cots, base)

    first[0], parcel = packet(0)
    third[0] = send_packet(parcel)
    for h in later_halves:
        got[h] = swap_gated(h)
    rest[0] = rows_rest(0)
    second, rest[0], gateds = fence(second, rest[0], gateds)
    for h in later_halves:
        base[h] = rows_own(h)
    third[0], second, base = fence(third[0], second, base)

    sums[0] = send_second(0, third[0])

    parts[0] = shares(0)
    parts[0], got[1:] = fence(parts[0], got[1:])
    others[0] = send_shares(parts[0])

    for h in later_halves:
        first[h], parcel = packet(h)
        third[h] = send_packet(parcel)
    sums[0] = send_third(0, *sums[0])
    for h in later_halves:
        rest[h] = rows_rest(h)
    third, rest[1:] = fence(third, rest[1:])

    for h in later_halves:
        parts[h] = shares(h)
    parts[1:], sums = fence(parts[1:], sums)
    for h in later_halves:
        others[h] = send_shares(parts[h])
        sums[h] = send_second(h, third[h])
    owns = [gate_grad(pick, cots[0], weights(h)) for h in each]
    others[0], owns = fence(others[0], owns)

    grad_queries = None
    grad_kv = None
    taps, gms, laters = ([None] * chunks for _ in range(3))
    for h in each:
        grad_queries, gms[h], edge, taps[h] = middle(
            owns[h], others[h], queries, keys, values, mixeds[h], prior, grad_queries, h, chunks
        )
        laters[h] = send(edge, [(i + 1, i) for i in range(seq - 1)])
        if h == 0:
            for g in later_halves:
                sums[g] = send_third(g, *after(sums[g], edge))
            done = [last_sum(0)]
            others, owns, done = fence(others, owns, done)
    for h in later_halves:
        sums[h], gms[0], _ = fence(sums[h], gms[0], edge)
        done.append(last_sum(h))
    for h in each:
        grad_kv = backward(gms[h], laters[h], keys, values, ahead, grad_kv, h, chunks)
    grad_weight = jnp.concatenate(done, axis=1)
    taps = jnp.concatenate(taps, axis=0)[:, 1 : FILT + 1][:, ::-1]
    taps = taps.T.reshape(seq, FILT // seq, -1)
    taps = jnp.sum(lax.all_to_all(taps, "seq", 0, 0), axis=0)
    return grad_queries, *grad_kv, taps.T, grad_weight


def solution(mesh):
    sizes = dict(mesh.shape)
    return jax.shard_map(
        functools.partial(shards, sizes["seq"], sizes["ch"]),
        mesh=mesh,
        in_specs=(
            P("seq", "ch"),
            P("seq", "ch"),
            P("seq", "ch"),
            P("ch", None),
            P("seq", "ch"),
            P("seq", "ch"),
        ),
        out_specs=(P("seq", "ch"), P("seq", "ch"), P("seq", "ch"), P("ch", "seq"), P("seq", "ch")),
        check_vma=False,
    )
```

```python
import functools

import jax
import jax.numpy as jnp
from jax import lax
from jax.experimental import pallas as pl
from jax.experimental.pallas import tpu as pltpu
from jax.sharding import PartitionSpec as P

GROUP = 16
FILT = 128
LANES = 128
GPT = LANES // GROUP
LINE = 4
F32 = jnp.float32
BF16 = jnp.bfloat16
VMEM_LIMIT = 48 * 1024 * 1024


def params():
    return pltpu.CompilerParams(vmem_limit_bytes=VMEM_LIMIT)


def cost(flops, nbytes):
    return pl.CostEstimate(flops=int(flops) // 64, bytes_accessed=int(nbytes) // 64, transcendentals=0)


def fence(*arrays):
    return lax.optimization_barrier(arrays)


def after(x, *others):
    return lax.optimization_barrier((x, *others))[0]


def table_kernel(back_ref, ahead_ref, back_out, ahead_out):
    for seed, out in ((back_ref, back_out), (ahead_ref, ahead_out)):
        for g in range(GPT):
            rows = jnp.broadcast_to(seed[g : g + 1, :], (FILT, 2 * FILT))
            turned = pltpu.roll(rows, 0, 1, stride=1, stride_axis=0)
            out[g * FILT : (g + 1) * FILT, :] = turned.astype(BF16)


def tables(filters):
    groups = filters.shape[0]
    taps = filters.astype(F32)
    back = jnp.concatenate(
        [jnp.zeros((groups, 1), F32), taps[:, ::-1], jnp.zeros((groups, FILT - 1), F32)], axis=1
    )
    ahead = jnp.concatenate([taps, jnp.zeros((groups, FILT), F32)], axis=1)
    seed = pl.BlockSpec((GPT, 2 * FILT), lambda i: (i, 0))
    full = pl.BlockSpec((GPT * FILT, 2 * FILT), lambda i: (i, 0))
    shape = jax.ShapeDtypeStruct((groups * FILT, 2 * FILT), BF16)
    return pl.pallas_call(
        table_kernel,
        grid=(groups // GPT,),
        in_specs=[seed, seed],
        out_specs=[full, full],
        out_shape=[shape, shape],
        compiler_params=params(),
        cost_estimate=cost(groups * 2**18, groups * 2**17),
    )(back, ahead)


def group_of_lane(rows, cols):
    return (lax.broadcasted_iota(jnp.int32, (rows, cols), 1) % LANES) // GROUP


def windows(ext, b):
    lo = b * FILT
    return jnp.concatenate([ext[lo : lo + 2 * FILT], ext[lo + FILT : lo + 3 * FILT]], axis=1)


def toeplitz(table, ext, blocks):
    group = group_of_lane(FILT, 2 * LANES)
    rows = []
    for b in range(0, blocks, 2):
        out = jnp.dot(table, windows(ext, b), preferred_element_type=F32)
        picked = out[:FILT]
        for g in range(1, GPT):
            picked = jnp.where(group == g, out[g * FILT : (g + 1) * FILT], picked)
        rows += [picked[:, :LANES], picked[:, LANES:]]
    return jnp.concatenate(rows, axis=0)


def product_of(k, v):
    return (k.astype(F32) * v.astype(F32)).astype(BF16)


def forward_kernel(q, k, v, prior, table, gated, mixed_out):
    blocks = q.shape[0] // FILT
    ext = jnp.concatenate([prior[...], product_of(k[...], v[...])], axis=0)
    mixed = toeplitz(table[...], ext, blocks)
    mixed_out[...] = mixed.astype(BF16)
    gated[...] = (q[...].astype(F32) * mixed).astype(BF16)


def forward(q, k, v, prior, table, chunk, chunks):
    rows, width = q.shape
    tiles = width // LANES // chunks
    here = pl.BlockSpec((rows, LANES), lambda i: (0, chunk * tiles + i))
    out = pl.BlockSpec((rows, LANES), lambda i: (0, i))
    shape = jax.ShapeDtypeStruct((rows, width // chunks), BF16)
    return pl.pallas_call(
        forward_kernel,
        grid=(tiles,),
        in_specs=[
            here,
            here,
            here,
            pl.BlockSpec((FILT, LANES), lambda i: (0, chunk * tiles + i)),
            pl.BlockSpec((GPT * FILT, 2 * FILT), lambda i: (chunk * tiles + i, 0)),
        ],
        out_specs=[out, out],
        out_shape=[shape, shape],
        compiler_params=params(),
        cost_estimate=cost(tiles * rows * 2 * 2**18, tiles * rows * 5 * 256 + tiles * 2**19),
    )(q, k, v, prior, table)


def middle_kernel(own, others, q, k, v, mixed, prior, *rest):
    gq_out, gm_out, edge_out, taps_out = rest[-4:]
    blocks = q.shape[0] // FILT
    total = own[...].astype(F32)
    for other in others:
        total = total + other[...].astype(F32)
    gg = total.astype(BF16).astype(F32)
    gq_out[...] = (gg * mixed[...].astype(F32)).astype(BF16)
    gm = (gg * q[...].astype(F32)).astype(BF16)
    gm_out[...] = gm
    edge_out[...] = gm[:FILT]
    ext = jnp.concatenate([prior[...], product_of(k[...], v[...])], axis=0)
    wide = jnp.concatenate([gm[b * FILT : (b + 1) * FILT] for b in range(blocks)], axis=1)
    group = group_of_lane(FILT, blocks * LANES)
    stack = jnp.concatenate(
        [jnp.where(group == g, wide, jnp.zeros_like(wide)) for g in range(GPT)], axis=0
    )
    near = jnp.concatenate([ext[b * FILT : (b + 2) * FILT] for b in range(blocks)], axis=1)
    lag = lax.dot_general(stack, near, (((1,), (1,)), ((), ())), preferred_element_type=F32)
    lag = lag.reshape(GPT, FILT, 2 * FILT)
    half = FILT // 2
    while half >= 8:
        lag = lag[:, :half] + pltpu.roll(lag[:, half:], 2 * FILT - half, 2)
        half //= 2
    while half >= 1:
        lag = lag + pltpu.roll(pltpu.roll(lag, 2 * FILT - half, 2), 8 - half, 1)
        half //= 2
    taps_out[...] = lag[:, 0, :]


def middle(own, others, q, k, v, mixed, prior, filled, chunk, chunks):
    rows, width = q.shape
    tiles = width // LANES // chunks
    groups = width // GROUP // chunks
    here = pl.BlockSpec((rows, LANES), lambda i: (0, chunk * tiles + i))
    part = pl.BlockSpec((rows, LANES), lambda i: (0, i))
    edge = pl.BlockSpec((FILT, LANES), lambda i: (0, i))
    n_other = len(others)

    def kernel(own_ref, *refs):
        middle_kernel(own_ref, refs[:n_other], *refs[n_other:])

    args = [own, *others, q, k, v, mixed, prior]
    in_specs = [part] * (1 + n_other) + [here] * 3 + [part]
    in_specs.append(pl.BlockSpec((FILT, LANES), lambda i: (0, chunk * tiles + i)))
    aliases = {}
    if filled is not None:
        aliases = {len(args): 0}
        args.append(filled)
        in_specs.append(pl.BlockSpec(memory_space=pl.ANY))
    return pl.pallas_call(
        kernel,
        grid=(tiles,),
        in_specs=in_specs,
        out_specs=[here, part, edge, pl.BlockSpec((GPT, 2 * FILT), lambda i: (i, 0))],
        out_shape=[
            jax.ShapeDtypeStruct((rows, width), BF16),
            jax.ShapeDtypeStruct((rows, width // chunks), BF16),
            jax.ShapeDtypeStruct((FILT, width // chunks), BF16),
            jax.ShapeDtypeStruct((groups, 2 * FILT), F32),
        ],
        input_output_aliases=aliases,
        compiler_params=params(),
        cost_estimate=cost(tiles * rows * 2 * 2**18, tiles * rows * 9 * 256),
    )(*args)


def backward_kernel(gm, later, k, v, table, *rest):
    gk_out, gv_out = rest[-2:]
    blocks = gm.shape[0] // FILT
    ext = jnp.concatenate([gm[...], later[...]], axis=0)
    gp = toeplitz(table[...], ext, blocks)
    gk_out[...] = (gp * v[...].astype(F32)).astype(BF16)
    gv_out[...] = (gp * k[...].astype(F32)).astype(BF16)


def backward(gm, later, k, v, table, filled, chunk, chunks):
    rows, width = k.shape
    tiles = width // LANES // chunks
    here = pl.BlockSpec((rows, LANES), lambda i: (0, chunk * tiles + i))
    part = pl.BlockSpec((rows, LANES), lambda i: (0, i))
    args = [gm, later, k, v, table]
    in_specs = [
        part,
        pl.BlockSpec((FILT, LANES), lambda i: (0, i)),
        here,
        here,
        pl.BlockSpec((GPT * FILT, 2 * FILT), lambda i: (chunk * tiles + i, 0)),
    ]
    aliases = {}
    if filled is not None:
        aliases = {len(args): 0, len(args) + 1: 1}
        args += filled
        in_specs += [pl.BlockSpec(memory_space=pl.ANY)] * 2
    shape = jax.ShapeDtypeStruct((rows, width), BF16)
    return pl.pallas_call(
        backward_kernel,
        grid=(tiles,),
        in_specs=in_specs,
        out_specs=[here, here],
        out_shape=[shape, shape],
        input_output_aliases=aliases,
        compiler_params=params(),
        cost_estimate=cost(tiles * rows * 2 * 2**18, tiles * rows * 5 * 256 + tiles * 2**19),
    )(*args)


def gate_kernel(slots, pick, *refs):
    out = refs[-1]
    cots, refs = refs[: len(slots)], list(refs[len(slots) : -1])
    blocks = []
    for slot in slots:
        block = refs.pop(0)[...]
        if slot:
            block = jnp.where(pick[LINE + slot - 1] == 1, block, refs.pop(0)[...])
        blocks.append(block)
    cot, block = cots[0][0], blocks[0]
    if len(slots) > 1:
        cot = jnp.concatenate([ref[0] for ref in cots], axis=1)
        block = jnp.concatenate(blocks, axis=0)
    total = jnp.dot(cot, block, preferred_element_type=F32)
    if refs:
        total = total + refs[0][...].astype(F32)
    out[...] = total.astype(out.dtype)


def gate_grad(pick, cot, weights, slots=(0, 1, 2, 3), base=None):
    _, rows, depth = cot.shape
    width = weights[0][0].shape[1]
    tile = min(256, width)

    def cot_spec(j):
        return pl.BlockSpec((1, rows, depth), lambda i, pick: (pick[j], 0, 0))

    blocks = [x for slot in slots for x in weights[slot]]
    part = pl.BlockSpec((rows, tile), lambda i, pick: (0, i))
    in_specs = [cot_spec(j) for j in slots]
    in_specs += [pl.BlockSpec((depth, tile), lambda i, pick: (0, i))] * len(blocks)
    args = [cot] * len(slots) + blocks
    if base is not None:
        in_specs.append(part)
        args.append(base)
    return pl.pallas_call(
        functools.partial(gate_kernel, slots),
        grid_spec=pltpu.PrefetchScalarGridSpec(
            num_scalar_prefetch=1,
            grid=(width // tile,),
            in_specs=in_specs,
            out_specs=part,
        ),
        out_shape=jax.ShapeDtypeStruct((rows, width), BF16),
        compiler_params=params(),
        cost_estimate=cost(
            2 * rows * len(slots) * depth * width, 2 * len(slots) * depth * (rows + width)
        ),
    )(pick, *args)


def rows_kernel(n, pick, *refs):
    out = refs[-1]
    cot, gated = refs[0][0], refs[n][...]
    if n > 1:
        cot = jnp.concatenate([ref[0] for ref in refs[:n]], axis=0)
        gated = jnp.concatenate([ref[...] for ref in refs[n : 2 * n]], axis=0)
    total = lax.dot_general(cot, gated, (((0,), (0,)), ((), ())), preferred_element_type=F32)
    if len(refs) > 2 * n + 1:
        total = total + refs[2 * n][0]
    out[0] = total.astype(out.dtype)


def weight_rows(pick, cots, gateds, dtype, base=None, skip=0):
    _, rows, depth = cots[0].shape
    width = gateds[0].shape[1]
    blocks = pick.shape[0]
    tile = width if blocks > 1 else min(512, width)
    n = len(cots)
    in_specs = [pl.BlockSpec((1, rows, depth), lambda j, i, pick: (pick[j], 0, 0))] * n
    in_specs += [pl.BlockSpec((rows, tile), lambda j, i, pick: (0, i))] * n
    args = [*cots, *gateds]
    if base is not None:
        in_specs.append(pl.BlockSpec((1, depth, tile), lambda j, i, pick: (j + skip, 0, i)))
        args.append(base)
    return pl.pallas_call(
        functools.partial(rows_kernel, n),
        grid_spec=pltpu.PrefetchScalarGridSpec(
            num_scalar_prefetch=1,
            grid=(blocks, width // tile),
            in_specs=in_specs,
            out_specs=pl.BlockSpec((1, depth, tile), lambda j, i, pick: (j, 0, i)),
        ),
        out_shape=jax.ShapeDtypeStruct((blocks, depth, width), dtype),
        compiler_params=params(),
        cost_estimate=cost(2 * n * rows * depth * width, 2 * n * rows * (depth + width)),
    )(pick, *args)


def packet_kernel(n, pick, *refs):
    base, up, down, first_out, packet_out = refs[2 * n :]
    cot, gated = refs[0][0], refs[n][...]
    if n > 1:
        cot = jnp.concatenate([ref[0] for ref in refs[:n]], axis=0)
        gated = jnp.concatenate([ref[...] for ref in refs[n : 2 * n]], axis=0)
    total = lax.dot_general(cot, gated, (((0,), (0,)), ((), ())), preferred_element_type=F32)
    rows = (total + base[0]).astype(BF16)
    first_out[...] = rows
    passed = jnp.where(pick[2] == 1, up[...], down[...])
    packet_out[...] = jnp.where(pick[1] == 1, rows, passed)


def packet_rows(pick, cots, gateds, base, up, down):
    _, rows, depth = cots[0].shape
    width = gateds[0].shape[1]
    tile = min(512, width)
    n = len(cots)
    part = pl.BlockSpec((depth, tile), lambda i, pick: (0, i))
    shape = jax.ShapeDtypeStruct((depth, width), BF16)
    return pl.pallas_call(
        functools.partial(packet_kernel, n),
        grid_spec=pltpu.PrefetchScalarGridSpec(
            num_scalar_prefetch=1,
            grid=(width // tile,),
            in_specs=[pl.BlockSpec((1, rows, depth), lambda i, pick: (pick[0], 0, 0))] * n
            + [pl.BlockSpec((rows, tile), lambda i, pick: (0, i))] * n
            + [pl.BlockSpec((1, depth, tile), lambda i, pick: (0, 0, i)), part, part],
            out_specs=[part, part],
        ),
        out_shape=[shape, shape],
        compiler_params=params(),
        cost_estimate=cost(2 * n * rows * depth * width, 2 * n * rows * (depth + width)),
    )(pick, *cots, *gateds, base, up, down)


def shards(seq, ch, queries, keys, values, filters, grad_out, out_weight):
    inner = seq // LINE
    rows, width = queries.shape
    depth = out_weight.shape[0]
    chunks = 2 if width % (2 * LANES) == 0 else 1
    cols = width // chunks
    place = lax.axis_index("seq")
    z, y = place // inner, place % inner

    def send(x, pairs):
        return lax.ppermute(x, "seq", pairs)

    def along_line(x, pairs):
        return send(x, [(a * inner + i, b * inner + i) for a, b in pairs for i in range(inner)])

    def around_inner(x, shift):
        return send(
            x, [(a * inner + i, a * inner + (i + shift) % inner) for a in range(LINE) for i in range(inner)]
        )

    each = range(chunks)
    up_pairs, down_pairs = [(0, 1), (1, 2), (2, 3)], [(1, 0), (2, 1), (3, 2)]

    def second_step(h):
        return along_line(up1[h], [(1, 2), (2, 3)]), along_line(down1[h], [(2, 1), (1, 0)])

    at_end = (z == 0) | (z == 3)
    pick = jnp.stack(
        [
            z,
            jnp.where(z == 0, 1, z - 1),
            jnp.where(z >= 2, z - 2, z + 2),
            jnp.where(z == 3, 0, jnp.where(z == 1, 2, 3)),
            z == 0,
            z >= 2,
            at_end,
        ]
    ).astype(jnp.int32)

    def weights(h):
        return [[halves[h]], [down1[h], up1[h]], second[h], [third[h], down1[h]]]

    def swap_gated(h):
        return [around_inner(gateds[h], r) for r in range(1, inner)]

    even = z % 2 == 0
    first_pick = jnp.where(even, 3, 0).astype(jnp.int32).reshape(1)
    rest_pick = jnp.stack(
        [
            jnp.where(z == 0, 2, jnp.where(z == 1, 3, jnp.where(z == 2, 0, 1))),
            jnp.where(even, 1, 2),
            z,
        ]
    ).astype(jnp.int32)

    def rows_own(h):
        return weight_rows(jnp.concatenate([first_pick, rest_pick]), cots[:1], [gateds[h]], F32)

    packet_pick = jnp.concatenate([first_pick, jnp.stack([at_end, z >= 2]).astype(jnp.int32)])

    def packet(h):
        return packet_rows(packet_pick, cots[1:], got[h], base[h], *second[h])

    def rows_rest(h):
        return weight_rows(rest_pick, cots[1:], got[h], BF16, base[h], 1)

    def send_packet(x):
        return along_line(x, [(0, 1), (3, 2), (2, 3), (1, 0)])

    def send_second(h, came):
        came = jnp.where(at_end, 0.0, came.astype(F32))
        x = (rest[h][0].astype(F32) + came).astype(BF16)
        return along_line(x, [(0, 1), (3, 2)]), along_line(x, [(1, 2), (2, 1)])

    def send_third(h, outer_in, inner_in):
        mine, other = rest[h][1].astype(F32), first[h].astype(F32)
        outer_in, inner_in = outer_in.astype(F32), inner_in.astype(F32)
        up = jnp.where(z == 2, other, mine) + jnp.where(z == 1, outer_in, inner_in)
        down = jnp.where(z == 1, other, mine) + jnp.where(z == 1, inner_in, outer_in)
        return along_line(up.astype(BF16), up_pairs), along_line(down.astype(BF16), down_pairs)

    def last_sum(h):
        below, above = sums[h]
        return (rest[h][2].astype(F32) + below.astype(F32) + above.astype(F32)).astype(BF16)

    def shares(h):
        return [gate_grad(pick, cots[r], weights(h)) for r in range(1, inner)]

    def send_shares(parts):
        return [around_inner(part, inner - r) for r, part in enumerate(parts, 1)]

    up1, down1, gateds, mixeds, got = ([None] * chunks for _ in range(5))
    second, third, sums, parts, others, owns = ([None] * chunks for _ in range(6))
    first, rest = ([None] * chunks for _ in range(2))
    later_halves = list(each[1:])

    prior = product_of(keys[rows - FILT :], values[rows - FILT :])
    cot_here = after(grad_out, prior)
    prior = send(prior, [(i, i + 1) for i in range(seq - 1)])
    paired = inner == 2 and ch == LINE
    other = cot_here
    cots = []
    if paired:
        kept = lax.dynamic_slice(cot_here, (0, y * depth), (rows, depth))
        other = lax.dynamic_slice(cot_here, (0, (1 - y) * depth), (rows, depth))
        cots = [lax.all_gather(kept, "ch", axis=0, tiled=False)]
    back, ahead = tables(filters)
    halves = [out_weight[:, h * cols : (h + 1) * cols] for h in each]
    prior, other, halves, back = fence(prior, other, halves, back)

    up1[0], down1[0] = along_line(halves[0], up_pairs), along_line(halves[0], down_pairs)
    swapped = around_inner(other, 1) if paired else other
    gateds[0], mixeds[0] = forward(queries, keys, values, prior, back, 0, chunks)
    up1[0], down1[0], swapped, gateds, cots = fence(up1[0], down1[0], swapped, gateds, cots)

    for h in later_halves:
        up1[h], down1[h] = along_line(halves[h], up_pairs), along_line(halves[h], down_pairs)
    second[0] = second_step(0)
    if paired:
        cots.append(lax.all_gather(swapped, "ch", axis=0, tiled=False))
    else:
        full = lax.all_gather(swapped, "ch", axis=1, tiled=True)
        full = full.reshape(rows, LINE, inner, depth).transpose(2, 1, 0, 3)
        for shift in range(inner):
            part = lax.dynamic_index_in_dim(full, (y + shift) % inner, 0, keepdims=False)
            cots.append(part if shift == 0 else around_inner(part, shift))
    got[0] = swap_gated(0)
    for h in later_halves:
        gateds[h], mixeds[h] = forward(queries, keys, values, prior, back, h, chunks)
    up1, down1, gateds, cots[0] = fence(up1, down1, gateds, cots[0])

    for h in later_halves:
        second[h] = second_step(h)
    base = [None] * chunks
    base[0] = rows_own(0)
    second[0], got[0], gateds, cots, base = fence(second[0], got[0], gateds, cots, base)

    first[0], parcel = packet(0)
    third[0] = send_packet(parcel)
    for h in later_halves:
        got[h] = swap_gated(h)
    rest[0] = rows_rest(0)
    begun = [gate_grad(pick, cot, weights(0), (0, 1, 2)) for cot in cots[1:]]
    second, rest[0], gateds, begun = fence(second, rest[0], gateds, begun)
    for h in later_halves:
        base[h] = rows_own(h)
    own_begun = gate_grad(pick, cots[0], weights(0), (0, 1, 2))
    third[0], second, base, own_begun = fence(third[0], second, base, own_begun)

    sums[0] = send_second(0, third[0])

    parts[0] = [
        gate_grad(pick, cot, weights(0), (3,), x) for cot, x in zip(cots[1:], begun)
    ]
    parts[0], got[1:], own_begun = fence(parts[0], got[1:], own_begun)
    others[0] = send_shares(parts[0])

    for h in later_halves:
        first[h], parcel = packet(h)
        third[h] = send_packet(parcel)
    sums[0] = send_third(0, *sums[0])
    for h in later_halves:
        rest[h] = rows_rest(h)
    owns[0] = gate_grad(pick, cots[0], weights(0), (3,), own_begun)
    third, rest[1:], owns[0] = fence(third, rest[1:], owns[0])

    for h in later_halves:
        parts[h] = shares(h)
    parts[1:], third = fence(parts[1:], third)
    for h in later_halves:
        others[h] = send_shares(parts[h])
        sums[h] = send_second(h, third[h])
    for h in later_halves:
        owns[h] = gate_grad(pick, cots[0], weights(h))
    others[0], owns = fence(others[0], owns)

    grad_queries = None
    grad_kv = None
    taps, gms, laters = ([None] * chunks for _ in range(3))
    for h in each:
        grad_queries, gms[h], edge, taps[h] = middle(
            owns[h], others[h], queries, keys, values, mixeds[h], prior, grad_queries, h, chunks
        )
        laters[h] = send(edge, [(i + 1, i) for i in range(seq - 1)])
        if h == 0:
            for g in later_halves:
                sums[g] = send_third(g, *after(sums[g], edge))
            done = [last_sum(0)]
            others, owns, done = fence(others, owns, done)
    for h in later_halves:
        sums[h], gms[0], _ = fence(sums[h], gms[0], edge)
        done.append(last_sum(h))
    for h in each:
        grad_kv = backward(gms[h], laters[h], keys, values, ahead, grad_kv, h, chunks)
    grad_weight = jnp.concatenate(done, axis=1)
    taps = jnp.concatenate(taps, axis=0)[:, 1 : FILT + 1][:, ::-1]
    taps = taps.T.reshape(seq, FILT // seq, -1)
    taps = jnp.sum(lax.all_to_all(taps, "seq", 0, 0), axis=0)
    return grad_queries, *grad_kv, taps.T, grad_weight


def solution(mesh):
    sizes = dict(mesh.shape)
    return jax.shard_map(
        functools.partial(shards, sizes["seq"], sizes["ch"]),
        mesh=mesh,
        in_specs=(
            P("seq", "ch"),
            P("seq", "ch"),
            P("seq", "ch"),
            P("ch", None),
            P("seq", "ch"),
            P("seq", "ch"),
        ),
        out_specs=(P("seq", "ch"), P("seq", "ch"), P("seq", "ch"), P("ch", "seq"), P("seq", "ch")),
        check_vma=False,
    )
```

```python
import functools

import jax
import jax.numpy as jnp
from jax import lax
from jax.experimental import pallas as pl
from jax.experimental.pallas import tpu as pltpu
from jax.sharding import PartitionSpec as P

GROUP = 16
FILT = 128
LANES = 128
GPT = LANES // GROUP
LINE = 4
F32 = jnp.float32
BF16 = jnp.bfloat16
VMEM_LIMIT = 48 * 1024 * 1024


def params():
    return pltpu.CompilerParams(vmem_limit_bytes=VMEM_LIMIT)


def cost(flops, nbytes):
    return pl.CostEstimate(flops=int(flops) // 64, bytes_accessed=int(nbytes) // 64, transcendentals=0)


def fence(*arrays):
    return lax.optimization_barrier(arrays)


def after(x, *others):
    return lax.optimization_barrier((x, *others))[0]


def table_kernel(back_ref, ahead_ref, back_out, ahead_out):
    for seed, out in ((back_ref, back_out), (ahead_ref, ahead_out)):
        for g in range(GPT):
            rows = jnp.broadcast_to(seed[g : g + 1, :], (FILT, 2 * FILT))
            turned = pltpu.roll(rows, 0, 1, stride=1, stride_axis=0)
            out[g * FILT : (g + 1) * FILT, :] = turned.astype(BF16)


def tables(filters):
    groups = filters.shape[0]
    taps = filters.astype(F32)
    back = jnp.concatenate(
        [jnp.zeros((groups, 1), F32), taps[:, ::-1], jnp.zeros((groups, FILT - 1), F32)], axis=1
    )
    ahead = jnp.concatenate([taps, jnp.zeros((groups, FILT), F32)], axis=1)
    seed = pl.BlockSpec((GPT, 2 * FILT), lambda i: (i, 0))
    full = pl.BlockSpec((GPT * FILT, 2 * FILT), lambda i: (i, 0))
    shape = jax.ShapeDtypeStruct((groups * FILT, 2 * FILT), BF16)
    return pl.pallas_call(
        table_kernel,
        grid=(groups // GPT,),
        in_specs=[seed, seed],
        out_specs=[full, full],
        out_shape=[shape, shape],
        compiler_params=params(),
        cost_estimate=cost(groups * 2**18, groups * 2**17),
    )(back, ahead)


def group_of_lane(rows, cols):
    return (lax.broadcasted_iota(jnp.int32, (rows, cols), 1) % LANES) // GROUP


def windows(ext, b):
    lo = b * FILT
    return jnp.concatenate([ext[lo : lo + 2 * FILT], ext[lo + FILT : lo + 3 * FILT]], axis=1)


def toeplitz(table, ext, blocks):
    group = group_of_lane(FILT, 2 * LANES)
    rows = []
    for b in range(0, blocks, 2):
        out = jnp.dot(table, windows(ext, b), preferred_element_type=F32)
        picked = out[:FILT]
        for g in range(1, GPT):
            picked = jnp.where(group == g, out[g * FILT : (g + 1) * FILT], picked)
        rows += [picked[:, :LANES], picked[:, LANES:]]
    return jnp.concatenate(rows, axis=0)


def product_of(k, v):
    return (k.astype(F32) * v.astype(F32)).astype(BF16)


def forward_kernel(q, k, v, prior, table, gated, mixed_out):
    blocks = q.shape[0] // FILT
    ext = jnp.concatenate([prior[...], product_of(k[...], v[...])], axis=0)
    mixed = toeplitz(table[...], ext, blocks)
    mixed_out[...] = mixed.astype(BF16)
    gated[...] = (q[...].astype(F32) * mixed).astype(BF16)


def forward(q, k, v, prior, table, chunk, chunks):
    rows, width = q.shape
    tiles = width // LANES // chunks
    here = pl.BlockSpec((rows, LANES), lambda i: (0, chunk * tiles + i))
    out = pl.BlockSpec((rows, LANES), lambda i: (0, i))
    shape = jax.ShapeDtypeStruct((rows, width // chunks), BF16)
    return pl.pallas_call(
        forward_kernel,
        grid=(tiles,),
        in_specs=[
            here,
            here,
            here,
            pl.BlockSpec((FILT, LANES), lambda i: (0, chunk * tiles + i)),
            pl.BlockSpec((GPT * FILT, 2 * FILT), lambda i: (chunk * tiles + i, 0)),
        ],
        out_specs=[out, out],
        out_shape=[shape, shape],
        compiler_params=params(),
        cost_estimate=cost(tiles * rows * 2 * 2**18, tiles * rows * 5 * 256 + tiles * 2**19),
    )(q, k, v, prior, table)


def middle_kernel(own, others, q, k, v, mixed, prior, *rest):
    gq_out, gm_out, edge_out, taps_out = rest[-4:]
    blocks = q.shape[0] // FILT
    total = own[...].astype(F32)
    for other in others:
        total = total + other[...].astype(F32)
    gg = total.astype(BF16).astype(F32)
    gq_out[...] = (gg * mixed[...].astype(F32)).astype(BF16)
    gm = (gg * q[...].astype(F32)).astype(BF16)
    gm_out[...] = gm
    edge_out[...] = gm[:FILT]
    ext = jnp.concatenate([prior[...], product_of(k[...], v[...])], axis=0)
    wide = jnp.concatenate([gm[b * FILT : (b + 1) * FILT] for b in range(blocks)], axis=1)
    group = group_of_lane(FILT, blocks * LANES)
    stack = jnp.concatenate(
        [jnp.where(group == g, wide, jnp.zeros_like(wide)) for g in range(GPT)], axis=0
    )
    near = jnp.concatenate([ext[b * FILT : (b + 2) * FILT] for b in range(blocks)], axis=1)
    lag = lax.dot_general(stack, near, (((1,), (1,)), ((), ())), preferred_element_type=F32)
    lag = lag.reshape(GPT, FILT, 2 * FILT)
    half = FILT // 2
    while half >= 8:
        lag = lag[:, :half] + pltpu.roll(lag[:, half:], 2 * FILT - half, 2)
        half //= 2
    while half >= 1:
        lag = lag + pltpu.roll(pltpu.roll(lag, 2 * FILT - half, 2), 8 - half, 1)
        half //= 2
    taps_out[...] = lag[:, 0, :]


def middle(own, others, q, k, v, mixed, prior, filled, chunk, chunks):
    rows, width = q.shape
    tiles = width // LANES // chunks
    groups = width // GROUP // chunks
    here = pl.BlockSpec((rows, LANES), lambda i: (0, chunk * tiles + i))
    part = pl.BlockSpec((rows, LANES), lambda i: (0, i))
    edge = pl.BlockSpec((FILT, LANES), lambda i: (0, i))
    n_other = len(others)

    def kernel(own_ref, *refs):
        middle_kernel(own_ref, refs[:n_other], *refs[n_other:])

    args = [own, *others, q, k, v, mixed, prior]
    in_specs = [part] * (1 + n_other) + [here] * 3 + [part]
    in_specs.append(pl.BlockSpec((FILT, LANES), lambda i: (0, chunk * tiles + i)))
    aliases = {}
    if filled is not None:
        aliases = {len(args): 0}
        args.append(filled)
        in_specs.append(pl.BlockSpec(memory_space=pl.ANY))
    return pl.pallas_call(
        kernel,
        grid=(tiles,),
        in_specs=in_specs,
        out_specs=[here, part, edge, pl.BlockSpec((GPT, 2 * FILT), lambda i: (i, 0))],
        out_shape=[
            jax.ShapeDtypeStruct((rows, width), BF16),
            jax.ShapeDtypeStruct((rows, width // chunks), BF16),
            jax.ShapeDtypeStruct((FILT, width // chunks), BF16),
            jax.ShapeDtypeStruct((groups, 2 * FILT), F32),
        ],
        input_output_aliases=aliases,
        compiler_params=params(),
        cost_estimate=cost(tiles * rows * 2 * 2**18, tiles * rows * 9 * 256),
    )(*args)


def backward_kernel(gm, later, k, v, table, *rest):
    gk_out, gv_out = rest[-2:]
    blocks = gm.shape[0] // FILT
    ext = jnp.concatenate([gm[...], later[...]], axis=0)
    gp = toeplitz(table[...], ext, blocks)
    gk_out[...] = (gp * v[...].astype(F32)).astype(BF16)
    gv_out[...] = (gp * k[...].astype(F32)).astype(BF16)


def backward(gm, later, k, v, table, filled, chunk, chunks):
    rows, width = k.shape
    tiles = width // LANES // chunks
    here = pl.BlockSpec((rows, LANES), lambda i: (0, chunk * tiles + i))
    part = pl.BlockSpec((rows, LANES), lambda i: (0, i))
    args = [gm, later, k, v, table]
    in_specs = [
        part,
        pl.BlockSpec((FILT, LANES), lambda i: (0, i)),
        here,
        here,
        pl.BlockSpec((GPT * FILT, 2 * FILT), lambda i: (chunk * tiles + i, 0)),
    ]
    aliases = {}
    if filled is not None:
        aliases = {len(args): 0, len(args) + 1: 1}
        args += filled
        in_specs += [pl.BlockSpec(memory_space=pl.ANY)] * 2
    shape = jax.ShapeDtypeStruct((rows, width), BF16)
    return pl.pallas_call(
        backward_kernel,
        grid=(tiles,),
        in_specs=in_specs,
        out_specs=[here, here],
        out_shape=[shape, shape],
        input_output_aliases=aliases,
        compiler_params=params(),
        cost_estimate=cost(tiles * rows * 2 * 2**18, tiles * rows * 5 * 256 + tiles * 2**19),
    )(*args)


def gate_kernel(slots, pick, *refs):
    out = refs[-1]
    cots, refs = refs[: len(slots)], list(refs[len(slots) : -1])
    blocks = []
    for slot in slots:
        block = refs.pop(0)[...]
        if slot:
            block = jnp.where(pick[LINE + slot - 1] == 1, block, refs.pop(0)[...])
        blocks.append(block)
    cot, block = cots[0][0], blocks[0]
    if len(slots) > 1:
        cot = jnp.concatenate([ref[0] for ref in cots], axis=1)
        block = jnp.concatenate(blocks, axis=0)
    total = jnp.dot(cot, block, preferred_element_type=F32)
    if refs:
        total = total + refs[0][...].astype(F32)
    out[...] = total.astype(out.dtype)


def gate_grad(pick, cot, weights, slots=(0, 1, 2, 3), base=None):
    _, rows, depth = cot.shape
    width = weights[0][0].shape[1]
    tile = min(256, width)

    def cot_spec(j):
        return pl.BlockSpec((1, rows, depth), lambda i, pick: (pick[j], 0, 0))

    blocks = [x for slot in slots for x in weights[slot]]
    part = pl.BlockSpec((rows, tile), lambda i, pick: (0, i))
    in_specs = [cot_spec(j) for j in slots]
    in_specs += [pl.BlockSpec((depth, tile), lambda i, pick: (0, i))] * len(blocks)
    args = [cot] * len(slots) + blocks
    if base is not None:
        in_specs.append(part)
        args.append(base)
    return pl.pallas_call(
        functools.partial(gate_kernel, slots),
        grid_spec=pltpu.PrefetchScalarGridSpec(
            num_scalar_prefetch=1,
            grid=(width // tile,),
            in_specs=in_specs,
            out_specs=part,
        ),
        out_shape=jax.ShapeDtypeStruct((rows, width), BF16),
        compiler_params=params(),
        cost_estimate=cost(
            2 * rows * len(slots) * depth * width, 2 * len(slots) * depth * (rows + width)
        ),
    )(pick, *args)


def rows_kernel(n, pick, *refs):
    out = refs[-1]
    cot, gated = refs[0][0], refs[n][...]
    if n > 1:
        cot = jnp.concatenate([ref[0] for ref in refs[:n]], axis=0)
        gated = jnp.concatenate([ref[...] for ref in refs[n : 2 * n]], axis=0)
    total = lax.dot_general(cot, gated, (((0,), (0,)), ((), ())), preferred_element_type=F32)
    if len(refs) > 2 * n + 1:
        total = total + refs[2 * n][0]
    out[0] = total.astype(out.dtype)


def weight_rows(pick, cots, gateds, dtype, base=None, skip=0):
    _, rows, depth = cots[0].shape
    width = gateds[0].shape[1]
    blocks = pick.shape[0]
    tile = width if blocks > 1 else min(512, width)
    n = len(cots)
    in_specs = [pl.BlockSpec((1, rows, depth), lambda j, i, pick: (pick[j], 0, 0))] * n
    in_specs += [pl.BlockSpec((rows, tile), lambda j, i, pick: (0, i))] * n
    args = [*cots, *gateds]
    if base is not None:
        in_specs.append(pl.BlockSpec((1, depth, tile), lambda j, i, pick: (j + skip, 0, i)))
        args.append(base)
    return pl.pallas_call(
        functools.partial(rows_kernel, n),
        grid_spec=pltpu.PrefetchScalarGridSpec(
            num_scalar_prefetch=1,
            grid=(blocks, width // tile),
            in_specs=in_specs,
            out_specs=pl.BlockSpec((1, depth, tile), lambda j, i, pick: (j, 0, i)),
        ),
        out_shape=jax.ShapeDtypeStruct((blocks, depth, width), dtype),
        compiler_params=params(),
        cost_estimate=cost(2 * n * rows * depth * width, 2 * n * rows * (depth + width)),
    )(pick, *args)


def packet_kernel(n, pick, *refs):
    base, up, down, first_out, packet_out = refs[2 * n :]
    cot, gated = refs[0][0], refs[n][...]
    if n > 1:
        cot = jnp.concatenate([ref[0] for ref in refs[:n]], axis=0)
        gated = jnp.concatenate([ref[...] for ref in refs[n : 2 * n]], axis=0)
    total = lax.dot_general(cot, gated, (((0,), (0,)), ((), ())), preferred_element_type=F32)
    rows = (total + base[0]).astype(BF16)
    first_out[...] = rows
    passed = jnp.where(pick[2] == 1, up[...], down[...])
    packet_out[...] = jnp.where(pick[1] == 1, rows, passed)


def packet_rows(pick, cots, gateds, base, up, down):
    _, rows, depth = cots[0].shape
    width = gateds[0].shape[1]
    tile = min(512, width)
    n = len(cots)
    part = pl.BlockSpec((depth, tile), lambda i, pick: (0, i))
    shape = jax.ShapeDtypeStruct((depth, width), BF16)
    return pl.pallas_call(
        functools.partial(packet_kernel, n),
        grid_spec=pltpu.PrefetchScalarGridSpec(
            num_scalar_prefetch=1,
            grid=(width // tile,),
            in_specs=[pl.BlockSpec((1, rows, depth), lambda i, pick: (pick[0], 0, 0))] * n
            + [pl.BlockSpec((rows, tile), lambda i, pick: (0, i))] * n
            + [pl.BlockSpec((1, depth, tile), lambda i, pick: (0, 0, i)), part, part],
            out_specs=[part, part],
        ),
        out_shape=[shape, shape],
        compiler_params=params(),
        cost_estimate=cost(2 * n * rows * depth * width, 2 * n * rows * (depth + width)),
    )(pick, *cots, *gateds, base, up, down)


def shards(seq, ch, queries, keys, values, filters, grad_out, out_weight):
    inner = seq // LINE
    rows, width = queries.shape
    depth = out_weight.shape[0]
    chunks = 2 if width % (2 * LANES) == 0 else 1
    cols = width // chunks
    place = lax.axis_index("seq")
    z, y = place // inner, place % inner

    def send(x, pairs):
        return lax.ppermute(x, "seq", pairs)

    def along_line(x, pairs):
        return send(x, [(a * inner + i, b * inner + i) for a, b in pairs for i in range(inner)])

    def around_inner(x, shift):
        return send(
            x, [(a * inner + i, a * inner + (i + shift) % inner) for a in range(LINE) for i in range(inner)]
        )

    each = range(chunks)
    up_pairs, down_pairs = [(0, 1), (1, 2), (2, 3)], [(1, 0), (2, 1), (3, 2)]

    def second_step(h):
        return along_line(up1[h], [(1, 2), (2, 3)]), along_line(down1[h], [(2, 1), (1, 0)])

    at_end = (z == 0) | (z == 3)
    pick = jnp.stack(
        [
            z,
            jnp.where(z == 0, 1, z - 1),
            jnp.where(z >= 2, z - 2, z + 2),
            jnp.where(z == 3, 0, jnp.where(z == 1, 2, 3)),
            z == 0,
            z >= 2,
            at_end,
        ]
    ).astype(jnp.int32)

    def weights(h):
        return [[halves[h]], [down1[h], up1[h]], second[h], [third[h], down1[h]]]

    def swap_gated(h):
        return [around_inner(gateds[h], r) for r in range(1, inner)]

    even = z % 2 == 0
    first_pick = jnp.where(even, 3, 0).astype(jnp.int32).reshape(1)
    rest_pick = jnp.stack(
        [
            jnp.where(z == 0, 2, jnp.where(z == 1, 3, jnp.where(z == 2, 0, 1))),
            jnp.where(even, 1, 2),
            z,
        ]
    ).astype(jnp.int32)

    def rows_own(h):
        return weight_rows(jnp.concatenate([first_pick, rest_pick]), cots[:1], [gateds[h]], F32)

    packet_pick = jnp.concatenate([first_pick, jnp.stack([at_end, z >= 2]).astype(jnp.int32)])

    def packet(h):
        return packet_rows(packet_pick, cots[1:], got[h], base[h], *second[h])

    def rows_rest(h):
        return weight_rows(rest_pick, cots[1:], got[h], BF16, base[h], 1)

    def send_packet(x):
        return along_line(x, [(0, 1), (3, 2), (2, 3), (1, 0)])

    def send_second(h, came):
        came = jnp.where(at_end, 0.0, came.astype(F32))
        x = (rest[h][0].astype(F32) + came).astype(BF16)
        return along_line(x, [(0, 1), (3, 2)]), along_line(x, [(1, 2), (2, 1)])

    def send_third(h, outer_in, inner_in):
        mine, other = rest[h][1].astype(F32), first[h].astype(F32)
        outer_in, inner_in = outer_in.astype(F32), inner_in.astype(F32)
        up = jnp.where(z == 2, other, mine) + jnp.where(z == 1, outer_in, inner_in)
        down = jnp.where(z == 1, other, mine) + jnp.where(z == 1, inner_in, outer_in)
        return along_line(up.astype(BF16), up_pairs), along_line(down.astype(BF16), down_pairs)

    def last_sum(h):
        below, above = sums[h]
        return (rest[h][2].astype(F32) + below.astype(F32) + above.astype(F32)).astype(BF16)

    def shares(h):
        return [gate_grad(pick, cots[r], weights(h)) for r in range(1, inner)]

    def send_shares(parts):
        return [around_inner(part, inner - r) for r, part in enumerate(parts, 1)]

    up1, down1, gateds, mixeds, got = ([None] * chunks for _ in range(5))
    second, third, sums, parts, others, owns = ([None] * chunks for _ in range(6))
    first, rest = ([None] * chunks for _ in range(2))
    later_halves = list(each[1:])

    prior = product_of(keys[rows - FILT :], values[rows - FILT :])
    cot_here = after(grad_out, prior)
    prior = send(prior, [(i, i + 1) for i in range(seq - 1)])
    paired = inner == 2 and ch == LINE
    other = cot_here
    cots = []
    if paired:
        kept = lax.dynamic_slice(cot_here, (0, y * depth), (rows, depth))
        other = lax.dynamic_slice(cot_here, (0, (1 - y) * depth), (rows, depth))
        cots = [lax.all_gather(kept, "ch", axis=0, tiled=False)]
    back, ahead = tables(filters)
    halves = [out_weight[:, h * cols : (h + 1) * cols] for h in each]
    prior, other, halves, back = fence(prior, other, halves, back)

    up1[0], down1[0] = along_line(halves[0], up_pairs), along_line(halves[0], down_pairs)
    swapped = around_inner(other, 1) if paired else other
    gateds[0], mixeds[0] = forward(queries, keys, values, prior, back, 0, chunks)
    up1[0], down1[0], swapped, gateds, cots = fence(up1[0], down1[0], swapped, gateds, cots)

    second[0] = second_step(0)
    if paired:
        cots.append(lax.all_gather(swapped, "ch", axis=0, tiled=False))
    else:
        full = lax.all_gather(swapped, "ch", axis=1, tiled=True)
        full = full.reshape(rows, LINE, inner, depth).transpose(2, 1, 0, 3)
        for shift in range(inner):
            part = lax.dynamic_index_in_dim(full, (y + shift) % inner, 0, keepdims=False)
            cots.append(part if shift == 0 else around_inner(part, shift))
    got[0] = swap_gated(0)
    base = [None] * chunks
    base[0] = rows_own(0)
    for h in later_halves:
        gateds[h], mixeds[h] = forward(queries, keys, values, prior, back, h, chunks)
        held = after(halves[h], gateds[h])
        up1[h], down1[h] = along_line(held, up_pairs), along_line(held, down_pairs)
    second[0], got[0], gateds, cots, base = fence(second[0], got[0], gateds, cots, base)

    first[0], parcel = packet(0)
    third[0] = send_packet(parcel)
    for h in later_halves:
        got[h] = swap_gated(h)
    up1, down1, parcel = fence(up1, down1, parcel)
    for h in later_halves:
        second[h] = second_step(h)
    rest[0] = rows_rest(0)
    begun = [gate_grad(pick, cot, weights(0), (0, 1, 2)) for cot in cots[1:]]
    second, rest[0], gateds, begun = fence(second, rest[0], gateds, begun)
    for h in later_halves:
        base[h] = rows_own(h)
    own_begun = gate_grad(pick, cots[0], weights(0), (0, 1, 2))
    third[0], second, base, own_begun = fence(third[0], second, base, own_begun)

    sums[0] = send_second(0, third[0])

    parts[0] = [
        gate_grad(pick, cot, weights(0), (3,), x) for cot, x in zip(cots[1:], begun)
    ]
    parts[0], got[1:], own_begun = fence(parts[0], got[1:], own_begun)
    others[0] = send_shares(parts[0])

    for h in later_halves:
        first[h], parcel = packet(h)
        third[h] = send_packet(parcel)
    sums[0] = send_third(0, *sums[0])
    for h in later_halves:
        rest[h] = rows_rest(h)
    owns[0] = gate_grad(pick, cots[0], weights(0), (3,), own_begun)
    third, rest[1:], owns[0] = fence(third, rest[1:], owns[0])

    for h in later_halves:
        parts[h] = shares(h)
    parts[1:], third = fence(parts[1:], third)
    for h in later_halves:
        others[h] = send_shares(parts[h])
        sums[h] = send_second(h, third[h])
    for h in later_halves:
        owns[h] = gate_grad(pick, cots[0], weights(h))
    others[0], owns = fence(others[0], owns)

    grad_queries = None
    grad_kv = None
    taps, gms, laters = ([None] * chunks for _ in range(3))
    for h in each:
        grad_queries, gms[h], edge, taps[h] = middle(
            owns[h], others[h], queries, keys, values, mixeds[h], prior, grad_queries, h, chunks
        )
        laters[h] = send(edge, [(i + 1, i) for i in range(seq - 1)])
        if h == 0:
            for g in later_halves:
                sums[g] = send_third(g, *after(sums[g], edge))
            done = [last_sum(0)]
            others, owns, done = fence(others, owns, done)
    for h in later_halves:
        sums[h], gms[0], _ = fence(sums[h], gms[0], edge)
        done.append(last_sum(h))
    for h in each:
        grad_kv = backward(gms[h], laters[h], keys, values, ahead, grad_kv, h, chunks)
    grad_weight = jnp.concatenate(done, axis=1)
    taps = jnp.concatenate(taps, axis=0)[:, 1 : FILT + 1][:, ::-1]
    taps = taps.T.reshape(seq, FILT // seq, -1)
    taps = jnp.sum(lax.all_to_all(taps, "seq", 0, 0), axis=0)
    return grad_queries, *grad_kv, taps.T, grad_weight


def solution(mesh):
    sizes = dict(mesh.shape)
    return jax.shard_map(
        functools.partial(shards, sizes["seq"], sizes["ch"]),
        mesh=mesh,
        in_specs=(
            P("seq", "ch"),
            P("seq", "ch"),
            P("seq", "ch"),
            P("ch", None),
            P("seq", "ch"),
            P("seq", "ch"),
        ),
        out_specs=(P("seq", "ch"), P("seq", "ch"), P("seq", "ch"), P("ch", "seq"), P("seq", "ch")),
        check_vma=False,
    )
```

```python
import functools

import jax
import jax.numpy as jnp
from jax import lax
from jax.experimental import pallas as pl
from jax.experimental.pallas import tpu as pltpu
from jax.sharding import PartitionSpec as P

GROUP = 16
FILT = 128
LANES = 128
GPT = LANES // GROUP
LINE = 4
F32 = jnp.float32
BF16 = jnp.bfloat16
VMEM_LIMIT = 48 * 1024 * 1024


def params():
    return pltpu.CompilerParams(vmem_limit_bytes=VMEM_LIMIT)


def cost(flops, nbytes):
    return pl.CostEstimate(flops=int(flops) // 64, bytes_accessed=int(nbytes) // 64, transcendentals=0)


def fence(*arrays):
    return lax.optimization_barrier(arrays)


def after(x, *others):
    return lax.optimization_barrier((x, *others))[0]


def table_kernel(back_ref, ahead_ref, back_out, ahead_out):
    for seed, out in ((back_ref, back_out), (ahead_ref, ahead_out)):
        for g in range(GPT):
            rows = jnp.broadcast_to(seed[g : g + 1, :], (FILT, 2 * FILT))
            turned = pltpu.roll(rows, 0, 1, stride=1, stride_axis=0)
            out[g * FILT : (g + 1) * FILT, :] = turned.astype(BF16)


def tables(filters):
    groups = filters.shape[0]
    taps = filters.astype(F32)
    back = jnp.concatenate(
        [jnp.zeros((groups, 1), F32), taps[:, ::-1], jnp.zeros((groups, FILT - 1), F32)], axis=1
    )
    ahead = jnp.concatenate([taps, jnp.zeros((groups, FILT), F32)], axis=1)
    seed = pl.BlockSpec((GPT, 2 * FILT), lambda i: (i, 0))
    full = pl.BlockSpec((GPT * FILT, 2 * FILT), lambda i: (i, 0))
    shape = jax.ShapeDtypeStruct((groups * FILT, 2 * FILT), BF16)
    return pl.pallas_call(
        table_kernel,
        grid=(groups // GPT,),
        in_specs=[seed, seed],
        out_specs=[full, full],
        out_shape=[shape, shape],
        compiler_params=params(),
        cost_estimate=cost(groups * 2**18, groups * 2**17),
    )(back, ahead)


def group_of_lane(rows, cols):
    return (lax.broadcasted_iota(jnp.int32, (rows, cols), 1) % LANES) // GROUP


def windows(ext, b):
    lo = b * FILT
    return jnp.concatenate([ext[lo : lo + 2 * FILT], ext[lo + FILT : lo + 3 * FILT]], axis=1)


def toeplitz(table, ext, blocks):
    group = group_of_lane(FILT, 2 * LANES)
    rows = []
    for b in range(0, blocks, 2):
        out = jnp.dot(table, windows(ext, b), preferred_element_type=F32)
        picked = out[:FILT]
        for g in range(1, GPT):
            picked = jnp.where(group == g, out[g * FILT : (g + 1) * FILT], picked)
        rows += [picked[:, :LANES], picked[:, LANES:]]
    return jnp.concatenate(rows, axis=0)


def product_of(k, v):
    return (k.astype(F32) * v.astype(F32)).astype(BF16)


def forward_kernel(q, k, v, prior, table, gated, mixed_out):
    blocks = q.shape[0] // FILT
    ext = jnp.concatenate([prior[...], product_of(k[...], v[...])], axis=0)
    mixed = toeplitz(table[...], ext, blocks)
    mixed_out[...] = mixed.astype(BF16)
    gated[...] = (q[...].astype(F32) * mixed).astype(BF16)


def forward(q, k, v, prior, table, chunk, chunks):
    rows, width = q.shape
    tiles = width // LANES // chunks
    here = pl.BlockSpec((rows, LANES), lambda i: (0, chunk * tiles + i))
    out = pl.BlockSpec((rows, LANES), lambda i: (0, i))
    shape = jax.ShapeDtypeStruct((rows, width // chunks), BF16)
    return pl.pallas_call(
        forward_kernel,
        grid=(tiles,),
        in_specs=[
            here,
            here,
            here,
            pl.BlockSpec((FILT, LANES), lambda i: (0, chunk * tiles + i)),
            pl.BlockSpec((GPT * FILT, 2 * FILT), lambda i: (chunk * tiles + i, 0)),
        ],
        out_specs=[out, out],
        out_shape=[shape, shape],
        compiler_params=params(),
        cost_estimate=cost(tiles * rows * 2 * 2**18, tiles * rows * 5 * 256 + tiles * 2**19),
    )(q, k, v, prior, table)


def middle_kernel(own, others, q, k, v, mixed, prior, *rest):
    gq_out, gm_out, edge_out, taps_out = rest[-4:]
    blocks = q.shape[0] // FILT
    total = own[...].astype(F32)
    for other in others:
        total = total + other[...].astype(F32)
    gg = total.astype(BF16).astype(F32)
    gq_out[...] = (gg * mixed[...].astype(F32)).astype(BF16)
    gm = (gg * q[...].astype(F32)).astype(BF16)
    gm_out[...] = gm
    edge_out[...] = gm[:FILT]
    ext = jnp.concatenate([prior[...], product_of(k[...], v[...])], axis=0)
    wide = jnp.concatenate([gm[b * FILT : (b + 1) * FILT] for b in range(blocks)], axis=1)
    group = group_of_lane(FILT, blocks * LANES)
    stack = jnp.concatenate(
        [jnp.where(group == g, wide, jnp.zeros_like(wide)) for g in range(GPT)], axis=0
    )
    near = jnp.concatenate([ext[b * FILT : (b + 2) * FILT] for b in range(blocks)], axis=1)
    lag = lax.dot_general(stack, near, (((1,), (1,)), ((), ())), preferred_element_type=F32)
    lag = lag.reshape(GPT, FILT, 2 * FILT)
    half = FILT // 2
    while half >= 8:
        lag = lag[:, :half] + pltpu.roll(lag[:, half:], 2 * FILT - half, 2)
        half //= 2
    while half >= 1:
        lag = lag + pltpu.roll(pltpu.roll(lag, 2 * FILT - half, 2), 8 - half, 1)
        half //= 2
    taps_out[...] = lag[:, 0, :]


def middle(own, others, q, k, v, mixed, prior, filled, chunk, chunks):
    rows, width = q.shape
    tiles = width // LANES // chunks
    groups = width // GROUP // chunks
    here = pl.BlockSpec((rows, LANES), lambda i: (0, chunk * tiles + i))
    part = pl.BlockSpec((rows, LANES), lambda i: (0, i))
    edge = pl.BlockSpec((FILT, LANES), lambda i: (0, i))
    n_other = len(others)

    def kernel(own_ref, *refs):
        middle_kernel(own_ref, refs[:n_other], *refs[n_other:])

    args = [own, *others, q, k, v, mixed, prior]
    in_specs = [part] * (1 + n_other) + [here] * 3 + [part]
    in_specs.append(pl.BlockSpec((FILT, LANES), lambda i: (0, chunk * tiles + i)))
    aliases = {}
    if filled is not None:
        aliases = {len(args): 0}
        args.append(filled)
        in_specs.append(pl.BlockSpec(memory_space=pl.ANY))
    return pl.pallas_call(
        kernel,
        grid=(tiles,),
        in_specs=in_specs,
        out_specs=[here, part, edge, pl.BlockSpec((GPT, 2 * FILT), lambda i: (i, 0))],
        out_shape=[
            jax.ShapeDtypeStruct((rows, width), BF16),
            jax.ShapeDtypeStruct((rows, width // chunks), BF16),
            jax.ShapeDtypeStruct((FILT, width // chunks), BF16),
            jax.ShapeDtypeStruct((groups, 2 * FILT), F32),
        ],
        input_output_aliases=aliases,
        compiler_params=params(),
        cost_estimate=cost(tiles * rows * 2 * 2**18, tiles * rows * 9 * 256),
    )(*args)


def backward_kernel(gm, later, k, v, table, *rest):
    gk_out, gv_out = rest[-2:]
    blocks = gm.shape[0] // FILT
    ext = jnp.concatenate([gm[...], later[...]], axis=0)
    gp = toeplitz(table[...], ext, blocks)
    gk_out[...] = (gp * v[...].astype(F32)).astype(BF16)
    gv_out[...] = (gp * k[...].astype(F32)).astype(BF16)


def backward(gm, later, k, v, table, filled, chunk, chunks):
    rows, width = k.shape
    tiles = width // LANES // chunks
    here = pl.BlockSpec((rows, LANES), lambda i: (0, chunk * tiles + i))
    part = pl.BlockSpec((rows, LANES), lambda i: (0, i))
    args = [gm, later, k, v, table]
    in_specs = [
        part,
        pl.BlockSpec((FILT, LANES), lambda i: (0, i)),
        here,
        here,
        pl.BlockSpec((GPT * FILT, 2 * FILT), lambda i: (chunk * tiles + i, 0)),
    ]
    aliases = {}
    if filled is not None:
        aliases = {len(args): 0, len(args) + 1: 1}
        args += filled
        in_specs += [pl.BlockSpec(memory_space=pl.ANY)] * 2
    shape = jax.ShapeDtypeStruct((rows, width), BF16)
    return pl.pallas_call(
        backward_kernel,
        grid=(tiles,),
        in_specs=in_specs,
        out_specs=[here, here],
        out_shape=[shape, shape],
        input_output_aliases=aliases,
        compiler_params=params(),
        cost_estimate=cost(tiles * rows * 2 * 2**18, tiles * rows * 5 * 256 + tiles * 2**19),
    )(*args)


def gate_kernel(slots, pick, *refs):
    out, held = refs[-2:]
    cots, refs = refs[: len(slots)], list(refs[len(slots) : -2])
    choices = []
    for slot in slots:
        choices.append([refs.pop(0)] + ([refs.pop(0)] if slot else []))
    depth = choices[0][0].shape[0]

    @pl.when(pl.program_id(0) == 0)
    def _():
        for n, (slot, choice) in enumerate(zip(slots, choices)):
            block = choice[0][...]
            if slot:
                block = jnp.where(pick[LINE + slot - 1] == 1, block, choice[1][...])
            held[n * depth : (n + 1) * depth] = block

    cot = cots[0][0]
    if len(slots) > 1:
        cot = jnp.concatenate([ref[0] for ref in cots], axis=1)
    total = jnp.dot(cot, held[...], preferred_element_type=F32)
    if refs:
        total = total + refs[0][...].astype(F32)
    out[...] = total.astype(out.dtype)


def gate_grad(pick, cot, weights, slots=(0, 1, 2, 3), base=None):
    _, rows, depth = cot.shape
    width = weights[0][0].shape[1]
    tile = min(256, rows)

    def cot_spec(j):
        return pl.BlockSpec((1, tile, depth), lambda i, pick: (pick[j], i, 0))

    blocks = [x for slot in slots for x in weights[slot]]
    part = pl.BlockSpec((tile, width), lambda i, pick: (i, 0))
    in_specs = [cot_spec(j) for j in slots]
    in_specs += [pl.BlockSpec((depth, width), lambda i, pick: (0, 0))] * len(blocks)
    args = [cot] * len(slots) + blocks
    if base is not None:
        in_specs.append(part)
        args.append(base)
    return pl.pallas_call(
        functools.partial(gate_kernel, slots),
        grid_spec=pltpu.PrefetchScalarGridSpec(
            num_scalar_prefetch=1,
            grid=(rows // tile,),
            in_specs=in_specs,
            out_specs=part,
            scratch_shapes=[pltpu.VMEM((len(slots) * depth, width), BF16)],
        ),
        out_shape=jax.ShapeDtypeStruct((rows, width), BF16),
        compiler_params=params(),
        cost_estimate=cost(
            2 * rows * len(slots) * depth * width, 2 * len(slots) * depth * (rows + width)
        ),
    )(pick, *args)


def rows_kernel(n, pick, *refs):
    out = refs[-1]
    cot, gated = refs[0][0], refs[n][...]
    if n > 1:
        cot = jnp.concatenate([ref[0] for ref in refs[:n]], axis=0)
        gated = jnp.concatenate([ref[...] for ref in refs[n : 2 * n]], axis=0)
    total = lax.dot_general(cot, gated, (((0,), (0,)), ((), ())), preferred_element_type=F32)
    if len(refs) > 2 * n + 1:
        total = total + refs[2 * n][0]
    out[0] = total.astype(out.dtype)


def weight_rows(pick, cots, gateds, dtype, base=None, skip=0):
    _, rows, depth = cots[0].shape
    width = gateds[0].shape[1]
    blocks = pick.shape[0]
    tile = width if blocks > 1 else min(512, width)
    n = len(cots)
    in_specs = [pl.BlockSpec((1, rows, depth), lambda j, i, pick: (pick[j], 0, 0))] * n
    in_specs += [pl.BlockSpec((rows, tile), lambda j, i, pick: (0, i))] * n
    args = [*cots, *gateds]
    if base is not None:
        in_specs.append(pl.BlockSpec((1, depth, tile), lambda j, i, pick: (j + skip, 0, i)))
        args.append(base)
    return pl.pallas_call(
        functools.partial(rows_kernel, n),
        grid_spec=pltpu.PrefetchScalarGridSpec(
            num_scalar_prefetch=1,
            grid=(blocks, width // tile),
            in_specs=in_specs,
            out_specs=pl.BlockSpec((1, depth, tile), lambda j, i, pick: (j, 0, i)),
        ),
        out_shape=jax.ShapeDtypeStruct((blocks, depth, width), dtype),
        compiler_params=params(),
        cost_estimate=cost(2 * n * rows * depth * width, 2 * n * rows * (depth + width)),
    )(pick, *args)


def packet_kernel(n, pick, *refs):
    base, up, down, first_out, packet_out = refs[2 * n :]
    cot, gated = refs[0][0], refs[n][...]
    if n > 1:
        cot = jnp.concatenate([ref[0] for ref in refs[:n]], axis=0)
        gated = jnp.concatenate([ref[...] for ref in refs[n : 2 * n]], axis=0)
    total = lax.dot_general(cot, gated, (((0,), (0,)), ((), ())), preferred_element_type=F32)
    rows = (total + base[0]).astype(BF16)
    first_out[...] = rows
    passed = jnp.where(pick[2] == 1, up[...], down[...])
    packet_out[...] = jnp.where(pick[1] == 1, rows, passed)


def packet_rows(pick, cots, gateds, base, up, down):
    _, rows, depth = cots[0].shape
    width = gateds[0].shape[1]
    tile = min(512, width)
    n = len(cots)
    part = pl.BlockSpec((depth, tile), lambda i, pick: (0, i))
    shape = jax.ShapeDtypeStruct((depth, width), BF16)
    return pl.pallas_call(
        functools.partial(packet_kernel, n),
        grid_spec=pltpu.PrefetchScalarGridSpec(
            num_scalar_prefetch=1,
            grid=(width // tile,),
            in_specs=[pl.BlockSpec((1, rows, depth), lambda i, pick: (pick[0], 0, 0))] * n
            + [pl.BlockSpec((rows, tile), lambda i, pick: (0, i))] * n
            + [pl.BlockSpec((1, depth, tile), lambda i, pick: (0, 0, i)), part, part],
            out_specs=[part, part],
        ),
        out_shape=[shape, shape],
        compiler_params=params(),
        cost_estimate=cost(2 * n * rows * depth * width, 2 * n * rows * (depth + width)),
    )(pick, *cots, *gateds, base, up, down)


def shards(seq, ch, queries, keys, values, filters, grad_out, out_weight):
    inner = seq // LINE
    rows, width = queries.shape
    depth = out_weight.shape[0]
    chunks = 2 if width % (2 * LANES) == 0 else 1
    cols = width // chunks
    place = lax.axis_index("seq")
    z, y = place // inner, place % inner

    def send(x, pairs):
        return lax.ppermute(x, "seq", pairs)

    def along_line(x, pairs):
        return send(x, [(a * inner + i, b * inner + i) for a, b in pairs for i in range(inner)])

    def around_inner(x, shift):
        return send(
            x, [(a * inner + i, a * inner + (i + shift) % inner) for a in range(LINE) for i in range(inner)]
        )

    each = range(chunks)
    up_pairs, down_pairs = [(0, 1), (1, 2), (2, 3)], [(1, 0), (2, 1), (3, 2)]

    def second_step(h):
        return along_line(up1[h], [(1, 2), (2, 3)]), along_line(down1[h], [(2, 1), (1, 0)])

    at_end = (z == 0) | (z == 3)
    pick = jnp.stack(
        [
            z,
            jnp.where(z == 0, 1, z - 1),
            jnp.where(z >= 2, z - 2, z + 2),
            jnp.where(z == 3, 0, jnp.where(z == 1, 2, 3)),
            z == 0,
            z >= 2,
            at_end,
        ]
    ).astype(jnp.int32)

    def weights(h):
        return [[halves[h]], [down1[h], up1[h]], second[h], [third[h], down1[h]]]

    def swap_gated(h):
        return [around_inner(gateds[h], r) for r in range(1, inner)]

    even = z % 2 == 0
    first_pick = jnp.where(even, 3, 0).astype(jnp.int32).reshape(1)
    rest_pick = jnp.stack(
        [
            jnp.where(z == 0, 2, jnp.where(z == 1, 3, jnp.where(z == 2, 0, 1))),
            jnp.where(even, 1, 2),
            z,
        ]
    ).astype(jnp.int32)

    def rows_own(h):
        return weight_rows(jnp.concatenate([first_pick, rest_pick]), cots[:1], [gateds[h]], F32)

    packet_pick = jnp.concatenate([first_pick, jnp.stack([at_end, z >= 2]).astype(jnp.int32)])

    def packet(h):
        return packet_rows(packet_pick, cots[1:], got[h], base[h], *second[h])

    def rows_rest(h):
        return weight_rows(rest_pick, cots[1:], got[h], BF16, base[h], 1)

    def send_packet(x):
        return along_line(x, [(0, 1), (3, 2), (2, 3), (1, 0)])

    def send_second(h, came):
        came = jnp.where(at_end, 0.0, came.astype(F32))
        x = (rest[h][0].astype(F32) + came).astype(BF16)
        return along_line(x, [(0, 1), (3, 2)]), along_line(x, [(1, 2), (2, 1)])

    def send_third(h, outer_in, inner_in):
        mine, other = rest[h][1].astype(F32), first[h].astype(F32)
        outer_in, inner_in = outer_in.astype(F32), inner_in.astype(F32)
        up = jnp.where(z == 2, other, mine) + jnp.where(z == 1, outer_in, inner_in)
        down = jnp.where(z == 1, other, mine) + jnp.where(z == 1, inner_in, outer_in)
        return along_line(up.astype(BF16), up_pairs), along_line(down.astype(BF16), down_pairs)

    def last_sum(h):
        below, above = sums[h]
        return (rest[h][2].astype(F32) + below.astype(F32) + above.astype(F32)).astype(BF16)

    def shares(h):
        return [gate_grad(pick, cots[r], weights(h)) for r in range(1, inner)]

    def send_shares(parts):
        return [around_inner(part, inner - r) for r, part in enumerate(parts, 1)]

    up1, down1, gateds, mixeds, got = ([None] * chunks for _ in range(5))
    second, third, sums, parts, others, owns = ([None] * chunks for _ in range(6))
    first, rest = ([None] * chunks for _ in range(2))
    later_halves = list(each[1:])

    prior = product_of(keys[rows - FILT :], values[rows - FILT :])
    cot_here = after(grad_out, prior)
    prior = send(prior, [(i, i + 1) for i in range(seq - 1)])
    paired = inner == 2 and ch == LINE
    other = cot_here
    cots = []
    if paired:
        kept = lax.dynamic_slice(cot_here, (0, y * depth), (rows, depth))
        other = lax.dynamic_slice(cot_here, (0, (1 - y) * depth), (rows, depth))
        cots = [lax.all_gather(kept, "ch", axis=0, tiled=False)]
    back, ahead = tables(filters)
    halves = [out_weight[:, h * cols : (h + 1) * cols] for h in each]
    prior, other, halves, back = fence(prior, other, halves, back)

    up1[0], down1[0] = along_line(halves[0], up_pairs), along_line(halves[0], down_pairs)
    swapped = around_inner(other, 1) if paired else other
    gateds[0], mixeds[0] = forward(queries, keys, values, prior, back, 0, chunks)
    up1[0], down1[0], swapped, gateds, cots = fence(up1[0], down1[0], swapped, gateds, cots)

    for h in later_halves:
        up1[h], down1[h] = along_line(halves[h], up_pairs), along_line(halves[h], down_pairs)
    second[0] = second_step(0)
    if paired:
        cots.append(lax.all_gather(swapped, "ch", axis=0, tiled=False))
    else:
        full = lax.all_gather(swapped, "ch", axis=1, tiled=True)
        full = full.reshape(rows, LINE, inner, depth).transpose(2, 1, 0, 3)
        for shift in range(inner):
            part = lax.dynamic_index_in_dim(full, (y + shift) % inner, 0, keepdims=False)
            cots.append(part if shift == 0 else around_inner(part, shift))
    got[0] = swap_gated(0)
    for h in later_halves:
        gateds[h], mixeds[h] = forward(queries, keys, values, prior, back, h, chunks)
    up1, down1, gateds, cots[0] = fence(up1, down1, gateds, cots[0])

    for h in later_halves:
        second[h] = second_step(h)
    base = [None] * chunks
    base[0] = rows_own(0)
    second[0], got[0], gateds, cots, base = fence(second[0], got[0], gateds, cots, base)

    first[0], parcel = packet(0)
    third[0] = send_packet(parcel)
    for h in later_halves:
        got[h] = swap_gated(h)
    rest[0] = rows_rest(0)
    begun = [gate_grad(pick, cot, weights(0), (0, 1, 2)) for cot in cots[1:]]
    second, rest[0], gateds, begun = fence(second, rest[0], gateds, begun)
    for h in later_halves:
        base[h] = rows_own(h)
    own_begun = gate_grad(pick, cots[0], weights(0), (0, 1, 2))
    third[0], second, base, own_begun = fence(third[0], second, base, own_begun)

    sums[0] = send_second(0, third[0])

    parts[0] = [
        gate_grad(pick, cot, weights(0), (3,), x) for cot, x in zip(cots[1:], begun)
    ]
    parts[0], got[1:], own_begun = fence(parts[0], got[1:], own_begun)
    others[0] = send_shares(parts[0])

    for h in later_halves:
        first[h], parcel = packet(h)
        third[h] = send_packet(parcel)
    sums[0] = send_third(0, *sums[0])
    for h in later_halves:
        rest[h] = rows_rest(h)
    owns[0] = gate_grad(pick, cots[0], weights(0), (3,), own_begun)
    third, rest[1:], owns[0] = fence(third, rest[1:], owns[0])

    for h in later_halves:
        parts[h] = shares(h)
    parts[1:], third = fence(parts[1:], third)
    for h in later_halves:
        others[h] = send_shares(parts[h])
        sums[h] = send_second(h, third[h])
    for h in later_halves:
        owns[h] = gate_grad(pick, cots[0], weights(h))
    others[0], owns = fence(others[0], owns)

    grad_queries = None
    grad_kv = None
    taps, gms, laters = ([None] * chunks for _ in range(3))
    for h in each:
        grad_queries, gms[h], edge, taps[h] = middle(
            owns[h], others[h], queries, keys, values, mixeds[h], prior, grad_queries, h, chunks
        )
        laters[h] = send(edge, [(i + 1, i) for i in range(seq - 1)])
        if h == 0:
            for g in later_halves:
                sums[g] = send_third(g, *after(sums[g], edge))
            done = [last_sum(0)]
            others, owns, done = fence(others, owns, done)
    for h in later_halves:
        sums[h], gms[0], _ = fence(sums[h], gms[0], edge)
        done.append(last_sum(h))
    for h in each:
        grad_kv = backward(gms[h], laters[h], keys, values, ahead, grad_kv, h, chunks)
    grad_weight = jnp.concatenate(done, axis=1)
    taps = jnp.concatenate(taps, axis=0)[:, 1 : FILT + 1][:, ::-1]
    taps = taps.T.reshape(seq, FILT // seq, -1)
    taps = jnp.sum(lax.all_to_all(taps, "seq", 0, 0), axis=0)
    return grad_queries, *grad_kv, taps.T, grad_weight


def solution(mesh):
    sizes = dict(mesh.shape)
    return jax.shard_map(
        functools.partial(shards, sizes["seq"], sizes["ch"]),
        mesh=mesh,
        in_specs=(
            P("seq", "ch"),
            P("seq", "ch"),
            P("seq", "ch"),
            P("ch", None),
            P("seq", "ch"),
            P("seq", "ch"),
        ),
        out_specs=(P("seq", "ch"), P("seq", "ch"), P("seq", "ch"), P("ch", "seq"), P("seq", "ch")),
        check_vma=False,
    )
```

```python
import functools

import jax
import jax.numpy as jnp
from jax import lax
from jax.experimental import pallas as pl
from jax.experimental.pallas import tpu as pltpu
from jax.sharding import PartitionSpec as P

GROUP = 16
FILT = 128
LANES = 128
GPT = LANES // GROUP
LINE = 4
F32 = jnp.float32
BF16 = jnp.bfloat16
VMEM_LIMIT = 48 * 1024 * 1024


def params():
    return pltpu.CompilerParams(vmem_limit_bytes=VMEM_LIMIT)


def cost(flops, nbytes):
    return pl.CostEstimate(flops=int(flops) // 64, bytes_accessed=int(nbytes) // 64, transcendentals=0)


def fence(*arrays):
    return lax.optimization_barrier(arrays)


def after(x, *others):
    return lax.optimization_barrier((x, *others))[0]


def table_kernel(back_ref, ahead_ref, back_out, ahead_out):
    for seed, out in ((back_ref, back_out), (ahead_ref, ahead_out)):
        for g in range(GPT):
            rows = jnp.broadcast_to(seed[g : g + 1, :], (FILT, 2 * FILT))
            turned = pltpu.roll(rows, 0, 1, stride=1, stride_axis=0)
            out[g * FILT : (g + 1) * FILT, :] = turned.astype(BF16)


def tables(filters):
    groups = filters.shape[0]
    taps = filters.astype(F32)
    back = jnp.concatenate(
        [jnp.zeros((groups, 1), F32), taps[:, ::-1], jnp.zeros((groups, FILT - 1), F32)], axis=1
    )
    ahead = jnp.concatenate([taps, jnp.zeros((groups, FILT), F32)], axis=1)
    seed = pl.BlockSpec((GPT, 2 * FILT), lambda i: (i, 0))
    full = pl.BlockSpec((GPT * FILT, 2 * FILT), lambda i: (i, 0))
    shape = jax.ShapeDtypeStruct((groups * FILT, 2 * FILT), BF16)
    return pl.pallas_call(
        table_kernel,
        grid=(groups // GPT,),
        in_specs=[seed, seed],
        out_specs=[full, full],
        out_shape=[shape, shape],
        compiler_params=params(),
        cost_estimate=cost(groups * 2**18, groups * 2**17),
    )(back, ahead)


def group_of_lane(rows, cols):
    return (lax.broadcasted_iota(jnp.int32, (rows, cols), 1) % LANES) // GROUP


def windows(ext, b):
    lo = b * FILT
    return jnp.concatenate([ext[lo : lo + 2 * FILT], ext[lo + FILT : lo + 3 * FILT]], axis=1)


def toeplitz(table, ext, blocks):
    group = group_of_lane(FILT, 2 * LANES)
    rows = []
    for b in range(0, blocks, 2):
        out = jnp.dot(table, windows(ext, b), preferred_element_type=F32).astype(BF16)
        picked = out[:FILT]
        for g in range(1, GPT):
            picked = jnp.where(group == g, out[g * FILT : (g + 1) * FILT], picked)
        rows += [picked[:, :LANES], picked[:, LANES:]]
    return jnp.concatenate(rows, axis=0).astype(F32)


def product_of(k, v):
    return (k.astype(F32) * v.astype(F32)).astype(BF16)


def forward_kernel(q, k, v, prior, table, gated, mixed_out):
    blocks = q.shape[0] // FILT
    ext = jnp.concatenate([prior[...], product_of(k[...], v[...])], axis=0)
    mixed = toeplitz(table[...], ext, blocks)
    mixed_out[...] = mixed.astype(BF16)
    gated[...] = (q[...].astype(F32) * mixed).astype(BF16)


def forward(q, k, v, prior, table, chunk, chunks):
    rows, width = q.shape
    tiles = width // LANES // chunks
    here = pl.BlockSpec((rows, LANES), lambda i: (0, chunk * tiles + i))
    out = pl.BlockSpec((rows, LANES), lambda i: (0, i))
    shape = jax.ShapeDtypeStruct((rows, width // chunks), BF16)
    return pl.pallas_call(
        forward_kernel,
        grid=(tiles,),
        in_specs=[
            here,
            here,
            here,
            pl.BlockSpec((FILT, LANES), lambda i: (0, chunk * tiles + i)),
            pl.BlockSpec((GPT * FILT, 2 * FILT), lambda i: (chunk * tiles + i, 0)),
        ],
        out_specs=[out, out],
        out_shape=[shape, shape],
        compiler_params=params(),
        cost_estimate=cost(tiles * rows * 2 * 2**18, tiles * rows * 5 * 256 + tiles * 2**19),
    )(q, k, v, prior, table)


def middle_kernel(own, others, q, k, v, mixed, prior, *rest):
    gq_out, gm_out, edge_out, taps_out = rest[-4:]
    blocks = q.shape[0] // FILT
    total = own[...].astype(F32)
    for other in others:
        total = total + other[...].astype(F32)
    gg = total.astype(BF16).astype(F32)
    gq_out[...] = (gg * mixed[...].astype(F32)).astype(BF16)
    gm = (gg * q[...].astype(F32)).astype(BF16)
    gm_out[...] = gm
    edge_out[...] = gm[:FILT]
    ext = jnp.concatenate([prior[...], product_of(k[...], v[...])], axis=0)
    wide = jnp.concatenate([gm[b * FILT : (b + 1) * FILT] for b in range(blocks)], axis=1)
    group = group_of_lane(FILT, blocks * LANES)
    stack = jnp.concatenate(
        [jnp.where(group == g, wide, jnp.zeros_like(wide)) for g in range(GPT)], axis=0
    )
    near = jnp.concatenate([ext[b * FILT : (b + 2) * FILT] for b in range(blocks)], axis=1)
    lag = lax.dot_general(stack, near, (((1,), (1,)), ((), ())), preferred_element_type=F32)
    lag = lag.reshape(GPT, FILT, 2 * FILT)
    half = FILT // 2
    while half >= 8:
        lag = lag[:, :half] + pltpu.roll(lag[:, half:], 2 * FILT - half, 2)
        half //= 2
    while half >= 1:
        lag = lag + pltpu.roll(pltpu.roll(lag, 2 * FILT - half, 2), 8 - half, 1)
        half //= 2
    taps_out[...] = lag[:, 0, :]


def middle(own, others, q, k, v, mixed, prior, filled, chunk, chunks):
    rows, width = q.shape
    tiles = width // LANES // chunks
    groups = width // GROUP // chunks
    here = pl.BlockSpec((rows, LANES), lambda i: (0, chunk * tiles + i))
    part = pl.BlockSpec((rows, LANES), lambda i: (0, i))
    edge = pl.BlockSpec((FILT, LANES), lambda i: (0, i))
    n_other = len(others)

    def kernel(own_ref, *refs):
        middle_kernel(own_ref, refs[:n_other], *refs[n_other:])

    args = [own, *others, q, k, v, mixed, prior]
    in_specs = [part] * (1 + n_other) + [here] * 3 + [part]
    in_specs.append(pl.BlockSpec((FILT, LANES), lambda i: (0, chunk * tiles + i)))
    aliases = {}
    if filled is not None:
        aliases = {len(args): 0}
        args.append(filled)
        in_specs.append(pl.BlockSpec(memory_space=pl.ANY))
    return pl.pallas_call(
        kernel,
        grid=(tiles,),
        in_specs=in_specs,
        out_specs=[here, part, edge, pl.BlockSpec((GPT, 2 * FILT), lambda i: (i, 0))],
        out_shape=[
            jax.ShapeDtypeStruct((rows, width), BF16),
            jax.ShapeDtypeStruct((rows, width // chunks), BF16),
            jax.ShapeDtypeStruct((FILT, width // chunks), BF16),
            jax.ShapeDtypeStruct((groups, 2 * FILT), F32),
        ],
        input_output_aliases=aliases,
        compiler_params=params(),
        cost_estimate=cost(tiles * rows * 2 * 2**18, tiles * rows * 9 * 256),
    )(*args)


def backward_kernel(gm, later, k, v, table, *rest):
    gk_out, gv_out = rest[-2:]
    blocks = gm.shape[0] // FILT
    ext = jnp.concatenate([gm[...], later[...]], axis=0)
    gp = toeplitz(table[...], ext, blocks)
    gk_out[...] = (gp * v[...].astype(F32)).astype(BF16)
    gv_out[...] = (gp * k[...].astype(F32)).astype(BF16)


def backward(gm, later, k, v, table, filled, chunk, chunks):
    rows, width = k.shape
    tiles = width // LANES // chunks
    here = pl.BlockSpec((rows, LANES), lambda i: (0, chunk * tiles + i))
    part = pl.BlockSpec((rows, LANES), lambda i: (0, i))
    args = [gm, later, k, v, table]
    in_specs = [
        part,
        pl.BlockSpec((FILT, LANES), lambda i: (0, i)),
        here,
        here,
        pl.BlockSpec((GPT * FILT, 2 * FILT), lambda i: (chunk * tiles + i, 0)),
    ]
    aliases = {}
    if filled is not None:
        aliases = {len(args): 0, len(args) + 1: 1}
        args += filled
        in_specs += [pl.BlockSpec(memory_space=pl.ANY)] * 2
    shape = jax.ShapeDtypeStruct((rows, width), BF16)
    return pl.pallas_call(
        backward_kernel,
        grid=(tiles,),
        in_specs=in_specs,
        out_specs=[here, here],
        out_shape=[shape, shape],
        input_output_aliases=aliases,
        compiler_params=params(),
        cost_estimate=cost(tiles * rows * 2 * 2**18, tiles * rows * 5 * 256 + tiles * 2**19),
    )(*args)


def gate_kernel(slots, pick, *refs):
    out, held = refs[-2:]
    cots, refs = refs[: len(slots)], list(refs[len(slots) : -2])
    choices = []
    for slot in slots:
        choices.append([refs.pop(0)] + ([refs.pop(0)] if slot else []))
    depth = choices[0][0].shape[0]

    @pl.when(pl.program_id(0) == 0)
    def _():
        for n, (slot, choice) in enumerate(zip(slots, choices)):
            block = choice[0][...]
            if slot:
                block = jnp.where(pick[LINE + slot - 1] == 1, block, choice[1][...])
            held[n * depth : (n + 1) * depth] = block

    cot = cots[0][0]
    if len(slots) > 1:
        cot = jnp.concatenate([ref[0] for ref in cots], axis=1)
    total = jnp.dot(cot, held[...], preferred_element_type=F32)
    if refs:
        total = total + refs[0][...].astype(F32)
    out[...] = total.astype(out.dtype)


def gate_grad(pick, cot, weights, slots=(0, 1, 2, 3), base=None):
    _, rows, depth = cot.shape
    width = weights[0][0].shape[1]
    tile = min(256, rows)

    def cot_spec(j):
        return pl.BlockSpec((1, tile, depth), lambda i, pick: (pick[j], i, 0))

    blocks = [x for slot in slots for x in weights[slot]]
    part = pl.BlockSpec((tile, width), lambda i, pick: (i, 0))
    in_specs = [cot_spec(j) for j in slots]
    in_specs += [pl.BlockSpec((depth, width), lambda i, pick: (0, 0))] * len(blocks)
    args = [cot] * len(slots) + blocks
    if base is not None:
        in_specs.append(part)
        args.append(base)
    return pl.pallas_call(
        functools.partial(gate_kernel, slots),
        grid_spec=pltpu.PrefetchScalarGridSpec(
            num_scalar_prefetch=1,
            grid=(rows // tile,),
            in_specs=in_specs,
            out_specs=part,
            scratch_shapes=[pltpu.VMEM((len(slots) * depth, width), BF16)],
        ),
        out_shape=jax.ShapeDtypeStruct((rows, width), BF16),
        compiler_params=params(),
        cost_estimate=cost(
            2 * rows * len(slots) * depth * width, 2 * len(slots) * depth * (rows + width)
        ),
    )(pick, *args)


def rows_kernel(n, pick, *refs):
    out = refs[-1]
    cot, gated = refs[0][0], refs[n][...]
    if n > 1:
        cot = jnp.concatenate([ref[0] for ref in refs[:n]], axis=0)
        gated = jnp.concatenate([ref[...] for ref in refs[n : 2 * n]], axis=0)
    total = lax.dot_general(cot, gated, (((0,), (0,)), ((), ())), preferred_element_type=F32)
    if len(refs) > 2 * n + 1:
        total = total + refs[2 * n][0]
    out[0] = total.astype(out.dtype)


def weight_rows(pick, cots, gateds, dtype, base=None, skip=0):
    _, rows, depth = cots[0].shape
    width = gateds[0].shape[1]
    blocks = pick.shape[0]
    tile = width if blocks > 1 else min(512, width)
    n = len(cots)
    in_specs = [pl.BlockSpec((1, rows, depth), lambda j, i, pick: (pick[j], 0, 0))] * n
    in_specs += [pl.BlockSpec((rows, tile), lambda j, i, pick: (0, i))] * n
    args = [*cots, *gateds]
    if base is not None:
        in_specs.append(pl.BlockSpec((1, depth, tile), lambda j, i, pick: (j + skip, 0, i)))
        args.append(base)
    return pl.pallas_call(
        functools.partial(rows_kernel, n),
        grid_spec=pltpu.PrefetchScalarGridSpec(
            num_scalar_prefetch=1,
            grid=(blocks, width // tile),
            in_specs=in_specs,
            out_specs=pl.BlockSpec((1, depth, tile), lambda j, i, pick: (j, 0, i)),
        ),
        out_shape=jax.ShapeDtypeStruct((blocks, depth, width), dtype),
        compiler_params=params(),
        cost_estimate=cost(2 * n * rows * depth * width, 2 * n * rows * (depth + width)),
    )(pick, *args)


def packet_kernel(n, pick, *refs):
    base, up, down, first_out, packet_out = refs[2 * n :]
    cot, gated = refs[0][0], refs[n][...]
    if n > 1:
        cot = jnp.concatenate([ref[0] for ref in refs[:n]], axis=0)
        gated = jnp.concatenate([ref[...] for ref in refs[n : 2 * n]], axis=0)
    total = lax.dot_general(cot, gated, (((0,), (0,)), ((), ())), preferred_element_type=F32)
    rows = (total + base[0]).astype(BF16)
    first_out[...] = rows
    passed = jnp.where(pick[2] == 1, up[...], down[...])
    packet_out[...] = jnp.where(pick[1] == 1, rows, passed)


def packet_rows(pick, cots, gateds, base, up, down):
    _, rows, depth = cots[0].shape
    width = gateds[0].shape[1]
    tile = min(512, width)
    n = len(cots)
    part = pl.BlockSpec((depth, tile), lambda i, pick: (0, i))
    shape = jax.ShapeDtypeStruct((depth, width), BF16)
    return pl.pallas_call(
        functools.partial(packet_kernel, n),
        grid_spec=pltpu.PrefetchScalarGridSpec(
            num_scalar_prefetch=1,
            grid=(width // tile,),
            in_specs=[pl.BlockSpec((1, rows, depth), lambda i, pick: (pick[0], 0, 0))] * n
            + [pl.BlockSpec((rows, tile), lambda i, pick: (0, i))] * n
            + [pl.BlockSpec((1, depth, tile), lambda i, pick: (0, 0, i)), part, part],
            out_specs=[part, part],
        ),
        out_shape=[shape, shape],
        compiler_params=params(),
        cost_estimate=cost(2 * n * rows * depth * width, 2 * n * rows * (depth + width)),
    )(pick, *cots, *gateds, base, up, down)


def shards(seq, ch, queries, keys, values, filters, grad_out, out_weight):
    inner = seq // LINE
    rows, width = queries.shape
    depth = out_weight.shape[0]
    chunks = 2 if width % (2 * LANES) == 0 else 1
    cols = width // chunks
    place = lax.axis_index("seq")
    z, y = place // inner, place % inner

    def send(x, pairs):
        return lax.ppermute(x, "seq", pairs)

    def along_line(x, pairs):
        return send(x, [(a * inner + i, b * inner + i) for a, b in pairs for i in range(inner)])

    def around_inner(x, shift):
        return send(
            x, [(a * inner + i, a * inner + (i + shift) % inner) for a in range(LINE) for i in range(inner)]
        )

    each = range(chunks)
    up_pairs, down_pairs = [(0, 1), (1, 2), (2, 3)], [(1, 0), (2, 1), (3, 2)]

    def second_step(h):
        return along_line(up1[h], [(1, 2), (2, 3)]), along_line(down1[h], [(2, 1), (1, 0)])

    at_end = (z == 0) | (z == 3)
    pick = jnp.stack(
        [
            z,
            jnp.where(z == 0, 1, z - 1),
            jnp.where(z >= 2, z - 2, z + 2),
            jnp.where(z == 3, 0, jnp.where(z == 1, 2, 3)),
            z == 0,
            z >= 2,
            at_end,
        ]
    ).astype(jnp.int32)

    def weights(h):
        return [[halves[h]], [down1[h], up1[h]], second[h], [third[h], down1[h]]]

    def swap_gated(h):
        return [around_inner(gateds[h], r) for r in range(1, inner)]

    even = z % 2 == 0
    first_pick = jnp.where(even, 3, 0).astype(jnp.int32).reshape(1)
    rest_pick = jnp.stack(
        [
            jnp.where(z == 0, 2, jnp.where(z == 1, 3, jnp.where(z == 2, 0, 1))),
            jnp.where(even, 1, 2),
            z,
        ]
    ).astype(jnp.int32)

    def rows_own(h):
        return weight_rows(jnp.concatenate([first_pick, rest_pick]), cots[:1], [gateds[h]], F32)

    packet_pick = jnp.concatenate([first_pick, jnp.stack([at_end, z >= 2]).astype(jnp.int32)])

    def packet(h):
        return packet_rows(packet_pick, cots[1:], got[h], base[h], *second[h])

    def rows_rest(h):
        return weight_rows(rest_pick, cots[1:], got[h], BF16, base[h], 1)

    def send_packet(x):
        return along_line(x, [(0, 1), (3, 2), (2, 3), (1, 0)])

    def send_second(h, came):
        came = jnp.where(at_end, 0.0, came.astype(F32))
        x = (rest[h][0].astype(F32) + came).astype(BF16)
        return along_line(x, [(0, 1), (3, 2)]), along_line(x, [(1, 2), (2, 1)])

    def send_third(h, outer_in, inner_in):
        mine, other = rest[h][1].astype(F32), first[h].astype(F32)
        outer_in, inner_in = outer_in.astype(F32), inner_in.astype(F32)
        up = jnp.where(z == 2, other, mine) + jnp.where(z == 1, outer_in, inner_in)
        down = jnp.where(z == 1, other, mine) + jnp.where(z == 1, inner_in, outer_in)
        return along_line(up.astype(BF16), up_pairs), along_line(down.astype(BF16), down_pairs)

    def last_sum(h):
        below, above = sums[h]
        return (rest[h][2].astype(F32) + below.astype(F32) + above.astype(F32)).astype(BF16)

    def shares(h):
        return [gate_grad(pick, cots[r], weights(h)) for r in range(1, inner)]

    def send_shares(parts):
        return [around_inner(part, inner - r) for r, part in enumerate(parts, 1)]

    up1, down1, gateds, mixeds, got = ([None] * chunks for _ in range(5))
    second, third, sums, parts, others, owns = ([None] * chunks for _ in range(6))
    first, rest = ([None] * chunks for _ in range(2))
    later_halves = list(each[1:])

    prior = product_of(keys[rows - FILT :], values[rows - FILT :])
    cot_here = after(grad_out, prior)
    prior = send(prior, [(i, i + 1) for i in range(seq - 1)])
    paired = inner == 2 and ch == LINE
    other = cot_here
    cots = []
    if paired:
        kept = lax.dynamic_slice(cot_here, (0, y * depth), (rows, depth))
        other = lax.dynamic_slice(cot_here, (0, (1 - y) * depth), (rows, depth))
        cots = [lax.all_gather(kept, "ch", axis=0, tiled=False)]
    back, ahead = tables(filters)
    halves = [out_weight[:, h * cols : (h + 1) * cols] for h in each]
    prior, other, halves, back = fence(prior, other, halves, back)

    up1[0], down1[0] = along_line(halves[0], up_pairs), along_line(halves[0], down_pairs)
    swapped = around_inner(other, 1) if paired else other
    gateds[0], mixeds[0] = forward(queries, keys, values, prior, back, 0, chunks)
    up1[0], down1[0], swapped, gateds, cots = fence(up1[0], down1[0], swapped, gateds, cots)

    for h in later_halves:
        up1[h], down1[h] = along_line(halves[h], up_pairs), along_line(halves[h], down_pairs)
    second[0] = second_step(0)
    if paired:
        cots.append(lax.all_gather(swapped, "ch", axis=0, tiled=False))
    else:
        full = lax.all_gather(swapped, "ch", axis=1, tiled=True)
        full = full.reshape(rows, LINE, inner, depth).transpose(2, 1, 0, 3)
        for shift in range(inner):
            part = lax.dynamic_index_in_dim(full, (y + shift) % inner, 0, keepdims=False)
            cots.append(part if shift == 0 else around_inner(part, shift))
    got[0] = swap_gated(0)
    for h in later_halves:
        gateds[h], mixeds[h] = forward(queries, keys, values, prior, back, h, chunks)
    up1, down1, gateds, cots[0] = fence(up1, down1, gateds, cots[0])

    for h in later_halves:
        second[h] = second_step(h)
    base = [None] * chunks
    base[0] = rows_own(0)
    second[0], got[0], gateds, cots, base = fence(second[0], got[0], gateds, cots, base)

    first[0], parcel = packet(0)
    third[0] = send_packet(parcel)
    for h in later_halves:
        got[h] = swap_gated(h)
    rest[0] = rows_rest(0)
    begun = [gate_grad(pick, cot, weights(0), (0, 1, 2)) for cot in cots[1:]]
    second, rest[0], gateds, begun = fence(second, rest[0], gateds, begun)
    for h in later_halves:
        base[h] = rows_own(h)
    own_begun = gate_grad(pick, cots[0], weights(0), (0, 1, 2))
    third[0], second, base, own_begun = fence(third[0], second, base, own_begun)

    sums[0] = send_second(0, third[0])

    parts[0] = [
        gate_grad(pick, cot, weights(0), (3,), x) for cot, x in zip(cots[1:], begun)
    ]
    parts[0], got[1:], own_begun = fence(parts[0], got[1:], own_begun)
    others[0] = send_shares(parts[0])

    for h in later_halves:
        first[h], parcel = packet(h)
        third[h] = send_packet(parcel)
    sums[0] = send_third(0, *sums[0])
    for h in later_halves:
        rest[h] = rows_rest(h)
    owns[0] = gate_grad(pick, cots[0], weights(0), (3,), own_begun)
    third, rest[1:], owns[0] = fence(third, rest[1:], owns[0])

    for h in later_halves:
        parts[h] = shares(h)
    parts[1:], third = fence(parts[1:], third)
    for h in later_halves:
        others[h] = send_shares(parts[h])
        sums[h] = send_second(h, third[h])
    for h in later_halves:
        owns[h] = gate_grad(pick, cots[0], weights(h))
    others[0], owns = fence(others[0], owns)

    grad_queries = None
    grad_kv = None
    taps, gms, laters = ([None] * chunks for _ in range(3))
    for h in each:
        grad_queries, gms[h], edge, taps[h] = middle(
            owns[h], others[h], queries, keys, values, mixeds[h], prior, grad_queries, h, chunks
        )
        laters[h] = send(edge, [(i + 1, i) for i in range(seq - 1)])
        if h == 0:
            for g in later_halves:
                sums[g] = send_third(g, *after(sums[g], edge))
            done = [last_sum(0)]
            others, owns, done = fence(others, owns, done)
    for h in later_halves:
        sums[h], gms[0], _ = fence(sums[h], gms[0], edge)
        done.append(last_sum(h))
    for h in each:
        grad_kv = backward(gms[h], laters[h], keys, values, ahead, grad_kv, h, chunks)
    grad_weight = jnp.concatenate(done, axis=1)
    taps = jnp.concatenate(taps, axis=0)[:, 1 : FILT + 1][:, ::-1]
    taps = taps.T.reshape(seq, FILT // seq, -1)
    taps = jnp.sum(lax.all_to_all(taps, "seq", 0, 0), axis=0)
    return grad_queries, *grad_kv, taps.T, grad_weight


def solution(mesh):
    sizes = dict(mesh.shape)
    return jax.shard_map(
        functools.partial(shards, sizes["seq"], sizes["ch"]),
        mesh=mesh,
        in_specs=(
            P("seq", "ch"),
            P("seq", "ch"),
            P("seq", "ch"),
            P("ch", None),
            P("seq", "ch"),
            P("seq", "ch"),
        ),
        out_specs=(P("seq", "ch"), P("seq", "ch"), P("seq", "ch"), P("ch", "seq"), P("seq", "ch")),
        check_vma=False,
    )
```
